32 devices in a mesh: section: 2 (over core), dp: 16 (over z, y, x).
Axes of the slice: x: 2, y: 2, z: 4, core: 2. Of those that a mesh axis runs over, the one named last changes fastest.
Arguments:
- images: bfloat16 [6272, 768], P('dp'), may hold values from -6 to 6
- text: bfloat16 [4096, 768], P('dp'), may hold values from -6 to 6
- enc_mats: bfloat16 [9216, 768], P('dp')
- enc_vecs: bfloat16 [9216], P('dp'), may hold values from -0.8 to 1.3
- dec_mats: bfloat16 [12288, 768], P('dp')
- dec_vecs: bfloat16 [13056], P('dp'), may hold values from -0.8 to 1.3
- tissue: int32 [32, 196], P('dp'), may hold values from 0 to 1, as said below
- text_len: int32 [32], P('dp'), may hold values from 32 to 128, as said below
- enc_cot: bfloat16 [6272, 768], P('dp'), may hold values from -6 to 6
- dec_cot: bfloat16 [4096, 768], P('dp'), may hold values from -6 to 6
Outputs:
- enc_out: bfloat16 [6272, 768], P('dp')
- dec_out: bfloat16 [4096, 768], P('dp')
- image_grad: float32 [6272, 768], P('dp')
- text_grad: float32 [4096, 768], P('dp')
- enc_mats_grad: float32 [9216, 768], P('dp')
- enc_vecs_grad: float32 [9216], P('dp')
- dec_mats_grad: float32 [12288, 768], P('dp')
- dec_vecs_grad: float32 [13056], P('dp')
The draws below stay inside these ranges and needn't reach their ends.
Inputs may be any that keep to these rules, and one draw needn't show every extreme that they name: `tissue`: each image has between 40 and 196 kept slots, anywhere among its slots; some image has exactly 196 and some exactly 40. `text_len`: some caption has exactly 128 tokens and some exactly 32.
All inputs are finite; a program needn't handle non-finite values.
Results may differ from the reference program's by a relative error of at most 0.025.
The reference program's roundings to bfloat16 on the way count: a program that leaves them out, or rounds other values in their place, can miss the bound.
Values may be sent and summed in bfloat16 or wider, within the bound.
A program may use at most 512 MiB of HBM per device.

```python
import jax
import jax.numpy as jnp
from jax import lax

D = 768
HEADS = 12
HEAD = 64
FF = 3072
SLOTS = 196
MIN_TISSUE = 40
TEXT = 128
IMAGES = 32


def scaled_rows(key, blocks):
    scales = jnp.concatenate([jnp.full((rows,), factor, jnp.float32) for rows, factor in blocks])
    normals = jnp.clip(jax.random.normal(key, (scales.shape[0], D), jnp.float32), -4.0, 4.0)
    return (normals * scales[:, None]).astype(jnp.bfloat16)


def gains_biases(key, count, gain_pieces):
    index = jnp.arange(count)
    piece = index // D
    is_gain = jnp.zeros((count,), bool)
    for number in gain_pieces:
        is_gain = is_gain | (piece == number)
    spread_key, bias_key = jax.random.split(key)
    gains = 1.0 + 0.3 * jax.random.uniform(spread_key, (count,), jnp.float32, -1.0, 1.0)
    biases = 0.2 * jnp.clip(jax.random.normal(bias_key, (count,), jnp.float32), -4.0, 4.0)
    return jnp.where(is_gain, gains, biases).astype(jnp.bfloat16)


def draw_enc_mats(key, part):
    key = jax.random.fold_in(key, 3)
    unit = D ** (-0.5)
    return scaled_rows(key, [(D, 1.5 * unit), (2 * D, unit), (D, 4.0 * unit), (FF, unit), (FF, FF ** (-0.5))])


def draw_dec_mats(key, part):
    key = jax.random.fold_in(key, 5)
    unit = D ** (-0.5)
    return scaled_rows(key, [(D, 1.5 * unit), (2 * D, unit), (D, 4.0 * unit), (D, 1.5 * unit), (2 * D, unit), (D, 4.0 * unit), (FF, unit), (FF, FF ** (-0.5))])


def draw_enc_vecs(key, part):
    key = jax.random.fold_in(key, 7)
    return gains_biases(key, 8 * D + FF, (0, 5))


def draw_dec_vecs(key, part):
    key = jax.random.fold_in(key, 9)
    return gains_biases(key, 13 * D + FF, (0, 5, 10))


def forced_pair(key, total):
    first_key, second_key = jax.random.split(key)
    first_pick = jax.random.randint(first_key, (), 0, total)
    second_pick = (first_pick + 1 + jax.random.randint(second_key, (), 0, total - 1)) % total
    return (first_pick, second_pick)


def draw_tissue(key, part):
    key = jax.random.fold_in(key, 11)
    count_key, pick_key, order_key = jax.random.split(key, 3)
    counts = jax.random.randint(count_key, (IMAGES,), MIN_TISSUE, SLOTS + 1)
    full_pick, least_pick = forced_pair(pick_key, IMAGES)
    index = jnp.arange(IMAGES)
    counts = jnp.where(index == full_pick, SLOTS, jnp.where(index == least_pick, MIN_TISSUE, counts))
    orders = jax.vmap(lambda sub: jax.random.permutation(sub, SLOTS))(jax.random.split(order_key, IMAGES))
    return (orders < counts[:, None]).astype(jnp.int32)


def draw_text_len(key, part):
    key = jax.random.fold_in(key, 13)
    length_key, pick_key = jax.random.split(key)
    lengths = jax.random.randint(length_key, (IMAGES,), TEXT // 4, TEXT + 1)
    full_pick, least_pick = forced_pair(pick_key, IMAGES)
    index = jnp.arange(IMAGES)
    return jnp.where(index == full_pick, TEXT, jnp.where(index == least_pick, TEXT // 4, lengths)).astype(jnp.int32)


def shard_levels(rng, shape, cuts, low, high):
    gain, own = 1.0, jax.random.fold_in(rng, 6)
    for position, shards_of in cuts:
        steps = jnp.exp(jax.random.uniform(jax.random.fold_in(own, position), (shards_of,), jnp.float32, low / len(cuts), high / len(cuts)))
        gain = gain * jnp.repeat(steps, shape[position] // shards_of).reshape([-1 if axis == position else 1 for axis in range(len(shape))])
    return gain


def bell_draw(rng, dims, scale, limit, shards=(), dtype=jnp.bfloat16):
    entries = scale * jax.random.normal(rng, dims, jnp.float32)
    if shards:
        entries = entries * shard_levels(rng, dims, shards, -0.22, 0.18)
    return jnp.clip(entries, -limit, limit).astype(dtype)


def setup_inputs(seed: int = 0) -> dict:
    arg_keys = jax.random.split(jax.random.key(seed), 11)
    return {
        "images": bell_draw(arg_keys[0], (IMAGES * SLOTS, D), 1.0, 6.0, ((0, 16),)),
        "text": bell_draw(arg_keys[1], (IMAGES * TEXT, D), 1.0, 6.0, ((0, 16),)),
        "enc_mats": draw_enc_mats(jax.random.fold_in(arg_keys[10], 71), 0),
        "enc_vecs": draw_enc_vecs(jax.random.fold_in(arg_keys[10], 71), 0),
        "dec_mats": draw_dec_mats(jax.random.fold_in(arg_keys[10], 71), 0),
        "dec_vecs": draw_dec_vecs(jax.random.fold_in(arg_keys[10], 71), 0),
        "tissue": draw_tissue(jax.random.fold_in(arg_keys[10], 71), 0),
        "text_len": draw_text_len(jax.random.fold_in(arg_keys[10], 71), 0),
        "enc_cot": bell_draw(arg_keys[8], (IMAGES * SLOTS, D), 1.0, 6.0, ((0, 16),)),
        "dec_cot": bell_draw(arg_keys[9], (IMAGES * TEXT, D), 1.0, 6.0, ((0, 16),)),
    }


@jax.custom_vjp
def low(v):
    return lax.optimization_barrier(v.astype(jnp.bfloat16)).astype(jnp.float32)

@jax.custom_vjp
def low_back(v):
    return v

def low_keep(v):
    return (low(v), None)

def low_pass(kept, grad):
    return (grad,)

def back_keep(v):
    return (v, None)

def back_low(kept, grad):
    return (low(grad),)
low.defvjp(low_keep, low_pass)
low_back.defvjp(back_keep, back_low)

def layer_norm(inputs, scale_vec, shift_vec):
    centre = inputs - lax.optimization_barrier(jnp.mean(inputs, axis=-1, keepdims=True))
    spread = lax.optimization_barrier(jnp.mean(centre * centre, axis=-1, keepdims=True))
    return centre * lax.rsqrt(spread + 1e-06) * scale_vec + shift_vec

def linear(inputs, weight):
    return jnp.einsum('gsd,de->gse', inputs, weight, precision=lax.Precision.HIGHEST)

def linear_t(inputs, weight_t):
    return jnp.einsum('gsd,fd->gsf', inputs, weight_t, precision=lax.Precision.HIGHEST)

def split_heads(rows):
    return rows.reshape(rows.shape[0], rows.shape[1], HEADS, HEAD)

def attend(queries, key_rows, value_rows, allowed):
    scores = jnp.einsum('gqhe,gkhe->ghqk', split_heads(queries), split_heads(key_rows), precision=lax.Precision.HIGHEST) * 0.125
    scores = jnp.where(allowed, low_back(scores), -1000000000.0)
    peak = lax.optimization_barrier(jnp.max(scores, axis=-1, keepdims=True))
    expd = jnp.exp(scores - peak)
    probs = expd / lax.optimization_barrier(jnp.sum(expd, axis=-1, keepdims=True))
    mixed = jnp.einsum('ghqk,gkhe->gqhe', low(probs), split_heads(value_rows), precision=lax.Precision.HIGHEST)
    return mixed.reshape(queries.shape)

def part_of(vecs, index):
    return vecs[index * D:(index + 1) * D]

def self_block(inputs, allowed, mats, vecs):
    normed = low(layer_norm(inputs, part_of(vecs, 0), part_of(vecs, 1)))
    queries = low(low_back(linear(normed, mats[0:D]) + part_of(vecs, 2)))
    key_rows = low(low_back(linear(normed, mats[D:2 * D])))
    value_rows = low(low_back(linear(normed, mats[2 * D:3 * D]) + part_of(vecs, 3)))
    mixed = low(low_back(attend(queries, key_rows, value_rows, allowed)))
    return inputs + low_back(linear(mixed, mats[3 * D:4 * D]) + part_of(vecs, 4))

def mlp_block(inputs, w_in_t, w_out, norm_gain, norm_shift, bias_in, bias_out):
    normed = low(layer_norm(inputs, norm_gain, norm_shift))
    inner = low_back(linear_t(normed, w_in_t) + bias_in)
    hidden = low(jax.nn.gelu(inner))
    return inputs + low_back(jnp.einsum('gsf,fd->gsd', hidden, w_out, precision=lax.Precision.HIGHEST) + bias_out)

def encoder(inputs, keep, mats, vecs):
    allowed = (keep > 0.5)[:, None, None, :]
    middle = self_block(inputs, allowed, mats, vecs)
    result = mlp_block(middle, mats[4 * D:4 * D + FF], mats[4 * D + FF:], part_of(vecs, 5), part_of(vecs, 6), vecs[8 * D:8 * D + FF], part_of(vecs, 7))
    return low(low_back(result * keep[..., None]))

def decoder(inputs, image_rows, keep, length, mats, vecs):
    positions = jnp.arange(TEXT)
    causal = (positions[None, :] <= positions[:, None])[None, None] & (positions[None, None, None, :] < length[:, None, None, None])
    after_self = self_block(inputs, causal, mats, vecs)
    normed = low(layer_norm(after_self, part_of(vecs, 5), part_of(vecs, 6)))
    cross_q = low(low_back(linear(normed, mats[4 * D:5 * D]) + part_of(vecs, 7)))
    cross_k = low(low_back(linear(image_rows, mats[5 * D:6 * D])))
    cross_v = low(low_back(linear(image_rows, mats[6 * D:7 * D]) + part_of(vecs, 8)))
    crossing = (keep > 0.5)[:, None, None, :]
    mixed = low(low_back(attend(cross_q, cross_k, cross_v, crossing)))
    after_cross = after_self + low_back(linear(mixed, mats[7 * D:8 * D]) + part_of(vecs, 9))
    return mlp_block(after_cross, mats[8 * D:8 * D + FF], mats[8 * D + FF:], part_of(vecs, 10), part_of(vecs, 11), vecs[13 * D:13 * D + FF], part_of(vecs, 12))

def reference(images, text, enc_mats, enc_vecs, dec_mats, dec_vecs, tissue, text_len, enc_cot, dec_cot):
    group = 16
    count = tissue.shape[0] // group
    keep = tissue.astype(jnp.float32).reshape(count, group, SLOTS)
    lengths = text_len.reshape(count, group)

    def forward(image_in, text_in, emats, evecs, dmats, dvecs):

        def one_group(items):
            image_part, text_part, keep_part, length_part = items
            encoded = encoder(image_part, keep_part, emats, evecs)
            decoded = decoder(text_part, encoded, keep_part, length_part, dmats, dvecs)
            return (encoded, decoded)
        encoded, decoded = lax.map(jax.checkpoint(one_group), (image_in.reshape(count, group, SLOTS, D), text_in.reshape(count, group, TEXT, D), keep, lengths))
        return (encoded.reshape(-1, D), decoded.reshape(-1, D))
    floats = (images.astype(jnp.float32), text.astype(jnp.float32), enc_mats.astype(jnp.float32), enc_vecs.astype(jnp.float32), dec_mats.astype(jnp.float32), dec_vecs.astype(jnp.float32))
    outputs, pullback = jax.vjp(forward, *floats)
    grads = pullback((enc_cot.astype(jnp.float32), dec_cot.astype(jnp.float32)))
    return (outputs[0].astype(jnp.bfloat16), outputs[1].astype(jnp.bfloat16), grads[0], grads[1], grads[2], grads[3], grads[4], grads[5])
```

```python
import functools

import jax
import jax.numpy as jnp
from jax import lax
from jax.experimental import pallas as pl
from jax.experimental.pallas import tpu as pltpu
from jax.sharding import PartitionSpec as P

D = 768
HEAD = 64
FF = 3072
MICRO = 2


def shifted(block, axis, distance):
    devices = range(lax.axis_size(axis))
    route = [(i - distance, i) for i in devices if i - distance in devices]
    return lax.ppermute(block, axis, route)


def layer_norm(inputs, scale_vec, shift_vec):
    centre = inputs - jnp.mean(inputs, axis=-1, keepdims=True)
    spread = jnp.mean(centre * centre, axis=-1, keepdims=True)
    return centre * lax.rsqrt(spread + 1e-06) * scale_vec + shift_vec


def norm_back(inputs, scale_vec, shift_vec, grads):
    _, pullback = jax.vjp(layer_norm, inputs, scale_vec, shift_vec)
    return pullback(grads)


def gelu_back(inner, grads):
    _, pullback = jax.vjp(jax.nn.gelu, inner)
    return pullback(grads)[0]


def part_of(vecs, index):
    return vecs[index * D : (index + 1) * D].astype(jnp.float32)


def split_heads(rows):
    return rows.reshape(rows.shape[0], rows.shape[1], -1, HEAD)


def project(rows, weight):
    return jnp.einsum("bsd,de->bse", rows, weight, preferred_element_type=jnp.float32)


def row_sum(values):
    return jnp.sum(values.astype(jnp.float32), axis=(0, 1))


def attn_scores(queries, key_rows, allowed):
    scores = (
        jnp.einsum(
            "bqhe,bkhe->bhqk",
            split_heads(queries),
            split_heads(key_rows),
            preferred_element_type=jnp.float32,
        )
        * 0.125
    )
    return jnp.where(allowed, scores, -1000000000.0)


def attn_forward(queries, key_rows, value_rows, allowed):
    scores = attn_scores(queries, key_rows, allowed)
    peak = jnp.max(scores, axis=-1, keepdims=True)
    expd = jnp.exp(scores - peak)
    total = jnp.sum(expd, axis=-1, keepdims=True)
    probs = (expd / total).astype(jnp.bfloat16)
    mixed = jnp.einsum(
        "bhqk,bkhe->bqhe", probs, split_heads(value_rows), preferred_element_type=jnp.float32
    )
    return (mixed.reshape(queries.shape).astype(jnp.bfloat16), peak + jnp.log(total))


def attn_backward(queries, key_rows, value_rows, allowed, log_total, grad_mixed):
    scores = attn_scores(queries, key_rows, allowed)
    probs = jnp.exp(scores - log_total)
    grad_heads = split_heads(grad_mixed)
    grad_probs = jnp.einsum(
        "bqhe,bkhe->bhqk", grad_heads, split_heads(value_rows), preferred_element_type=jnp.float32
    )
    grad_scores = probs * (grad_probs - jnp.sum(grad_probs * probs, axis=-1, keepdims=True))
    grad_low = grad_scores.astype(jnp.bfloat16)
    grad_q = (
        jnp.einsum(
            "bhqk,bkhe->bqhe", grad_low, split_heads(key_rows), preferred_element_type=jnp.float32
        )
        * 0.125
    )
    grad_k = (
        jnp.einsum(
            "bhqk,bqhe->bkhe", grad_low, split_heads(queries), preferred_element_type=jnp.float32
        )
        * 0.125
    )
    grad_v = jnp.einsum(
        "bhqk,bqhe->bkhe",
        probs.astype(jnp.bfloat16),
        grad_heads,
        preferred_element_type=jnp.float32,
    )
    return (
        grad_q.reshape(queries.shape),
        grad_k.reshape(key_rows.shape),
        grad_v.reshape(value_rows.shape),
    )


def self_block(inputs, allowed, mats, vecs):
    wqkv = mats[0 : 3 * D].reshape(3, D, D)
    normed = layer_norm(inputs, part_of(vecs, 0), part_of(vecs, 1)).astype(jnp.bfloat16)
    qkv = jnp.einsum("bsd,kde->kbse", normed, wqkv, preferred_element_type=jnp.float32)
    queries = (qkv[0] + part_of(vecs, 2)).astype(jnp.bfloat16)
    key_rows = qkv[1].astype(jnp.bfloat16)
    value_rows = (qkv[2] + part_of(vecs, 3)).astype(jnp.bfloat16)
    mixed, log_total = attn_forward(queries, key_rows, value_rows, allowed)
    after = inputs + project(mixed, mats[3 * D : 4 * D]) + part_of(vecs, 4)
    return (after, (normed, queries, key_rows, value_rows, mixed, log_total))


def self_block_back(inputs, allowed, mats, vecs, saved, grad_after):
    normed, queries, key_rows, value_rows, mixed, log_total = saved
    wqkv = mats[0 : 3 * D].reshape(3, D, D)
    grad_low = grad_after.astype(jnp.bfloat16)
    grad_wout = jnp.einsum("bsd,bse->de", mixed, grad_low, preferred_element_type=jnp.float32)
    grad_mixed = jnp.einsum(
        "bse,de->bsd", grad_low, mats[3 * D : 4 * D], preferred_element_type=jnp.float32
    ).astype(jnp.bfloat16)
    grad_q, grad_k, grad_v = attn_backward(
        queries, key_rows, value_rows, allowed, log_total, grad_mixed
    )
    grad_qkv = jnp.stack([grad_q, grad_k, grad_v]).astype(jnp.bfloat16)
    grad_wqkv = jnp.einsum(
        "bsd,kbse->kde", normed, grad_qkv, preferred_element_type=jnp.float32
    ).reshape(3 * D, D)
    grad_normed = jnp.einsum("kbse,kde->bsd", grad_qkv, wqkv, preferred_element_type=jnp.float32)
    grad_in, grad_gain, grad_shift = norm_back(
        inputs, part_of(vecs, 0), part_of(vecs, 1), grad_normed
    )
    vec_grads = [
        grad_gain,
        grad_shift,
        row_sum(grad_qkv[0]),
        row_sum(grad_qkv[2]),
        row_sum(grad_low),
    ]
    return (grad_after + grad_in, [grad_wqkv, grad_wout], vec_grads)


def cross_block(inputs, image_rows, allowed, mats, vecs):
    normed = layer_norm(inputs, part_of(vecs, 5), part_of(vecs, 6)).astype(jnp.bfloat16)
    queries = (project(normed, mats[4 * D : 5 * D]) + part_of(vecs, 7)).astype(jnp.bfloat16)
    pair = jnp.einsum(
        "bsd,kde->kbse",
        image_rows,
        mats[5 * D : 7 * D].reshape(2, D, D),
        preferred_element_type=jnp.float32,
    )
    key_rows = pair[0].astype(jnp.bfloat16)
    value_rows = (pair[1] + part_of(vecs, 8)).astype(jnp.bfloat16)
    mixed, log_total = attn_forward(queries, key_rows, value_rows, allowed)
    after = inputs + project(mixed, mats[7 * D : 8 * D]) + part_of(vecs, 9)
    return (after, (normed, queries, key_rows, value_rows, mixed, log_total))


def cross_block_back(inputs, image_rows, allowed, mats, vecs, saved, grad_after):
    normed, queries, key_rows, value_rows, mixed, log_total = saved
    grad_low = grad_after.astype(jnp.bfloat16)
    grad_wout = jnp.einsum("bsd,bse->de", mixed, grad_low, preferred_element_type=jnp.float32)
    grad_mixed = jnp.einsum(
        "bse,de->bsd", grad_low, mats[7 * D : 8 * D], preferred_element_type=jnp.float32
    ).astype(jnp.bfloat16)
    grad_q, grad_k, grad_v = attn_backward(
        queries, key_rows, value_rows, allowed, log_total, grad_mixed
    )
    grad_query = grad_q.astype(jnp.bfloat16)
    grad_pair = jnp.stack([grad_k, grad_v]).astype(jnp.bfloat16)
    pair_weight = mats[5 * D : 7 * D].reshape(2, D, D)
    grad_wq = jnp.einsum("bsd,bse->de", normed, grad_query, preferred_element_type=jnp.float32)
    grad_wpair = jnp.einsum(
        "bsd,kbse->kde", image_rows, grad_pair, preferred_element_type=jnp.float32
    ).reshape(2 * D, D)
    grad_image = jnp.einsum(
        "kbse,kde->bsd", grad_pair, pair_weight, preferred_element_type=jnp.float32
    )
    grad_normed = jnp.einsum(
        "bse,de->bsd", grad_query, mats[4 * D : 5 * D], preferred_element_type=jnp.float32
    )
    grad_in, grad_gain, grad_shift = norm_back(
        inputs, part_of(vecs, 5), part_of(vecs, 6), grad_normed
    )
    vec_grads = [
        grad_gain,
        grad_shift,
        row_sum(grad_query),
        row_sum(grad_pair[1]),
        row_sum(grad_low),
    ]
    return (grad_after + grad_in, grad_image, [grad_wq, grad_wpair, grad_wout], vec_grads)


def mlp_block(inputs, w_in_t, w_out, norm_gain, norm_shift, bias_in, bias_out):
    normed = layer_norm(inputs, norm_gain, norm_shift).astype(jnp.bfloat16)
    inner = jnp.einsum("bsd,fd->bsf", normed, w_in_t, preferred_element_type=jnp.float32) + bias_in
    hidden = jax.nn.gelu(inner).astype(jnp.bfloat16)
    result = (
        inputs
        + jnp.einsum("bsf,fd->bsd", hidden, w_out, preferred_element_type=jnp.float32)
        + bias_out
    )
    return (result, (normed, inner, hidden))


def mlp_block_back(inputs, w_in_t, w_out, norm_gain, norm_shift, saved, grad_result):
    normed, inner, hidden = saved
    grad_low = grad_result.astype(jnp.bfloat16)
    grad_w_out = jnp.einsum("bsf,bsd->fd", hidden, grad_low, preferred_element_type=jnp.float32)
    grad_hidden = jnp.einsum("bsd,fd->bsf", grad_low, w_out, preferred_element_type=jnp.float32)
    grad_inner = gelu_back(inner, grad_hidden).astype(jnp.bfloat16)
    grad_w_in = jnp.einsum("bsf,bsd->fd", grad_inner, normed, preferred_element_type=jnp.float32)
    grad_normed = jnp.einsum("bsf,fd->bsd", grad_inner, w_in_t, preferred_element_type=jnp.float32)
    grad_in, grad_gain, grad_shift = norm_back(inputs, norm_gain, norm_shift, grad_normed)
    return (
        grad_result + grad_in,
        [grad_w_in, grad_w_out],
        [grad_gain, grad_shift, row_sum(grad_low), row_sum(grad_inner)],
    )


def encode(image_mb, keep, mats, vecs):
    inputs = image_mb.astype(jnp.float32)
    allowed = (keep > 0.5)[:, None, None, :]
    middle, saved_self = self_block(inputs, allowed, mats, vecs)
    result, saved_mlp = mlp_block(
        middle,
        mats[4 * D : 4 * D + FF],
        mats[4 * D + FF :],
        part_of(vecs, 5),
        part_of(vecs, 6),
        vecs[8 * D : 8 * D + FF].astype(jnp.float32),
        part_of(vecs, 7),
    )
    output = (result * keep[..., None]).astype(jnp.bfloat16)
    return (output, (inputs, allowed, middle, saved_self, saved_mlp))


def encode_back(saved, keep, mats, vecs, grad_out):
    inputs, allowed, middle, saved_self, saved_mlp = saved
    grad_result = grad_out.astype(jnp.float32) * keep[..., None]
    grad_middle, mats_mlp, vecs_mlp = mlp_block_back(
        middle,
        mats[4 * D : 4 * D + FF],
        mats[4 * D + FF :],
        part_of(vecs, 5),
        part_of(vecs, 6),
        saved_mlp,
        grad_result,
    )
    grad_inputs, mats_self, vecs_self = self_block_back(
        inputs, allowed, mats, vecs, saved_self, grad_middle
    )
    return (grad_inputs, mats_self + mats_mlp, vecs_self + vecs_mlp)


def decode(text_mb, image_rows, keep, length, mats, vecs):
    inputs = text_mb.astype(jnp.float32)
    positions = jnp.arange(inputs.shape[1])
    causal = (positions[None, :] <= positions[:, None])[None, None] & (
        positions[None, None, None, :] < length[:, None, None, None]
    )
    crossing = (keep > 0.5)[:, None, None, :]
    after_self, saved_self = self_block(inputs, causal, mats, vecs)
    after_cross, saved_cross = cross_block(after_self, image_rows, crossing, mats, vecs)
    result, saved_mlp = mlp_block(
        after_cross,
        mats[8 * D : 8 * D + FF],
        mats[8 * D + FF :],
        part_of(vecs, 10),
        part_of(vecs, 11),
        vecs[13 * D : 13 * D + FF].astype(jnp.float32),
        part_of(vecs, 12),
    )
    return (
        result.astype(jnp.bfloat16),
        (
            inputs,
            image_rows,
            causal,
            crossing,
            after_self,
            after_cross,
            saved_self,
            saved_cross,
            saved_mlp,
        ),
    )


def decode_back(saved, mats, vecs, grad_out):
    (
        inputs,
        image_rows,
        causal,
        crossing,
        after_self,
        after_cross,
        saved_self,
        saved_cross,
        saved_mlp,
    ) = saved
    grad_result = grad_out.astype(jnp.float32)
    grad_cross, mats_mlp, vecs_mlp = mlp_block_back(
        after_cross,
        mats[8 * D : 8 * D + FF],
        mats[8 * D + FF :],
        part_of(vecs, 10),
        part_of(vecs, 11),
        saved_mlp,
        grad_result,
    )
    grad_self, grad_image, mats_cross, vecs_cross = cross_block_back(
        after_self, image_rows, crossing, mats, vecs, saved_cross, grad_cross
    )
    grad_inputs, mats_self, vecs_self = self_block_back(
        inputs, causal, mats, vecs, saved_self, grad_self
    )
    return (
        grad_inputs,
        grad_image,
        mats_self + mats_cross + mats_mlp,
        vecs_self + vecs_cross + vecs_mlp,
    )


def body_plain(images, text, enc_mats, enc_vecs, dec_mats, dec_vecs, tissue, text_len, enc_cot, dec_cot):
    first = lax.axis_index("section") == 0
    shards = lax.axis_size("dp")
    img_count, slots = tissue.shape
    batch = img_count // MICRO
    text_rows = text.shape[0] // img_count
    enc_rows, dec_rows = (enc_mats.shape[0], dec_mats.shape[0])
    enc_len, dec_len = (enc_vecs.shape[0], dec_vecs.shape[0])
    keep_all = tissue.astype(jnp.float32).reshape(MICRO, batch, slots)
    image_in = images.reshape(MICRO, batch, slots, D)
    text_in = text.reshape(MICRO, batch, text_rows, D)
    length_in = text_len.reshape(MICRO, batch)
    image_cot = enc_cot.reshape(MICRO, batch, slots, D)
    text_cot = dec_cot.reshape(MICRO, batch, text_rows, D)

    def enc_view(weights):
        mats_part = (
            weights[0].reshape(shards, dec_rows, D)[:, :enc_rows].reshape(shards * enc_rows, D)
        )
        vecs_part = weights[1].reshape(shards, dec_len)[:, :enc_len].reshape(shards * enc_len)
        return (mats_part, vecs_part)

    def dec_view(weights):
        return (weights[0], weights[1])

    def to_padded(grad_mats, grad_vecs):
        mats_part = jnp.pad(
            grad_mats.reshape(shards, enc_rows, D), ((0, 0), (0, dec_rows - enc_rows), (0, 0))
        )
        vecs_part = jnp.pad(grad_vecs.reshape(shards, enc_len), ((0, 0), (0, dec_len - enc_len)))
        return (mats_part.reshape(shards * dec_rows, D), vecs_part.reshape(shards * dec_len))

    mats_pad = jnp.pad(enc_mats, ((0, dec_rows - enc_rows), (0, 0)))
    vecs_pad = jnp.pad(enc_vecs, (0, dec_len - enc_len))
    own_mats = jnp.where(first, mats_pad, dec_mats)
    own_vecs = jnp.where(first, vecs_pad, dec_vecs)
    weights = (
        lax.all_gather(own_mats, "dp", axis=0, tiled=True),
        lax.all_gather(own_vecs, "dp", axis=0, tiled=True),
    )
    zero_image = jnp.zeros((batch, slots, D), jnp.bfloat16)
    zero_text = jnp.zeros((batch, text_rows, D), jnp.bfloat16)
    encoded = [zero_image] * MICRO
    decoded = [zero_text] * MICRO
    for tick in range(MICRO + 1):

        def forward_encoder_work():
            if tick < MICRO:
                mats_part, vecs_part = enc_view(weights)
                return (encode(image_in[tick], keep_all[tick], mats_part, vecs_part)[0], zero_text)
            return (zero_image, zero_text)

        def forward_decoder_work():
            if tick > 0:
                mats_part, vecs_part = dec_view(weights)
                made = decode(
                    text_in[tick - 1],
                    encoded[tick - 1],
                    keep_all[tick - 1],
                    length_in[tick - 1],
                    mats_part,
                    vecs_part,
                )[0]
                return (zero_image, made)
            return (zero_image, zero_text)

        made_image, made_text = lax.cond(first, forward_encoder_work, forward_decoder_work)
        if tick < MICRO:
            arrived = shifted(made_image, "section", 1)
            encoded[tick] = jnp.where(first, made_image, arrived)
        if tick > 0:
            decoded[tick - 1] = made_text
    back_weights = weights
    zero_image_grad = jnp.zeros((batch, slots, D), jnp.float32)
    zero_text_grad = jnp.zeros((batch, text_rows, D), jnp.float32)
    zero_mats = jnp.zeros((shards * dec_rows, D), jnp.float32)
    zero_vecs = jnp.zeros((shards * dec_len,), jnp.float32)
    returned = [zero_image] * MICRO
    image_grads = [zero_image_grad] * MICRO
    text_grads = [zero_text_grad] * MICRO
    total_mats, total_vecs = (zero_mats, zero_vecs)
    for tick in range(MICRO + 1):

        def backward_encoder_work():
            if tick > 0:
                index = MICRO - tick
                mats_part, vecs_part = enc_view(back_weights)
                _, saved = encode(image_in[index], keep_all[index], mats_part, vecs_part)
                grad_in, grad_mats, grad_vecs = encode_back(
                    saved, keep_all[index], mats_part, vecs_part, returned[index]
                )
                grad_mats, grad_vecs = to_padded(
                    jnp.concatenate(grad_mats, axis=0), jnp.concatenate(grad_vecs, axis=0)
                )
                return (zero_image, zero_text_grad, grad_in, grad_mats, grad_vecs)
            return (zero_image, zero_text_grad, zero_image_grad, zero_mats, zero_vecs)

        def backward_decoder_work():
            if tick < MICRO:
                index = MICRO - 1 - tick
                mats_part, vecs_part = dec_view(back_weights)
                _, saved = decode(
                    text_in[index],
                    encoded[index],
                    keep_all[index],
                    length_in[index],
                    mats_part,
                    vecs_part,
                )
                grad_text, grad_image, grad_mats, grad_vecs = decode_back(
                    saved, mats_part, vecs_part, text_cot[index]
                )
                grad_mats = jnp.concatenate(grad_mats, axis=0)
                grad_vecs = jnp.concatenate(grad_vecs, axis=0)
                outgoing = (grad_image + image_cot[index].astype(jnp.float32)).astype(jnp.bfloat16)
                return (outgoing, grad_text, zero_image_grad, grad_mats, grad_vecs)
            return (zero_image, zero_text_grad, zero_image_grad, zero_mats, zero_vecs)

        outgoing, grad_text, grad_in, grad_mats, grad_vecs = lax.cond(
            first, backward_encoder_work, backward_decoder_work
        )
        if tick == 0:
            total_mats, total_vecs = (grad_mats, grad_vecs)
        else:
            total_mats = total_mats + grad_mats
            total_vecs = total_vecs + grad_vecs
        if tick < MICRO:
            returned[MICRO - 1 - tick] = shifted(outgoing, "section", -1)
            text_grads[MICRO - 1 - tick] = grad_text
        if tick > 0:
            image_grads[MICRO - tick] = grad_in
    shard_mats, shard_vecs = (
        lax.psum_scatter(total_mats, "dp", scatter_dimension=0, tiled=True),
        lax.psum_scatter(total_vecs, "dp", scatter_dimension=0, tiled=True),
    )
    image_grad_all = jnp.concatenate(image_grads, axis=0).reshape(-1, D)
    text_grad_all = jnp.concatenate(text_grads, axis=0).reshape(-1, D)
    decoded_all = jnp.concatenate(decoded, axis=0).reshape(-1, D).astype(jnp.float32)
    enc_mats_own = jnp.where(first, shard_mats[:enc_rows], 0.0)
    enc_vecs_own = jnp.where(first, shard_vecs[:enc_len], 0.0)
    dec_mats_own = jnp.where(first, 0.0, shard_mats)
    dec_vecs_own = jnp.where(first, 0.0, shard_vecs)
    image_own = jnp.where(first, image_grad_all, 0.0)
    decoded_own = jnp.where(first, 0.0, decoded_all)
    text_own = jnp.where(first, 0.0, text_grad_all)
    combined = (
        lax.psum(enc_mats_own.astype(jnp.bfloat16), "section").astype(jnp.float32),
        lax.psum(enc_vecs_own.astype(jnp.bfloat16), "section").astype(jnp.float32),
        lax.psum(dec_mats_own.astype(jnp.bfloat16), "section").astype(jnp.float32),
        lax.psum(dec_vecs_own.astype(jnp.bfloat16), "section").astype(jnp.float32),
        lax.psum(image_own.astype(jnp.bfloat16), "section").astype(jnp.float32),
        lax.psum(decoded_own.astype(jnp.bfloat16), "section").astype(jnp.float32),
        lax.psum(text_own.astype(jnp.bfloat16), "section").astype(jnp.float32),
    )
    enc_mats_grad, enc_vecs_grad, dec_mats_grad, dec_vecs_grad, image_grad, dec_full, text_grad = (
        combined
    )
    dec_out = dec_full.astype(jnp.bfloat16)
    enc_out = jnp.concatenate(encoded, axis=0).reshape(-1, D)
    return (
        enc_out,
        dec_out,
        image_grad,
        text_grad,
        enc_mats_grad,
        enc_vecs_grad,
        dec_mats_grad,
        dec_vecs_grad,
    )


MESH = pl.DeviceIdType.MESH
TILE = 16
ADD_ROWS = 32


def grid_of(shards):
    return (shards // 4, 2, 2)


def split_rows(rows, late):
    part = int(rows * late / 2) // TILE * TILE
    first = (rows - 2 * part) // 2 // TILE * TILE
    sizes = (first, rows - 2 * part - first, part, part)
    starts = (0, first, rows - 2 * part, rows - part)
    return tuple(zip(starts, sizes))


class Place:
    def __init__(self, depth):
        self.section = lax.axis_index("section")
        self.me = lax.axis_index("dp")
        self.depth = depth
        self.z = lax.div(self.me, 4)
        self.y = lax.rem(lax.div(self.me, 2), 2)
        self.x = lax.rem(self.me, 2)

    def shard(self, z, y, x):
        return (z * 2 + y) * 2 + x

    def pair(self, first_x, z, first, second):
        return self.shard(z, second, first) if first_x else self.shard(z, first, second)

    def own(self, first_x):
        return (self.x, self.y) if first_x else (self.y, self.x)


class Copies:
    def __init__(self, place, waiting=False):
        self.place = place
        self.waiting = waiting

    def start(self, cond, src, dst, send_sem, recv_sem, dp, section=None):
        section = self.place.section if section is None else section

        def act():
            copy = pltpu.make_async_remote_copy(
                src_ref=src,
                dst_ref=dst,
                send_sem=send_sem,
                recv_sem=recv_sem,
                device_id=(section, dp),
                device_id_type=MESH,
            )
            if self.waiting:
                copy.wait_send()
            else:
                copy.start()

        if cond is None:
            act()
        else:
            pl.when(cond)(act)

    def arrived(self, dst, send_sem, recv_sem):
        if self.waiting:
            return
        pltpu.make_async_remote_copy(
            src_ref=dst,
            dst_ref=dst,
            send_sem=send_sem,
            recv_sem=recv_sem,
            device_id=(self.place.section, self.place.me),
            device_id_type=MESH,
        ).wait_recv()


def guarded(cond, step, *args):
    if cond is None:
        step(*args)
    else:
        pl.when(cond)(functools.partial(step, *args))


def greet(place, shards, both):
    barrier = pltpu.get_barrier_semaphore()
    for step in range(1, shards):
        pl.semaphore_signal(
            barrier,
            inc=1,
            device_id=(place.section, lax.rem(place.me + step, shards)),
            device_id_type=MESH,
        )
    if both:
        pl.semaphore_signal(
            barrier, inc=1, device_id=(1 - place.section, place.me), device_id_type=MESH
        )
    pl.semaphore_wait(barrier, shards - 1 + int(both))


class Gather:
    def __init__(self, copies, place, depth, rows, cuts, w, send_sems, recv_sems, gate):
        self.copies = copies
        self.gate = gate
        self.place = place
        self.depth = depth
        self.rows = rows
        self.cuts = cuts
        self.w = w
        self.send_sems = send_sems
        self.recv_sems = recv_sems
        self.late = (2, 3) if cuts[2][1] else ()

    def piece(self, cls, shard):
        start, size = self.cuts[cls]
        return self.w.at[pl.ds(pl.multiple_of(shard * self.rows + start, TILE), size)]

    def send(self, cls, shard, way, dp):
        piece = self.piece(cls, shard)
        self.copies.start(
            None, piece, piece, self.send_sems.at[cls, shard, way], self.recv_sems.at[cls, shard], dp
        )

    def arrived(self, cls, shard):
        self.copies.arrived(
            self.piece(cls, shard), self.send_sems.at[cls, shard, 0], self.recv_sems.at[cls, shard]
        )

    def along(self, plane, distance, act):
        z, last = self.place.z, self.depth - 1
        if distance == 0:
            pl.when(z == plane)(lambda: act(plane, plane < last, plane > 0))
            return
        if plane + distance <= last:
            pl.when(z == plane + distance)(
                lambda: act(plane + distance, plane + distance < last, False)
            )
        if plane - distance >= 0:
            pl.when(z == plane - distance)(
                lambda: act(plane - distance, False, plane - distance > 0)
            )

    def L(self, plane, distance):
        place = self.place

        def act(at, up, down):
            shard = place.shard(plane, place.y, place.x)
            for cls in (0, 1):
                a, b = place.own(cls == 0)
                if distance:
                    self.arrived(cls, shard)
                if up:
                    self.send(cls, shard, 0, place.me + 4)
                if down:
                    self.send(cls, shard, 1, place.me - 4)
                self.send(cls, shard, 2, place.pair(cls == 0, at, 1 - a, b))

        self.along(plane, distance, act)

    def G(self, plane, distance):
        place = self.place

        def act(at, up, down):
            for cls in (0, 1):
                a, b = place.own(cls == 0)
                other = place.pair(cls == 0, plane, 1 - a, b)
                self.arrived(cls, other)
                to = place.pair(cls == 0, at, a, 1 - b)
                self.send(cls, place.shard(plane, place.y, place.x), 3, to)
                self.send(cls, other, 3, to)

        self.along(plane, distance, act)

    def H(self, plane):
        place = self.place
        for cls in (0, 1):
            a, b = place.own(cls == 0)
            self.arrived(cls, place.pair(cls == 0, plane, a, 1 - b))
            self.arrived(cls, place.pair(cls == 0, plane, 1 - a, 1 - b))

    def X(self):
        if not self.copies.waiting:
            self.gate()

    def M(self):
        place = self.place
        for cls in self.late:
            a, b = place.own(cls == 2)
            self.send(cls, place.me, 2, place.pair(cls == 2, place.z, 1 - a, b))

    def N(self):
        place = self.place
        for cls in self.late:
            a, b = place.own(cls == 2)
            other = place.pair(cls == 2, place.z, 1 - a, b)
            self.arrived(cls, other)
            to = place.pair(cls == 2, place.z, a, 1 - b)
            self.send(cls, place.me, 3, to)
            self.send(cls, other, 3, to)

    def T(self, plane, distance):
        place = self.place

        def act(at, up, down):
            for cls in self.late:
                a, b = place.own(cls == 2)
                if distance == 0:
                    self.arrived(cls, place.pair(cls == 2, plane, a, 1 - b))
                    self.arrived(cls, place.pair(cls == 2, plane, 1 - a, 1 - b))
                for index in range(4):
                    shard = plane * 4 + index
                    if distance:
                        self.arrived(cls, shard)
                    if up:
                        self.send(cls, shard, 0, place.me + 4)
                    if down:
                        self.send(cls, shard, 1, place.me - 4)

        self.along(plane, distance, act)


def add_rows(total, total_start, part, part_start, size):
    step = next(n for n in (64, 48, 32, TILE) if size % n == 0)

    @pl.loop(0, size // step)
    def _(index):
        at = pl.ds(pl.multiple_of(total_start + index * step, TILE), step)
        of = pl.ds(pl.multiple_of(part_start + index * step, TILE), step)
        total[at] = total[at] + part[of]


class Scatter:
    def __init__(self, copies, place, depth, rows, cuts, g, land, send_sems, recv_sems, done):
        self.copies = copies
        self.done = done
        self.place = place
        self.depth = depth
        self.rows = rows
        self.cuts = cuts
        self.g = g
        self.land = land
        self.send_sems = send_sems
        self.recv_sems = recv_sems
        self.late = (2, 3) if cuts[2][1] else ()
        self.early_slots = 4 * depth + 1
        self.late_slots = 4 * depth + 7

    @staticmethod
    def land_rows(depth, cuts):
        early = (4 * depth + 1) * (cuts[0][1] + cuts[1][1])
        return early + (4 * depth + 7) * (cuts[2][1] + cuts[3][1])

    def start_of(self, cls, shard):
        return pl.multiple_of(shard * self.rows + self.cuts[cls][0], TILE)

    def slot_start(self, cls, slot):
        base = 0
        for other in range(cls):
            base += (self.early_slots if other < 2 else self.late_slots) * self.cuts[other][1]
        return base + slot * self.cuts[cls][1]

    def slot_ref(self, cls, slot):
        return self.land.at[pl.ds(self.slot_start(cls, slot), self.cuts[cls][1])]

    def send(self, cls, shard, slot, dp):
        self.copies.start(
            None,
            self.g.at[pl.ds(self.start_of(cls, shard), self.cuts[cls][1])],
            self.slot_ref(cls, slot),
            self.send_sems.at[cls, slot],
            self.recv_sems.at[cls, slot],
            dp,
        )

    def take(self, cls, shard, slot):
        if self.copies.waiting:
            return
        self.copies.arrived(
            self.slot_ref(cls, slot), self.send_sems.at[cls, slot], self.recv_sems.at[cls, slot]
        )
        add_rows(
            self.g,
            self.start_of(cls, shard),
            self.land,
            self.slot_start(cls, slot),
            self.cuts[cls][1],
        )

    def A(self, plane):
        place = self.place
        for cls in (0, 1):
            first_x = cls == 0
            a, b = place.own(first_x)
            to = place.pair(first_x, place.z, 1 - a, b)
            self.send(cls, place.pair(first_x, plane, 1 - a, 1 - b), plane * 3, to)
            self.send(cls, place.pair(first_x, plane, 1 - a, b), plane * 3 + 1, to)

    def B(self, plane):
        place = self.place
        for cls in (0, 1):
            first_x = cls == 0
            a, b = place.own(first_x)
            away = place.pair(first_x, plane, a, 1 - b)
            self.take(cls, away, plane * 3)
            self.send(cls, away, plane * 3 + 2, place.pair(first_x, place.z, a, 1 - b))
        for cls in (0, 1):
            first_x = cls == 0
            a, b = place.own(first_x)
            self.take(cls, place.pair(first_x, plane, a, b), plane * 3 + 1)

    def P(self, plane):
        place = self.place
        for cls in (0, 1):
            self.take(cls, place.shard(plane, place.y, place.x), plane * 3 + 2)

    def hop(self, plane, number, act):
        z = self.place.z
        low, high = number - 1, self.depth - number
        if low < plane:
            pl.when(z == low)(lambda: act(1, low + 1 == plane))
        if high > plane:
            pl.when(z == high)(lambda: act(-1, high - 1 == plane))

    def Z(self, plane, number):
        place = self.place
        slot = 3 * self.depth + plane

        def act(way, ends):
            shard = place.shard(plane, place.y, place.x)
            for cls in (0, 1):
                if number > 1:
                    self.take(cls, shard, slot)
                to = 4 * self.depth if ends and way < 0 else slot
                self.send(cls, shard, to, place.me + 4 * way)

        self.hop(plane, number, act)

    def E(self, plane):
        place = self.place

        @pl.when(place.z == plane)
        def _():
            shard = place.shard(plane, place.y, place.x)
            for cls in (0, 1):
                if plane > 0:
                    self.take(cls, shard, 3 * self.depth + plane)
                if plane < self.depth - 1:
                    self.take(cls, shard, 4 * self.depth)
                if not self.copies.waiting:
                    self.done(cls)

    def Q(self, plane, number):
        place = self.place

        def act(way, ends):
            for cls in self.late:
                for index in range(4):
                    slot = plane * 4 + index
                    if number > 1:
                        self.take(cls, slot, slot)
                    to = 4 * self.depth + index if ends and way < 0 else slot
                    self.send(cls, slot, to, place.me + 4 * way)

        self.hop(plane, number, act)

    def R(self, plane):
        place = self.place
        base = 4 * self.depth + 4

        @pl.when(place.z == plane)
        def _():
            for cls in self.late:
                for index in range(4):
                    slot = plane * 4 + index
                    if plane > 0:
                        self.take(cls, slot, slot)
                    if plane < self.depth - 1:
                        self.take(cls, slot, 4 * self.depth + index)
                first_x = cls == 2
                a, b = place.own(first_x)
                to = place.pair(first_x, plane, 1 - a, b)
                self.send(cls, place.pair(first_x, plane, 1 - a, 1 - b), base, to)
                self.send(cls, place.pair(first_x, plane, 1 - a, b), base + 1, to)

    def S(self, plane):
        place = self.place
        base = 4 * self.depth + 4

        @pl.when(place.z == plane)
        def _():
            for cls in self.late:
                first_x = cls == 2
                a, b = place.own(first_x)
                away = place.pair(first_x, plane, a, 1 - b)
                self.take(cls, away, base)
                self.send(cls, away, base + 2, place.pair(first_x, plane, a, 1 - b))
            for cls in self.late:
                a, b = place.own(cls == 2)
                self.take(cls, place.pair(cls == 2, plane, a, b), base + 1)
            for cls in self.late:
                self.take(cls, place.me, base + 2)
                if not self.copies.waiting:
                    self.done(cls)


STEPS = "CLGHMNTABPZEQRSX"


LAG = 14


class Plan:
    def __init__(self, steps, copies, sent, stages):
        self.steps = steps
        self.copies = copies
        self.sent = sent
        self.stages = stages
        self.open = []

    @staticmethod
    def act(copies, step):
        kind, plane, hop = step // 100, step // 10 % 10, step % 10
        act = getattr(copies, STEPS[kind])
        if STEPS[kind] in "LGTZQ":
            act(plane, hop)
        elif STEPS[kind] in "MNX":
            act()
        else:
            act(plane)

    def run(self):
        for step in self.steps:
            if step < 100:
                self.stages[step]()
                continue
            self.act(self.copies, step)
            self.open.append(step)
            if len(self.open) > LAG:
                self.act(self.sent, self.open.pop(0))

    def flush(self):
        for step in self.open:
            self.act(self.sent, step)
        self.open.clear()


BLOCK = 256
LINES = 32
NORM_ROWS = 64
UNROLL = 3
ATTEND_UNROLL = 2
PAIRS = D // 128
VEC_UNIT = 48
VEC_ROWS = 32
F32 = jnp.float32
BF16 = jnp.bfloat16


def dot_nn(left, right):
    return lax.dot_general(left, right, (((1,), (0,)), ((), ())), preferred_element_type=F32)


def dot_nt(left, right):
    return lax.dot_general(left, right, (((1,), (1,)), ((), ())), preferred_element_type=F32)


def dot_tn(left, right):
    return lax.dot_general(left, right, (((0,), (0,)), ((), ())), preferred_element_type=F32)


def chunk(start, size=BLOCK):
    if isinstance(start, int):
        return pl.ds(start, size)
    return pl.ds(pl.multiple_of(start, 128 if size % 128 == 0 else TILE), size)


def iota(shape, dim):
    return lax.broadcasted_iota(jnp.int32, shape, dim)


def unit_of(column):
    return lax.shift_right_logical(column * 1366, 16)


def unit_spread():
    column = iota((128, D), 1)
    return (column - VEC_UNIT * unit_of(column) == iota((128, D), 0)).astype(BF16)


def vec_gathered(tiles, per):
    shards = tiles.shape[0]
    count = shards * VEC_ROWS
    spread = dot_nn(tiles[...].reshape(count, 128), unit_spread())
    row = iota((count, D), 0)
    inner = row & (VEC_ROWS - 1)
    unit = lax.shift_right_logical(row, 5) * per + inner
    mask = ((unit & 15) == unit_of(iota((count, D), 1))) & (inner < per)
    spread = jnp.where(mask, spread, 0.0).astype(BF16)
    row = iota((VEC_ROWS, count), 1)
    inner = row & (VEC_ROWS - 1)
    unit = lax.shift_right_logical(row, 5) * per + inner
    pick = (lax.shift_right_logical(unit, 4) == iota((VEC_ROWS, count), 0)) & (inner < per)
    return dot_nn(pick.astype(F32).astype(BF16), spread)


def exact_dot(pick, values, dot):
    high = values.astype(BF16)
    rest = values - high.astype(F32)
    middle = rest.astype(BF16)
    low = (rest - middle.astype(F32)).astype(BF16)
    return dot(pick, high) + dot(pick, middle) + dot(pick, low)


def vec_shard(rows, me, per):
    unit = me * per + iota((VEC_ROWS, VEC_ROWS), 0)
    pick = (lax.shift_right_logical(unit, 4) == iota((VEC_ROWS, VEC_ROWS), 1)).astype(F32)
    lines = exact_dot(pick.astype(BF16), rows, dot_nn)
    unit = me * per + iota((VEC_ROWS, D), 0)
    mask = (unit & 15) == unit_of(iota((VEC_ROWS, D), 1))
    lines = jnp.where(mask, lines, 0.0)
    spread = unit_spread()
    return exact_dot(spread, lines, lambda pick, part: dot_nt(part, pick))


def in_line(tile):
    group = 8 * VEC_UNIT
    column = iota((128, group), 1)
    pick = (column - VEC_UNIT * unit_of(column) == iota((128, group), 0)).astype(F32)
    spread = exact_dot(pick.astype(BF16), tile, lambda pick, part: dot_nn(part, pick))
    mask = (iota((VEC_ROWS, group), 0) & 7) == unit_of(iota((VEC_ROWS, group), 1))
    spread = jnp.where(mask, spread, 0.0)
    gather = lax.shift_right_logical(iota((8, VEC_ROWS), 1), 3) == iota((8, VEC_ROWS), 0)
    lines = exact_dot(gather.astype(F32).astype(BF16), spread, dot_nn)
    rows = [lines[row // 3 : row // 3 + 1, row % 3 * 128 : row % 3 * 128 + 128] for row in range(8)]
    return jnp.concatenate(rows, axis=0)


class Compute:
    def __init__(self, w, vrows, gvec, red):
        self.w = w
        self.vrows = vrows
        self.gvec = gvec
        self.red = red

    def vec(self, index):
        return self.vrows[pl.ds(index, 1), :]

    def norm(self, src, src_row, dst, dst_row, rows, gain, shift, unit, unit_row, rate, rate_row):
        scale_vec, shift_vec = self.vec(gain), self.vec(shift)

        @pl.loop(0, rows // NORM_ROWS)
        def _(index):
            x = src[chunk(src_row + index * NORM_ROWS, NORM_ROWS), :].astype(F32)
            centre = x - jnp.mean(x, axis=-1, keepdims=True)
            spread = jnp.mean(centre * centre, axis=-1, keepdims=True)
            scale = lax.rsqrt(spread + 1e-06)
            even = centre * scale
            result = even * scale_vec + shift_vec
            dst[chunk(dst_row + index * NORM_ROWS, NORM_ROWS), :] = result.astype(BF16)
            if unit is not None:
                unit[chunk(unit_row + index * NORM_ROWS, NORM_ROWS), :] = even.astype(unit.dtype)
            rate[chunk(rate_row + index * NORM_ROWS, NORM_ROWS), :] = jnp.broadcast_to(
                scale, (NORM_ROWS, 128)
            )

    def unit_rows(self, src, rows):
        @pl.loop(0, rows // NORM_ROWS)
        def _(index):
            at = chunk(index * NORM_ROWS, NORM_ROWS)
            x = src[at, :].astype(F32)
            centre = x - jnp.mean(x, axis=-1, keepdims=True)
            spread = jnp.mean(centre * centre, axis=-1, keepdims=True)
            src[at, :] = (centre * lax.rsqrt(spread + 1e-06)).astype(src.dtype)

    def norm_back(
        self, unit, unit_row, rate, rate_row, grad, rest, out, low, rows, gain, shift
    ):
        scale_vec = self.vec(gain)
        self.red[...] = jnp.zeros_like(self.red)

        @pl.loop(0, rows // NORM_ROWS)
        def _(index):
            at = chunk(index * NORM_ROWS, NORM_ROWS)
            even = unit[chunk(unit_row + index * NORM_ROWS, NORM_ROWS), :].astype(F32)
            scale = rate[chunk(rate_row + index * NORM_ROWS, NORM_ROWS), 0:1]
            d = grad[at, :]
            along = d * even
            self.red[0] += jnp.sum(along.reshape(NORM_ROWS // 8, 8, D), axis=0)
            self.red[1] += jnp.sum(d.reshape(NORM_ROWS // 8, 8, D), axis=0)
            d = d * scale_vec
            mean = jnp.mean(d, axis=-1, keepdims=True)
            along = jnp.mean(along * scale_vec, axis=-1, keepdims=True)
            total = rest[at, :].astype(F32) + scale * (d - mean - even * along)
            if out is not None:
                out[at, :] = total
            if low is not None:
                low[at, :] = total.astype(BF16)

        self.gvec[pl.ds(gain, 1), :] = jnp.sum(self.red[0], axis=0, keepdims=True)
        self.gvec[pl.ds(shift, 1), :] = jnp.sum(self.red[1], axis=0, keepdims=True)

    def row_sum(self, values):
        ones = jnp.ones((TILE, values.shape[0]), BF16)
        return dot_nn(ones, values)[0:1]

    def linear(self, src, row, rows, index, bias, emit):
        @pl.loop(0, D // BLOCK, unroll=UNROLL)
        def _(part):
            cols = chunk(part * BLOCK)
            made = dot_nn(src[pl.ds(row, rows), :], self.w[chunk(index * D, D), cols])
            if bias is not None:
                made = made + self.vrows[pl.ds(bias, 1), cols]
            emit(cols, made)

    def linear_back(self, pairs, emit):
        @pl.loop(0, D // BLOCK, unroll=UNROLL)
        def _(part):
            total = None
            for grad, index in pairs:
                made = dot_nt(grad(), self.w[chunk(index * D + part * BLOCK), :])
                total = made if total is None else total + made
            emit(chunk(part * BLOCK), total)

    def weight_grad(self, left, right, index, parts=D // BLOCK):
        @pl.loop(0, parts, unroll=UNROLL)
        def _(part):
            total = None
            for one, other in zip(left(part), right):
                made = dot_tn(one, other())
                total = made if total is None else total + made
            self.w[chunk(index * D + part * BLOCK), :] = total.astype(BF16)

    def hidden(self, src, row, rows, first, bias, act, slope, pieces=(0, FF // D)):
        each = D // BLOCK

        @pl.loop(pieces[0] * each, pieces[1] * each, unroll=UNROLL)
        def _(part):
            piece = lax.div(part, each)
            u = dot_nt(src[pl.ds(row, rows), :], self.w[chunk(first * D + part * BLOCK), :])
            u = u + self.vrows[pl.ds(bias + piece, 1), chunk(lax.rem(part, each) * BLOCK)]
            square = u * u
            t = jnp.tanh(u * (0.7978845608028654 + 0.035677408136300125 * square))
            half = 0.5 + 0.5 * t
            at = (pl.ds(0, rows), chunk(part * BLOCK))
            made = u * half
            act[at] = made.astype(BF16)
            rise = 1.5957691216057308 + 0.21406444881780074 * square
            slope[at] = (half + made * (1.0 - half) * rise).astype(BF16)

    def project(self, act, rows, first, emit):
        @pl.loop(0, D // BLOCK)
        def _(part):
            cols = chunk(part * BLOCK)
            emit(cols, dot_nn(act[pl.ds(0, rows), :], self.w[chunk(first * D, FF), cols]))

    def hidden_back(self, low, rows, first, slope):
        @pl.loop(0, FF // BLOCK, unroll=UNROLL)
        def _(part):
            made = dot_nt(low[pl.ds(0, rows), :], self.w[chunk(first * D + part * BLOCK), :])
            at = (pl.ds(0, rows), chunk(part * BLOCK))
            slope[at] = (made * slope[at].astype(F32)).astype(BF16)

    def wide_grad(self, left, rows, right, first):
        self.weight_grad(
            lambda part: [left[pl.ds(0, rows), chunk(part * BLOCK)]], [right], first, FF // BLOCK
        )

    def wide_sums(self, slope, rows, bias):
        for piece in range(FF // D):
            self.gvec[pl.ds(bias + piece, 1), :] = self.row_sum(
                slope[pl.ds(0, rows), pl.ds(piece * D, D)]
            )

    @staticmethod
    def halves(tile, scale=1.0):
        low = jnp.where(iota(tile.shape, 1) < HEAD, scale, 0.0).astype(BF16)
        high = jnp.where(iota(tile.shape, 1) < HEAD, 0.0, scale).astype(BF16)
        return tile * low, tile * high

    def attend(self, allowed, q_at, k_at, v_at, p_at, o_at):
        @pl.loop(0, PAIRS, unroll=ATTEND_UNROLL)
        def _(pair):
            keys = k_at(pair)[...]
            values = v_at(pair)[...].T
            mixed = []
            for half, queries in enumerate(self.halves(q_at(pair)[...], 0.125)):
                scores = jnp.where(allowed, dot_nt(keys, queries), -1000000000.0)
                expd = jnp.exp(scores - jnp.max(scores, axis=0, keepdims=True))
                rate = 1.0 / jnp.sum(expd, axis=0, keepdims=True)
                probs = (expd * rate).astype(BF16)
                p_at(pair, half)[...] = probs
                mixed.append(dot_nn(values, probs)[half * HEAD : (half + 1) * HEAD])
            o_at(pair)[...] = jnp.concatenate(mixed, axis=0).T.astype(BF16)

    def attend_back(self, q_at, k_at, v_at, p_at, do_at):
        @pl.loop(0, PAIRS, unroll=ATTEND_UNROLL)
        def _(pair):
            keys = k_at(pair)[...].T
            values = v_at(pair)[...]
            grad_q, grad_k, grad_v = [], 0.0, 0.0
            both = zip(self.halves(q_at(pair)[...], 0.125), self.halves(do_at(pair)[...]))
            for half, (queries, grads) in enumerate(both):
                low = p_at(pair, half)[...]
                probs = low.astype(F32)
                grad_probs = dot_nt(values, grads)
                inner = jnp.sum(probs * grad_probs, axis=0, keepdims=True)
                grad_scores = (probs * (grad_probs - inner)).astype(BF16)
                grad_q.append(dot_nn(keys, grad_scores)[half * HEAD : (half + 1) * HEAD])
                grad_k = grad_k + dot_nn(grad_scores, queries)
                grad_v = grad_v + dot_nn(low, grads)
            q_at(pair)[...] = (jnp.concatenate(grad_q, axis=0) * 0.125).T.astype(BF16)
            k_at(pair)[...] = grad_k.astype(BF16)
            v_at(pair)[...] = grad_v.astype(BF16)


def store_to(ref, row, rows, col=0):
    def emit(cols, values):
        ref[pl.ds(row, rows), chunk(col + cols.start)] = values.astype(ref.dtype)

    return emit


def fused_kernel(
    depth,
    sizes,
    pers,
    slots,
    words,
    images_in,
    enc_cot,
    tissue,
    text_len,
    text_in,
    enc_in,
    dec_in,
    enc_tile,
    dec_tile,
    dec_cot,
    enc_out,
    dec_out,
    image_out,
    text_out,
    enc_g,
    dec_g,
    enc_v,
    dec_v,
    w,
    land,
    xin,
    n1,
    q,
    k,
    v,
    o,
    h,
    n2,
    act,
    gp,
    e,
    cot,
    acc,
    dh,
    low,
    dmix,
    keep_col,
    rates,
    tiles,
    vrows,
    gvec,
    vland,
    vout,
    red,
    load_sems,
    ag_send,
    ag_recv,
    vec_send,
    vec_recv,
    rs_send,
    rs_recv,
    sum_send,
    sum_recv,
    x_send,
    x_recv,
    out_local,
    out_send,
    out_recv,
    gate_sem,
):
    shards = depth * 4
    place = Place(depth)
    me, z = place.me, place.z
    section = place.section
    image_rows, text_rows = xin.shape[0], text_in.shape[0]
    images, used = tissue.shape
    comp = Compute(w, vrows, gvec, red)
    cuts = [split_rows(rows, LATE) for rows in sizes]

    def load(index, src, dst, waiting=False):
        copy = pltpu.make_async_copy(src, dst, load_sems.at[index])
        if waiting:
            copy.wait()
        else:
            copy.start()

    def own_rows(which):
        return w.at[pl.ds(pl.multiple_of(me * sizes[which], TILE), sizes[which])]

    def load_own(which, waiting):
        load(0, (enc_in, dec_in)[which], own_rows(which), waiting)
        load(1, (enc_tile, dec_tile)[which], tiles.at[me], waiting)

    def load_text(waiting):
        load(2, text_in, xin.at[pl.ds(0, text_rows)], waiting)
        load(3, dec_cot, low.at[pl.ds(0, text_rows)], waiting)

    for which in (0, 1):

        @pl.when(section == which)
        def _():
            load_own(which, False)
            if which == 1:
                load_text(False)

    greet(place, shards, True)

    def give_vecs(waiting):
        src = tiles.at[me]
        for step in range(1, shards):
            Copies(place, waiting).start(
                None, src, src, vec_send.at[step], vec_recv.at[me], lax.rem(me + step, shards)
            )

    def got_vecs():
        for step in range(1, shards):
            frm = lax.rem(me + step, shards)
            Copies(place).arrived(tiles.at[frm], vec_send.at[step], vec_recv.at[frm])

    def across(waiting, index, src, dst):
        Copies(place, waiting).start(
            None, src, dst, x_send.at[index], x_recv.at[index], me, 1 - section
        )

    def crossed(index, dst):
        Copies(place).arrived(dst, x_send.at[index], x_recv.at[index])

    def give(waiting, index, src, dst):
        local = pltpu.make_async_copy(src, dst, out_local.at[index])
        if waiting:
            local.wait()
        else:
            local.start()
        Copies(place, waiting).start(
            None, src, dst, out_send.at[index], out_recv.at[index], me, 1 - section
        )

    def got(index, dst):
        Copies(place).arrived(dst, out_send.at[index], out_recv.at[index])

    def share_sums(waiting, slot, to):
        Copies(place, waiting).start(
            None, gvec, vland.at[slot], sum_send.at[slot], sum_recv.at[slot], to
        )

    def got_sums(slot):
        Copies(place).arrived(vland.at[slot], sum_send.at[slot], sum_recv.at[slot])

    def open_gate():
        pl.semaphore_signal(
            gate_sem, inc=1, device_id=(1 - section, me), device_id_type=MESH
        )

    def pass_gate():
        pl.semaphore_wait(gate_sem, 1)

    flips = (place.shard(z, place.y, 1 - place.x), place.shard(z, 1 - place.y, place.x))

    def sum_stages(which):
        def along_x():
            share_sums(False, 0, flips[0])

        def along_y():
            got_sums(0)
            share_sums(True, 0, flips[0])
            gvec[...] = gvec[...] + vland[0]
            share_sums(False, 1, flips[1])

        def along_z():
            got_sums(1)
            share_sums(True, 1, flips[1])
            gvec[...] = gvec[...] + vland[1]
            for step in range(1, depth):
                share_sums(False, 1 + step, lax.rem(me + 4 * step, shards))

        def ended():
            summed = gvec[...]
            for step in range(1, depth):
                got_sums(1 + step)
                share_sums(True, 1 + step, lax.rem(me + 4 * step, shards))
                summed = summed + vland[1 + step]
            vout[...] = vec_shard(summed, me, pers[which])
            give(False, 6, vout, (enc_v, dec_v)[which])

        return {30: along_x, 31: along_y, 32: along_z, 33: ended}

    def gather(which, waiting=False):
        return Gather(
            Copies(place, waiting),
            place,
            depth,
            sizes[which],
            cuts[which],
            w,
            ag_send,
            ag_recv,
            open_gate if which == 0 else pass_gate,
        )

    def give_class(waiting, which, cls):
        start, size = cuts[which][cls]
        if size:
            src = w.at[pl.ds(pl.multiple_of(me * sizes[which] + start, TILE), size)]
            give(waiting, 2 + cls, src, (enc_g, dec_g)[which].at[pl.ds(start, size)])

    def got_class(which, cls):
        start, size = cuts[which][cls]
        if size:
            got(2 + cls, (enc_g, dec_g)[which].at[pl.ds(start, size)])

    def scatter(which, waiting=False):
        return Scatter(
            Copies(place, waiting),
            place,
            depth,
            sizes[which],
            cuts[which],
            w,
            land,
            rs_send,
            rs_recv,
            functools.partial(give_class, False, which),
        )

    def start_stage(which):
        got_vecs()
        vrows[...] = vec_gathered(tiles, pers[which])
        gvec[...] = jnp.zeros_like(gvec)

    def padded(src):
        row = iota((image_rows, src.shape[0]), 0)
        slot = row & (slots - 1)
        frm = lax.shift_right_logical(row, 8) * used + slot
        pick = (iota((image_rows, src.shape[0]), 1) == frm) & (slot < used)
        return dot_nn(pick.astype(F32).astype(BF16), src[...]).astype(BF16)

    def fill_keep():
        keep_col[...] = jnp.zeros_like(keep_col)
        for image in range(images):
            line = tissue[pl.ds(image, 1), :].astype(F32).astype(BF16)
            lines = jnp.broadcast_to(line, (TILE, used))
            keep_col[pl.ds(image * slots, used), :] = dot_tn(
                lines, jnp.full((TILE, 128), 1.0 / TILE, BF16)
            )

    def spread(column, wide):
        return jnp.concatenate([column] * (wide // 128), axis=1) > 0.5

    def section_program(which, make):
        stages = sum_stages(which)
        gathering = Plan(GATHER_PLANS[which], gather(which), gather(which, True), stages)
        scattering = Plan(SCATTER_PLANS[which], scatter(which), scatter(which, True), stages)

        def gathered():
            gathering.flush()
            give_vecs(True)

        made, last = make(gathered)
        stages.update(made)
        load_own(which, True)
        gathering.run()
        scattering.run()
        scattering.flush()
        for cls in range(4):
            give_class(True, which, cls)
        give(True, 6, vout, (enc_v, dec_v)[which])
        last()
        for cls in range(4):
            got_class(1 - which, cls)
        got(6, (enc_v, dec_v)[1 - which])

    def encoder(gathered):
        rows = image_rows
        every = pl.ds(0, rows)
        stages = {}

        def stage(number):
            def keep(step):
                stages[number] = step
                return step

            return keep

        spare = shards * sizes[0]

        def at(ref, image):
            return lambda pair: ref.at[pl.ds(image * slots, slots), chunk(pair * 128, 128)]

        def p_at(image):
            def of(pair, half):
                index = (image * PAIRS + pair) * 2 + half
                row = spare + lax.div(index, 3) * slots
                return w.at[chunk(row, slots), chunk(lax.rem(index, 3) * slots, slots)]

            return of

        stages[8] = lambda: give_vecs(False)

        @stage(0)
        def _():
            fill_keep()
            xin[...] = padded(images_in)
            start_stage(0)
            comp.norm(xin, 0, n1, 0, rows, 0, 1, None, 0, rates.at[0], 0)

        @stage(1)
        def _():
            comp.linear(n1, 0, rows, 0, 2, store_to(q, 0, rows))
            comp.linear(n1, 0, rows, 1, None, store_to(k, 0, rows))
            comp.linear(n1, 0, rows, 2, 3, store_to(v, 0, rows))

        @stage(2)
        def _():
            for image in range(images):
                allowed = spread(keep_col[pl.ds(image * slots, slots), :], slots)
                comp.attend(
                    allowed, at(q, image), at(k, image), at(v, image), p_at(image), at(o, image)
                )

        @stage(3)
        def _():
            def add_input(cols, values):
                h[every, cols] = xin[every, cols].astype(F32) + values

            comp.linear(o, 0, rows, 3, 4, add_input)
            comp.norm(h, 0, n2, 0, rows, 5, 6, dh, 0, rates.at[1], 0)

        @stage(4)
        def _():
            comp.hidden(n2, 0, rows, 4, 8, act, gp, (0, 2))

        @stage(5)
        def _():
            comp.hidden(n2, 0, rows, 4, 8, act, gp, (2, 4))

        @stage(6)
        def _():
            def add_middle(cols, values):
                keep = jnp.concatenate([keep_col[...]] * (BLOCK // 128), axis=1)
                made = h[every, cols] + values + vrows[pl.ds(7, 1), cols]
                e[every, cols] = (made * keep).astype(BF16)

            comp.project(act, rows, 8, add_middle)
            across(False, 0, e, e)
            load(5, e, enc_out)

        @stage(7)
        def _():
            gathered()

            comp.unit_rows(xin, rows)

        @stage(10)
        def _():
            crossed(1, cot)

            @pl.loop(0, rows // LINES)
            def _(index):
                some = chunk(index * LINES, LINES)
                low[some, :] = (cot[some, :].astype(F32) * keep_col[some, 0:1]).astype(BF16)

            gvec[pl.ds(7, 1), :] = comp.row_sum(low[...])

        @stage(11)
        def _():
            comp.hidden_back(low, rows, 8, gp)

        @stage(12)
        def _():
            comp.wide_grad(act, rows, lambda: low[...], 8)

        @stage(13)
        def _():
            comp.project(gp, rows, 4, store_to(acc, 0, rows))

        @stage(14)
        def _():
            comp.wide_sums(gp, rows, 8)
            comp.wide_grad(gp, rows, lambda: n2[...], 4)

        @stage(15)
        def _():
            comp.norm_back(dh, 0, rates.at[1], 0, acc, low, dh, low, rows, 5, 6)

        @stage(16)
        def _():
            comp.linear_back([(lambda: low[...], 3)], store_to(dmix, 0, rows))

        @stage(17)
        def _():
            gvec[pl.ds(4, 1), :] = comp.row_sum(low[...])
            comp.weight_grad(lambda part: [o[:, chunk(part * BLOCK)]], [lambda: low[...]], 3)

        def heads_back(image):
            comp.attend_back(
                at(q, image), at(k, image), at(v, image), p_at(image), at(dmix, image)
            )

        stages[18] = lambda: heads_back(0)
        stages[19] = lambda: [heads_back(image) for image in range(1, images)]

        @stage(20)
        def _():
            comp.linear_back(
                [(lambda: q[...], 0), (lambda: k[...], 1), (lambda: v[...], 2)],
                store_to(acc, 0, rows),
            )

        @stage(21)
        def _():
            gvec[pl.ds(2, 1), :] = comp.row_sum(q[...])
            gvec[pl.ds(3, 1), :] = comp.row_sum(v[...])
            for index, ref in enumerate((q, k, v)):
                comp.weight_grad(
                    lambda part: [n1[:, chunk(part * BLOCK)]], [lambda: ref[...]], index
                )

        @stage(22)
        def _():
            comp.norm_back(xin, 0, rates.at[0], 0, acc, dh, None, low, rows, 0, 1)
            give(False, 1, low, image_out)

        def last():
            across(True, 0, e, e)
            load(5, e, enc_out, True)
            give(True, 1, low, image_out)
            got(0, dec_out)
            got(1, text_out)

        return stages, last

    def decoder(gathered):
        half = text_rows
        lower, upper = pl.ds(0, half), pl.ds(half, half)
        stages = {}

        def stage(number):
            def keep(step):
                stages[number] = step
                return step

            return keep

        def at(ref, image, base=0):
            return lambda pair: ref.at[
                pl.ds(base + image * words, words), chunk(pair * 128, 128)
            ]

        def p_self(image):
            ref = (k, v)[image]

            def of(pair, side):
                row = half + lax.div(pair, 3) * words
                return ref.at[
                    chunk(row, words), chunk((lax.rem(pair, 3) * 2 + side) * words, words)
                ]

            return of

        def p_cross(image):
            return lambda pair, side: act.at[
                upper, chunk(((image * PAIRS + pair) * 2 + side) * words, words)
            ]

        def cross_kv(image, which):
            col = (which * images + image) * D
            return lambda pair: gp.at[pl.ds(half, slots), chunk(col + pair * 128, 128)]

        def pair_ref(image, which):
            return lambda: gp[pl.ds(half, slots), pl.ds((which * images + image) * D, D)]

        def low_rows():
            return low[lower, :]

        dz = dmix.at[upper]
        decoded = xin.at[upper]
        text_grad = low.at[upper]

        stages[29] = lambda: give_vecs(False)

        @stage(0)
        def _():
            load_text(True)
            fill_keep()
            cot[...] = padded(enc_cot)
            start_stage(1)
            comp.norm(xin, 0, n1, 0, half, 0, 1, n1, half, rates.at[0], 0)

        @stage(1)
        def _():
            comp.linear(n1, 0, half, 0, 2, store_to(q, 0, half))
            comp.linear(n1, 0, half, 1, None, store_to(k, 0, half))
            comp.linear(n1, 0, half, 2, 3, store_to(v, 0, half))

        @stage(2)
        def _():
            key, query = iota((words, words), 0), iota((words, words), 1)
            for image in range(images):
                allowed = (key <= query) & (key < text_len[image])
                comp.attend(
                    allowed, at(q, image), at(k, image), at(v, image), p_self(image), at(o, image)
                )

        @stage(3)
        def _():
            def add_input(cols, values):
                h[lower, cols] = xin[lower, cols].astype(F32) + values

            comp.linear(o, 0, half, 3, 4, add_input)
            comp.norm(h, 0, n2, 0, half, 5, 6, acc, half, rates.at[1], 0)

        @stage(4)
        def _():
            comp.linear(n2, 0, half, 4, 7, store_to(q, half, half))

        @stage(5)
        def _():
            crossed(0, e)
            load(5, e, enc_out)
            for image in range(images):
                row = image * slots
                comp.linear(e, row, slots, 5, None, store_to(gp, half, slots, image * D))
                comp.linear(e, row, slots, 6, 8, store_to(gp, half, slots, (images + image) * D))

        @stage(6)
        def _():
            for image in range(images):
                allowed = spread(keep_col[pl.ds(image * slots, slots), :], words)
                comp.attend(
                    allowed,
                    at(q, image, half),
                    cross_kv(image, 0),
                    cross_kv(image, 1),
                    p_cross(image),
                    at(o, image, half),
                )

        @stage(7)
        def _():
            def add_self(cols, values):
                h[upper, cols] = h[lower, cols] + values

            comp.linear(o, half, half, 7, 9, add_self)
            comp.norm(h, half, n2, half, half, 10, 11, dh, half, rates.at[2], 0)

        @stage(8)
        def _():
            comp.hidden(n2, half, half, 8, 13, act, gp)

        @stage(9)
        def _():
            def add_middle(cols, values):
                made = h[upper, cols] + values + vrows[pl.ds(12, 1), cols]
                xin[upper, cols] = made.astype(BF16)

            comp.project(act.at[lower], half, 12, add_middle)
            give(False, 0, decoded, dec_out)

        @stage(10)
        def _():
            comp.hidden_back(low, half, 12, gp)
            dz[...] = low_rows()

        @stage(11)
        def _():
            gathered()
            gvec[pl.ds(12, 1), :] = comp.row_sum(dz[...])
            comp.wide_grad(act, half, lambda: dz[...], 12)

        @stage(12)
        def _():
            comp.project(gp.at[lower], half, 8, store_to(acc, 0, half))

        @stage(13)
        def _():
            comp.wide_sums(gp, half, 13)
            comp.wide_grad(gp, half, lambda: n2[upper, :], 8)

        @stage(14)
        def _():
            comp.norm_back(dh, half, rates.at[2], 0, acc, low, dh, low, half, 10, 11)
            comp.linear_back([(low_rows, 7)], store_to(dmix, 0, half))

        @stage(15)
        def _():
            for image in range(images):
                comp.attend_back(
                    at(q, image, half),
                    cross_kv(image, 0),
                    cross_kv(image, 1),
                    p_cross(image),
                    at(dmix, image),
                )

        @stage(16)
        def _():
            for image in range(images):
                rows = pl.ds(image * slots, slots)

                def add_cot(cols, values):
                    cot[rows, cols] = (cot[rows, cols].astype(F32) + values).astype(BF16)

                comp.linear_back([(pair_ref(image, 0), 5), (pair_ref(image, 1), 6)], add_cot)
            across(False, 1, cot, cot)

        @stage(17)
        def _():
            gvec[pl.ds(9, 1), :] = comp.row_sum(low_rows())
            comp.weight_grad(lambda part: [o[upper, chunk(part * BLOCK)]], [low_rows], 7)

        @stage(18)
        def _():
            comp.linear_back([(lambda: q[upper, :], 4)], store_to(acc, 0, half))

        @stage(19)
        def _():
            gvec[pl.ds(7, 1), :] = comp.row_sum(q[upper, :])
            total = comp.row_sum(pair_ref(0, 1)())
            for image in range(1, images):
                total = total + comp.row_sum(pair_ref(image, 1)())
            gvec[pl.ds(8, 1), :] = total
            comp.weight_grad(
                lambda part: [n2[lower, chunk(part * BLOCK)]], [lambda: q[upper, :]], 4
            )
            for which in (0, 1):
                comp.weight_grad(
                    lambda part: [
                        e[pl.ds(image * slots, slots), chunk(part * BLOCK)]
                        for image in range(images)
                    ],
                    [pair_ref(image, which) for image in range(images)],
                    5 + which,
                )

        @stage(20)
        def _():
            comp.norm_back(acc, half, rates.at[1], 0, acc, dh, dh, low, half, 5, 6)

        @stage(21)
        def _():
            comp.linear_back([(low_rows, 3)], store_to(dmix, 0, half))

        @stage(22)
        def _():
            gvec[pl.ds(4, 1), :] = comp.row_sum(low_rows())
            comp.weight_grad(lambda part: [o[lower, chunk(part * BLOCK)]], [low_rows], 3)

        @stage(23)
        def _():
            for image in range(images):
                comp.attend_back(
                    at(q, image), at(k, image), at(v, image), p_self(image), at(dmix, image)
                )

        @stage(24)
        def _():
            comp.linear_back(
                [(lambda: q[lower, :], 0), (lambda: k[lower, :], 1), (lambda: v[lower, :], 2)],
                store_to(acc, 0, half),
            )

        @stage(25)
        def _():
            gvec[pl.ds(2, 1), :] = comp.row_sum(q[lower, :])
            gvec[pl.ds(3, 1), :] = comp.row_sum(v[lower, :])
            for index, ref in enumerate((q, k, v)):
                comp.weight_grad(
                    lambda part: [n1[lower, chunk(part * BLOCK)]], [lambda: ref[lower, :]], index
                )

        @stage(26)
        def _():
            comp.norm_back(n1, half, rates.at[0], 0, acc, dh, None, text_grad, half, 0, 1)
            give(False, 1, text_grad, text_out)

        def last():
            across(True, 1, cot, cot)
            load(5, e, enc_out, True)
            give(True, 0, decoded, dec_out)
            give(True, 1, text_grad, text_out)
            got(1, image_out)

        return stages, last

    pl.when(section == 0)(lambda: section_program(0, encoder))
    pl.when(section == 1)(lambda: section_program(1, decoder))


def finish_kernel(
    used, encoded, decoded, images, text, enc, dec, enc_v, dec_v, *outs
):
    enc_out, dec_out, image_out, text_out, enc_out_g, dec_out_g, enc_out_v, dec_out_v = outs
    slots = BLOCK

    def cut(ref):
        rows = ref[...].astype(F32)
        parts = [
            rows[image * slots : image * slots + used] for image in range(rows.shape[0] // slots)
        ]
        return jnp.concatenate(parts, axis=0)

    @pl.when(pl.program_id(0) == 0)
    def _():
        enc_out[...] = cut(encoded).astype(BF16)
        image_out[...] = cut(images)
        enc_out_v[...] = in_line(enc_v[...])
        dec_out_v[...] = in_line(dec_v[...])

    dec_out[...] = decoded[...]
    text_out[...] = text[...].astype(F32)
    enc_out_g[...] = enc[...].astype(F32)
    dec_out_g[...] = dec[...].astype(F32)


def vec_tile_of(vecs):
    units = vecs.reshape(-1, VEC_UNIT)
    return jnp.pad(units, ((0, VEC_ROWS - units.shape[0]), (0, 128 - VEC_UNIT)))


def body_fast(
    images, text, enc_mats, enc_vecs, dec_mats, dec_vecs, tissue, text_len, enc_cot, dec_cot
):
    shards = lax.axis_size("dp")
    depth = grid_of(shards)[0]
    img_count, slots = tissue.shape
    words = text.shape[0] // img_count
    sizes = (enc_mats.shape[0], dec_mats.shape[0])
    pers = (enc_vecs.shape[0] // VEC_UNIT, dec_vecs.shape[0] // VEC_UNIT)
    wide = BLOCK
    image_rows, text_rows = img_count * wide, img_count * words
    any_space = pl.BlockSpec(memory_space=pl.ANY)
    vmem_space = pl.BlockSpec(memory_space=pltpu.VMEM)
    smem_space = pl.BlockSpec(memory_space=pltpu.SMEM)
    most = sizes[1]

    def low_buffer(rows=image_rows, columns=D):
        return pltpu.VMEM((rows, columns), BF16)

    def wide_buffer(rows=image_rows):
        return pltpu.VMEM((rows, D), F32)

    dma = pltpu.SemaphoreType.DMA
    made = pl.pallas_call(
        functools.partial(fused_kernel, depth, sizes, pers, wide, words),
        out_shape=(
            jax.ShapeDtypeStruct((image_rows, D), BF16),
            jax.ShapeDtypeStruct((text_rows, D), BF16),
            jax.ShapeDtypeStruct((image_rows, D), BF16),
            jax.ShapeDtypeStruct((text_rows, D), BF16),
            jax.ShapeDtypeStruct((sizes[0], D), BF16),
            jax.ShapeDtypeStruct((sizes[1], D), BF16),
            jax.ShapeDtypeStruct((VEC_ROWS, 128), F32),
            jax.ShapeDtypeStruct((VEC_ROWS, 128), F32),
        ),
        in_specs=[vmem_space] * 3 + [smem_space] + [any_space] * 6,
        out_specs=[any_space] * 8,
        scratch_shapes=[
            low_buffer(shards * most),
            low_buffer(max(Scatter.land_rows(depth, split_rows(rows, LATE)) for rows in sizes)),
            low_buffer(),
            low_buffer(),
            low_buffer(),
            low_buffer(),
            low_buffer(),
            low_buffer(),
            wide_buffer(),
            low_buffer(),
            low_buffer(image_rows, FF),
            low_buffer(image_rows, FF),
            low_buffer(),
            low_buffer(),
            wide_buffer(),
            wide_buffer(),
            low_buffer(),
            low_buffer(),
            pltpu.VMEM((image_rows, 128), F32),
            pltpu.VMEM((3, image_rows, 128), F32),
            pltpu.VMEM((shards, VEC_ROWS, 128), BF16),
            wide_buffer(VEC_ROWS),
            wide_buffer(VEC_ROWS),
            pltpu.VMEM((1 + depth, VEC_ROWS, D), F32),
            pltpu.VMEM((VEC_ROWS, 128), F32),
            pltpu.VMEM((2, 8, D), F32),
            dma((6,)),
            dma((4, shards, 4)),
            dma((4, shards)),
            dma((shards,)),
            dma((shards,)),
            dma((4, 4 * depth + 7)),
            dma((4, 4 * depth + 7)),
            dma((1 + depth,)),
            dma((1 + depth,)),
            dma((2,)),
            dma((2,)),
            dma((7,)),
            dma((7,)),
            dma((7,)),
            pltpu.SemaphoreType.REGULAR,
        ],
        compiler_params=pltpu.CompilerParams(
            collective_id=0, has_side_effects=True, vmem_limit_bytes=VMEM_LIMIT
        ),
        name="blocks_and_grads",
    )(
        images,
        enc_cot,
        tissue,
        text_len,
        text,
        enc_mats,
        dec_mats,
        vec_tile_of(enc_vecs),
        vec_tile_of(dec_vecs),
        dec_cot,
    )

    def tiled(rows):
        return pl.BlockSpec((rows // FINISH_STEPS, D), lambda step: (step, 0))

    def whole(shape):
        return pl.BlockSpec(shape, lambda step: (0, 0))

    image_spec, tile_spec = whole((image_rows, D)), whole((VEC_ROWS, 128))
    out_spec = whole((img_count * slots, D))
    outs = pl.pallas_call(
        functools.partial(finish_kernel, slots),
        grid=(FINISH_STEPS,),
        in_specs=[
            image_spec,
            tiled(text_rows),
            image_spec,
            tiled(text_rows),
            tiled(sizes[0]),
            tiled(sizes[1]),
            tile_spec,
            tile_spec,
        ],
        out_specs=[
            out_spec,
            tiled(text_rows),
            out_spec,
            tiled(text_rows),
            tiled(sizes[0]),
            tiled(sizes[1]),
            whole((8, 128)),
            whole((8, 128)),
        ],
        out_shape=(
            jax.ShapeDtypeStruct((img_count * slots, D), BF16),
            jax.ShapeDtypeStruct((text_rows, D), BF16),
            jax.ShapeDtypeStruct((img_count * slots, D), F32),
            jax.ShapeDtypeStruct((text_rows, D), F32),
            jax.ShapeDtypeStruct((sizes[0], D), F32),
            jax.ShapeDtypeStruct((sizes[1], D), F32),
            jax.ShapeDtypeStruct((8, 128), F32),
            jax.ShapeDtypeStruct((8, 128), F32),
        ),
        name="finish_outputs",
    )(*made)

    def vec_of(tile, per):
        return tile.reshape(-1)[: per * VEC_UNIT]

    return (
        outs[0],
        outs[1],
        outs[2],
        outs[3],
        outs[4],
        vec_of(outs[6], pers[0]),
        outs[5],
        vec_of(outs[7], pers[1]),
    )


FINISH_STEPS = 4
VMEM_LIMIT = 63 * 2**20
LATE = 0.21
GATHER_PLANS = (
    (
        120, 110, 400, 100, 130, 500, 121, 131, 8, 101, 111, 200, 231, 620, 630, 230, 102, 1500,
        221, 112, 201, 600, 631, 621, 601, 0, 103, 122, 211, 202, 132, 203, 610, 602, 603, 300,
        212, 220, 210, 611, 133, 1, 222, 2, 233, 632, 622, 612, 232, 310, 3, 4, 320, 5, 633, 330,
    ),
    (
        400, 500, 110, 130, 630, 100, 120, 101, 121, 102, 201, 1500, 29, 131, 111, 210, 600, 202,
        103, 601, 132, 112, 203, 631, 212, 610, 632, 620, 621, 200, 602, 0, 122, 222, 133, 603,
        211, 300, 221, 1, 2, 611, 232, 230, 3, 231, 612, 310, 233, 220, 4, 5, 633, 6, 7, 622, 320,
        8, 330, 10, 12,
    ),
)
SCATTER_PLANS = (
    (
        6, 7, 10, 11, 13, 14, 12, 1221, 730, 15, 16, 1231, 17, 1211, 18, 720, 19, 20, 1212, 830,
        1232, 21, 700, 1201, 1202, 930, 1310, 1031, 1233, 800, 1222, 820, 22, 30, 710, 1203, 900,
        1001, 920, 1021, 1002, 31, 1032, 810, 1300, 32, 1033, 1320, 1022, 910, 1410, 1011, 1330,
        1430, 1400, 33, 1012, 1003, 1110, 1420, 1130, 1100, 1120,
    ),
    (
        9, 11, 1231, 730, 14, 15, 16, 830, 13, 720, 1221, 18, 19, 17, 710, 1211, 930, 1031, 820,
        20, 21, 22, 23, 24, 1212, 25, 810, 700, 920, 1201, 1202, 26, 1222, 1021, 1232, 910, 1310,
        1011, 30, 1233, 1032, 800, 1022, 31, 1320, 32, 1012, 1420, 900, 1203, 1033, 1001, 1410,
        1130, 1002, 33, 1300, 1110, 1330, 1120, 1003, 1400, 1100, 1430,
    ),
)


def body(images, text, enc_mats, enc_vecs, dec_mats, dec_vecs, tissue, text_len, enc_cot, dec_cot):
    shards = lax.axis_size("dp")
    img_count, slots = tissue.shape
    words = text.shape[0] // img_count
    fits = (
        shards == 16
        and img_count == 2
        and slots <= BLOCK == 256
        and img_count * words == BLOCK
        and enc_mats.shape[0] % LINES == 0
        and dec_mats.shape[0] % LINES == 0
        and enc_vecs.shape[0] % VEC_UNIT == 0
        and dec_vecs.shape[0] % VEC_UNIT == 0
    )
    run = body_fast if fits else body_plain
    return run(
        images, text, enc_mats, enc_vecs, dec_mats, dec_vecs, tissue, text_len, enc_cot, dec_cot
    )


def solution(mesh):
    placed = (
        P("dp", None),
        P("dp", None),
        P("dp", None),
        P("dp"),
        P("dp", None),
        P("dp"),
        P("dp", None),
        P("dp"),
        P("dp", None),
        P("dp", None),
    )
    return jax.shard_map(
        body,
        mesh=mesh,
        in_specs=placed,
        out_specs=(
            P("dp", None),
            P("dp", None),
            P("dp", None),
            P("dp", None),
            P("dp", None),
            P("dp"),
            P("dp", None),
            P("dp"),
        ),
        check_vma=False,
    )
```

```python
import functools

import jax
import jax.numpy as jnp
from jax import lax
from jax.experimental import pallas as pl
from jax.experimental.pallas import tpu as pltpu
from jax.sharding import PartitionSpec as P

D = 768
HEAD = 64
FF = 3072
MICRO = 2


def shifted(block, axis, distance):
    devices = range(lax.axis_size(axis))
    route = [(i - distance, i) for i in devices if i - distance in devices]
    return lax.ppermute(block, axis, route)


def layer_norm(inputs, scale_vec, shift_vec):
    centre = inputs - jnp.mean(inputs, axis=-1, keepdims=True)
    spread = jnp.mean(centre * centre, axis=-1, keepdims=True)
    return centre * lax.rsqrt(spread + 1e-06) * scale_vec + shift_vec


def norm_back(inputs, scale_vec, shift_vec, grads):
    _, pullback = jax.vjp(layer_norm, inputs, scale_vec, shift_vec)
    return pullback(grads)


def gelu_back(inner, grads):
    _, pullback = jax.vjp(jax.nn.gelu, inner)
    return pullback(grads)[0]


def part_of(vecs, index):
    return vecs[index * D : (index + 1) * D].astype(jnp.float32)


def split_heads(rows):
    return rows.reshape(rows.shape[0], rows.shape[1], -1, HEAD)


def project(rows, weight):
    return jnp.einsum("bsd,de->bse", rows, weight, preferred_element_type=jnp.float32)


def row_sum(values):
    return jnp.sum(values.astype(jnp.float32), axis=(0, 1))


def attn_scores(queries, key_rows, allowed):
    scores = (
        jnp.einsum(
            "bqhe,bkhe->bhqk",
            split_heads(queries),
            split_heads(key_rows),
            preferred_element_type=jnp.float32,
        )
        * 0.125
    )
    return jnp.where(allowed, scores, -1000000000.0)


def attn_forward(queries, key_rows, value_rows, allowed):
    scores = attn_scores(queries, key_rows, allowed)
    peak = jnp.max(scores, axis=-1, keepdims=True)
    expd = jnp.exp(scores - peak)
    total = jnp.sum(expd, axis=-1, keepdims=True)
    probs = (expd / total).astype(jnp.bfloat16)
    mixed = jnp.einsum(
        "bhqk,bkhe->bqhe", probs, split_heads(value_rows), preferred_element_type=jnp.float32
    )
    return (mixed.reshape(queries.shape).astype(jnp.bfloat16), peak + jnp.log(total))


def attn_backward(queries, key_rows, value_rows, allowed, log_total, grad_mixed):
    scores = attn_scores(queries, key_rows, allowed)
    probs = jnp.exp(scores - log_total)
    grad_heads = split_heads(grad_mixed)
    grad_probs = jnp.einsum(
        "bqhe,bkhe->bhqk", grad_heads, split_heads(value_rows), preferred_element_type=jnp.float32
    )
    grad_scores = probs * (grad_probs - jnp.sum(grad_probs * probs, axis=-1, keepdims=True))
    grad_low = grad_scores.astype(jnp.bfloat16)
    grad_q = (
        jnp.einsum(
            "bhqk,bkhe->bqhe", grad_low, split_heads(key_rows), preferred_element_type=jnp.float32
        )
        * 0.125
    )
    grad_k = (
        jnp.einsum(
            "bhqk,bqhe->bkhe", grad_low, split_heads(queries), preferred_element_type=jnp.float32
        )
        * 0.125
    )
    grad_v = jnp.einsum(
        "bhqk,bqhe->bkhe",
        probs.astype(jnp.bfloat16),
        grad_heads,
        preferred_element_type=jnp.float32,
    )
    return (
        grad_q.reshape(queries.shape),
        grad_k.reshape(key_rows.shape),
        grad_v.reshape(value_rows.shape),
    )


def self_block(inputs, allowed, mats, vecs):
    wqkv = mats[0 : 3 * D].reshape(3, D, D)
    normed = layer_norm(inputs, part_of(vecs, 0), part_of(vecs, 1)).astype(jnp.bfloat16)
    qkv = jnp.einsum("bsd,kde->kbse", normed, wqkv, preferred_element_type=jnp.float32)
    queries = (qkv[0] + part_of(vecs, 2)).astype(jnp.bfloat16)
    key_rows = qkv[1].astype(jnp.bfloat16)
    value_rows = (qkv[2] + part_of(vecs, 3)).astype(jnp.bfloat16)
    mixed, log_total = attn_forward(queries, key_rows, value_rows, allowed)
    after = inputs + project(mixed, mats[3 * D : 4 * D]) + part_of(vecs, 4)
    return (after, (normed, queries, key_rows, value_rows, mixed, log_total))


def self_block_back(inputs, allowed, mats, vecs, saved, grad_after):
    normed, queries, key_rows, value_rows, mixed, log_total = saved
    wqkv = mats[0 : 3 * D].reshape(3, D, D)
    grad_low = grad_after.astype(jnp.bfloat16)
    grad_wout = jnp.einsum("bsd,bse->de", mixed, grad_low, preferred_element_type=jnp.float32)
    grad_mixed = jnp.einsum(
        "bse,de->bsd", grad_low, mats[3 * D : 4 * D], preferred_element_type=jnp.float32
    ).astype(jnp.bfloat16)
    grad_q, grad_k, grad_v = attn_backward(
        queries, key_rows, value_rows, allowed, log_total, grad_mixed
    )
    grad_qkv = jnp.stack([grad_q, grad_k, grad_v]).astype(jnp.bfloat16)
    grad_wqkv = jnp.einsum(
        "bsd,kbse->kde", normed, grad_qkv, preferred_element_type=jnp.float32
    ).reshape(3 * D, D)
    grad_normed = jnp.einsum("kbse,kde->bsd", grad_qkv, wqkv, preferred_element_type=jnp.float32)
    grad_in, grad_gain, grad_shift = norm_back(
        inputs, part_of(vecs, 0), part_of(vecs, 1), grad_normed
    )
    vec_grads = [
        grad_gain,
        grad_shift,
        row_sum(grad_qkv[0]),
        row_sum(grad_qkv[2]),
        row_sum(grad_low),
    ]
    return (grad_after + grad_in, [grad_wqkv, grad_wout], vec_grads)


def cross_block(inputs, image_rows, allowed, mats, vecs):
    normed = layer_norm(inputs, part_of(vecs, 5), part_of(vecs, 6)).astype(jnp.bfloat16)
    queries = (project(normed, mats[4 * D : 5 * D]) + part_of(vecs, 7)).astype(jnp.bfloat16)
    pair = jnp.einsum(
        "bsd,kde->kbse",
        image_rows,
        mats[5 * D : 7 * D].reshape(2, D, D),
        preferred_element_type=jnp.float32,
    )
    key_rows = pair[0].astype(jnp.bfloat16)
    value_rows = (pair[1] + part_of(vecs, 8)).astype(jnp.bfloat16)
    mixed, log_total = attn_forward(queries, key_rows, value_rows, allowed)
    after = inputs + project(mixed, mats[7 * D : 8 * D]) + part_of(vecs, 9)
    return (after, (normed, queries, key_rows, value_rows, mixed, log_total))


def cross_block_back(inputs, image_rows, allowed, mats, vecs, saved, grad_after):
    normed, queries, key_rows, value_rows, mixed, log_total = saved
    grad_low = grad_after.astype(jnp.bfloat16)
    grad_wout = jnp.einsum("bsd,bse->de", mixed, grad_low, preferred_element_type=jnp.float32)
    grad_mixed = jnp.einsum(
        "bse,de->bsd", grad_low, mats[7 * D : 8 * D], preferred_element_type=jnp.float32
    ).astype(jnp.bfloat16)
    grad_q, grad_k, grad_v = attn_backward(
        queries, key_rows, value_rows, allowed, log_total, grad_mixed
    )
    grad_query = grad_q.astype(jnp.bfloat16)
    grad_pair = jnp.stack([grad_k, grad_v]).astype(jnp.bfloat16)
    pair_weight = mats[5 * D : 7 * D].reshape(2, D, D)
    grad_wq = jnp.einsum("bsd,bse->de", normed, grad_query, preferred_element_type=jnp.float32)
    grad_wpair = jnp.einsum(
        "bsd,kbse->kde", image_rows, grad_pair, preferred_element_type=jnp.float32
    ).reshape(2 * D, D)
    grad_image = jnp.einsum(
        "kbse,kde->bsd", grad_pair, pair_weight, preferred_element_type=jnp.float32
    )
    grad_normed = jnp.einsum(
        "bse,de->bsd", grad_query, mats[4 * D : 5 * D], preferred_element_type=jnp.float32
    )
    grad_in, grad_gain, grad_shift = norm_back(
        inputs, part_of(vecs, 5), part_of(vecs, 6), grad_normed
    )
    vec_grads = [
        grad_gain,
        grad_shift,
        row_sum(grad_query),
        row_sum(grad_pair[1]),
        row_sum(grad_low),
    ]
    return (grad_after + grad_in, grad_image, [grad_wq, grad_wpair, grad_wout], vec_grads)


def mlp_block(inputs, w_in_t, w_out, norm_gain, norm_shift, bias_in, bias_out):
    normed = layer_norm(inputs, norm_gain, norm_shift).astype(jnp.bfloat16)
    inner = jnp.einsum("bsd,fd->bsf", normed, w_in_t, preferred_element_type=jnp.float32) + bias_in
    hidden = jax.nn.gelu(inner).astype(jnp.bfloat16)
    result = (
        inputs
        + jnp.einsum("bsf,fd->bsd", hidden, w_out, preferred_element_type=jnp.float32)
        + bias_out
    )
    return (result, (normed, inner, hidden))


def mlp_block_back(inputs, w_in_t, w_out, norm_gain, norm_shift, saved, grad_result):
    normed, inner, hidden = saved
    grad_low = grad_result.astype(jnp.bfloat16)
    grad_w_out = jnp.einsum("bsf,bsd->fd", hidden, grad_low, preferred_element_type=jnp.float32)
    grad_hidden = jnp.einsum("bsd,fd->bsf", grad_low, w_out, preferred_element_type=jnp.float32)
    grad_inner = gelu_back(inner, grad_hidden).astype(jnp.bfloat16)
    grad_w_in = jnp.einsum("bsf,bsd->fd", grad_inner, normed, preferred_element_type=jnp.float32)
    grad_normed = jnp.einsum("bsf,fd->bsd", grad_inner, w_in_t, preferred_element_type=jnp.float32)
    grad_in, grad_gain, grad_shift = norm_back(inputs, norm_gain, norm_shift, grad_normed)
    return (
        grad_result + grad_in,
        [grad_w_in, grad_w_out],
        [grad_gain, grad_shift, row_sum(grad_low), row_sum(grad_inner)],
    )


def encode(image_mb, keep, mats, vecs):
    inputs = image_mb.astype(jnp.float32)
    allowed = (keep > 0.5)[:, None, None, :]
    middle, saved_self = self_block(inputs, allowed, mats, vecs)
    result, saved_mlp = mlp_block(
        middle,
        mats[4 * D : 4 * D + FF],
        mats[4 * D + FF :],
        part_of(vecs, 5),
        part_of(vecs, 6),
        vecs[8 * D : 8 * D + FF].astype(jnp.float32),
        part_of(vecs, 7),
    )
    output = (result * keep[..., None]).astype(jnp.bfloat16)
    return (output, (inputs, allowed, middle, saved_self, saved_mlp))


def encode_back(saved, keep, mats, vecs, grad_out):
    inputs, allowed, middle, saved_self, saved_mlp = saved
    grad_result = grad_out.astype(jnp.float32) * keep[..., None]
    grad_middle, mats_mlp, vecs_mlp = mlp_block_back(
        middle,
        mats[4 * D : 4 * D + FF],
        mats[4 * D + FF :],
        part_of(vecs, 5),
        part_of(vecs, 6),
        saved_mlp,
        grad_result,
    )
    grad_inputs, mats_self, vecs_self = self_block_back(
        inputs, allowed, mats, vecs, saved_self, grad_middle
    )
    return (grad_inputs, mats_self + mats_mlp, vecs_self + vecs_mlp)


def decode(text_mb, image_rows, keep, length, mats, vecs):
    inputs = text_mb.astype(jnp.float32)
    positions = jnp.arange(inputs.shape[1])
    causal = (positions[None, :] <= positions[:, None])[None, None] & (
        positions[None, None, None, :] < length[:, None, None, None]
    )
    crossing = (keep > 0.5)[:, None, None, :]
    after_self, saved_self = self_block(inputs, causal, mats, vecs)
    after_cross, saved_cross = cross_block(after_self, image_rows, crossing, mats, vecs)
    result, saved_mlp = mlp_block(
        after_cross,
        mats[8 * D : 8 * D + FF],
        mats[8 * D + FF :],
        part_of(vecs, 10),
        part_of(vecs, 11),
        vecs[13 * D : 13 * D + FF].astype(jnp.float32),
        part_of(vecs, 12),
    )
    return (
        result.astype(jnp.bfloat16),
        (
            inputs,
            image_rows,
            causal,
            crossing,
            after_self,
            after_cross,
            saved_self,
            saved_cross,
            saved_mlp,
        ),
    )


def decode_back(saved, mats, vecs, grad_out):
    (
        inputs,
        image_rows,
        causal,
        crossing,
        after_self,
        after_cross,
        saved_self,
        saved_cross,
        saved_mlp,
    ) = saved
    grad_result = grad_out.astype(jnp.float32)
    grad_cross, mats_mlp, vecs_mlp = mlp_block_back(
        after_cross,
        mats[8 * D : 8 * D + FF],
        mats[8 * D + FF :],
        part_of(vecs, 10),
        part_of(vecs, 11),
        saved_mlp,
        grad_result,
    )
    grad_self, grad_image, mats_cross, vecs_cross = cross_block_back(
        after_self, image_rows, crossing, mats, vecs, saved_cross, grad_cross
    )
    grad_inputs, mats_self, vecs_self = self_block_back(
        inputs, causal, mats, vecs, saved_self, grad_self
    )
    return (
        grad_inputs,
        grad_image,
        mats_self + mats_cross + mats_mlp,
        vecs_self + vecs_cross + vecs_mlp,
    )


def body_plain(images, text, enc_mats, enc_vecs, dec_mats, dec_vecs, tissue, text_len, enc_cot, dec_cot):
    first = lax.axis_index("section") == 0
    shards = lax.axis_size("dp")
    img_count, slots = tissue.shape
    batch = img_count // MICRO
    text_rows = text.shape[0] // img_count
    enc_rows, dec_rows = (enc_mats.shape[0], dec_mats.shape[0])
    enc_len, dec_len = (enc_vecs.shape[0], dec_vecs.shape[0])
    keep_all = tissue.astype(jnp.float32).reshape(MICRO, batch, slots)
    image_in = images.reshape(MICRO, batch, slots, D)
    text_in = text.reshape(MICRO, batch, text_rows, D)
    length_in = text_len.reshape(MICRO, batch)
    image_cot = enc_cot.reshape(MICRO, batch, slots, D)
    text_cot = dec_cot.reshape(MICRO, batch, text_rows, D)

    def enc_view(weights):
        mats_part = (
            weights[0].reshape(shards, dec_rows, D)[:, :enc_rows].reshape(shards * enc_rows, D)
        )
        vecs_part = weights[1].reshape(shards, dec_len)[:, :enc_len].reshape(shards * enc_len)
        return (mats_part, vecs_part)

    def dec_view(weights):
        return (weights[0], weights[1])

    def to_padded(grad_mats, grad_vecs):
        mats_part = jnp.pad(
            grad_mats.reshape(shards, enc_rows, D), ((0, 0), (0, dec_rows - enc_rows), (0, 0))
        )
        vecs_part = jnp.pad(grad_vecs.reshape(shards, enc_len), ((0, 0), (0, dec_len - enc_len)))
        return (mats_part.reshape(shards * dec_rows, D), vecs_part.reshape(shards * dec_len))

    mats_pad = jnp.pad(enc_mats, ((0, dec_rows - enc_rows), (0, 0)))
    vecs_pad = jnp.pad(enc_vecs, (0, dec_len - enc_len))
    own_mats = jnp.where(first, mats_pad, dec_mats)
    own_vecs = jnp.where(first, vecs_pad, dec_vecs)
    weights = (
        lax.all_gather(own_mats, "dp", axis=0, tiled=True),
        lax.all_gather(own_vecs, "dp", axis=0, tiled=True),
    )
    zero_image = jnp.zeros((batch, slots, D), jnp.bfloat16)
    zero_text = jnp.zeros((batch, text_rows, D), jnp.bfloat16)
    encoded = [zero_image] * MICRO
    decoded = [zero_text] * MICRO
    for tick in range(MICRO + 1):

        def forward_encoder_work():
            if tick < MICRO:
                mats_part, vecs_part = enc_view(weights)
                return (encode(image_in[tick], keep_all[tick], mats_part, vecs_part)[0], zero_text)
            return (zero_image, zero_text)

        def forward_decoder_work():
            if tick > 0:
                mats_part, vecs_part = dec_view(weights)
                made = decode(
                    text_in[tick - 1],
                    encoded[tick - 1],
                    keep_all[tick - 1],
                    length_in[tick - 1],
                    mats_part,
                    vecs_part,
                )[0]
                return (zero_image, made)
            return (zero_image, zero_text)

        made_image, made_text = lax.cond(first, forward_encoder_work, forward_decoder_work)
        if tick < MICRO:
            arrived = shifted(made_image, "section", 1)
            encoded[tick] = jnp.where(first, made_image, arrived)
        if tick > 0:
            decoded[tick - 1] = made_text
    back_weights = weights
    zero_image_grad = jnp.zeros((batch, slots, D), jnp.float32)
    zero_text_grad = jnp.zeros((batch, text_rows, D), jnp.float32)
    zero_mats = jnp.zeros((shards * dec_rows, D), jnp.float32)
    zero_vecs = jnp.zeros((shards * dec_len,), jnp.float32)
    returned = [zero_image] * MICRO
    image_grads = [zero_image_grad] * MICRO
    text_grads = [zero_text_grad] * MICRO
    total_mats, total_vecs = (zero_mats, zero_vecs)
    for tick in range(MICRO + 1):

        def backward_encoder_work():
            if tick > 0:
                index = MICRO - tick
                mats_part, vecs_part = enc_view(back_weights)
                _, saved = encode(image_in[index], keep_all[index], mats_part, vecs_part)
                grad_in, grad_mats, grad_vecs = encode_back(
                    saved, keep_all[index], mats_part, vecs_part, returned[index]
                )
                grad_mats, grad_vecs = to_padded(
                    jnp.concatenate(grad_mats, axis=0), jnp.concatenate(grad_vecs, axis=0)
                )
                return (zero_image, zero_text_grad, grad_in, grad_mats, grad_vecs)
            return (zero_image, zero_text_grad, zero_image_grad, zero_mats, zero_vecs)

        def backward_decoder_work():
            if tick < MICRO:
                index = MICRO - 1 - tick
                mats_part, vecs_part = dec_view(back_weights)
                _, saved = decode(
                    text_in[index],
                    encoded[index],
                    keep_all[index],
                    length_in[index],
                    mats_part,
                    vecs_part,
                )
                grad_text, grad_image, grad_mats, grad_vecs = decode_back(
                    saved, mats_part, vecs_part, text_cot[index]
                )
                grad_mats = jnp.concatenate(grad_mats, axis=0)
                grad_vecs = jnp.concatenate(grad_vecs, axis=0)
                outgoing = (grad_image + image_cot[index].astype(jnp.float32)).astype(jnp.bfloat16)
                return (outgoing, grad_text, zero_image_grad, grad_mats, grad_vecs)
            return (zero_image, zero_text_grad, zero_image_grad, zero_mats, zero_vecs)

        outgoing, grad_text, grad_in, grad_mats, grad_vecs = lax.cond(
            first, backward_encoder_work, backward_decoder_work
        )
        if tick == 0:
            total_mats, total_vecs = (grad_mats, grad_vecs)
        else:
            total_mats = total_mats + grad_mats
            total_vecs = total_vecs + grad_vecs
        if tick < MICRO:
            returned[MICRO - 1 - tick] = shifted(outgoing, "section", -1)
            text_grads[MICRO - 1 - tick] = grad_text
        if tick > 0:
            image_grads[MICRO - tick] = grad_in
    shard_mats, shard_vecs = (
        lax.psum_scatter(total_mats, "dp", scatter_dimension=0, tiled=True),
        lax.psum_scatter(total_vecs, "dp", scatter_dimension=0, tiled=True),
    )
    image_grad_all = jnp.concatenate(image_grads, axis=0).reshape(-1, D)
    text_grad_all = jnp.concatenate(text_grads, axis=0).reshape(-1, D)
    decoded_all = jnp.concatenate(decoded, axis=0).reshape(-1, D).astype(jnp.float32)
    enc_mats_own = jnp.where(first, shard_mats[:enc_rows], 0.0)
    enc_vecs_own = jnp.where(first, shard_vecs[:enc_len], 0.0)
    dec_mats_own = jnp.where(first, 0.0, shard_mats)
    dec_vecs_own = jnp.where(first, 0.0, shard_vecs)
    image_own = jnp.where(first, image_grad_all, 0.0)
    decoded_own = jnp.where(first, 0.0, decoded_all)
    text_own = jnp.where(first, 0.0, text_grad_all)
    combined = (
        lax.psum(enc_mats_own.astype(jnp.bfloat16), "section").astype(jnp.float32),
        lax.psum(enc_vecs_own.astype(jnp.bfloat16), "section").astype(jnp.float32),
        lax.psum(dec_mats_own.astype(jnp.bfloat16), "section").astype(jnp.float32),
        lax.psum(dec_vecs_own.astype(jnp.bfloat16), "section").astype(jnp.float32),
        lax.psum(image_own.astype(jnp.bfloat16), "section").astype(jnp.float32),
        lax.psum(decoded_own.astype(jnp.bfloat16), "section").astype(jnp.float32),
        lax.psum(text_own.astype(jnp.bfloat16), "section").astype(jnp.float32),
    )
    enc_mats_grad, enc_vecs_grad, dec_mats_grad, dec_vecs_grad, image_grad, dec_full, text_grad = (
        combined
    )
    dec_out = dec_full.astype(jnp.bfloat16)
    enc_out = jnp.concatenate(encoded, axis=0).reshape(-1, D)
    return (
        enc_out,
        dec_out,
        image_grad,
        text_grad,
        enc_mats_grad,
        enc_vecs_grad,
        dec_mats_grad,
        dec_vecs_grad,
    )


MESH = pl.DeviceIdType.MESH
TILE = 16
ADD_ROWS = 32


def grid_of(shards):
    return (shards // 4, 2, 2)


def split_rows(rows, late):
    part = int(rows * late / 2) // TILE * TILE
    first = (rows - 2 * part) // 2 // TILE * TILE
    sizes = (first, rows - 2 * part - first, part, part)
    starts = (0, first, rows - 2 * part, rows - part)
    return tuple(zip(starts, sizes))


class Place:
    def __init__(self, depth):
        self.section = lax.axis_index("section")
        self.me = lax.axis_index("dp")
        self.depth = depth
        self.z = lax.div(self.me, 4)
        self.y = lax.rem(lax.div(self.me, 2), 2)
        self.x = lax.rem(self.me, 2)

    def shard(self, z, y, x):
        return (z * 2 + y) * 2 + x

    def pair(self, first_x, z, first, second):
        return self.shard(z, second, first) if first_x else self.shard(z, first, second)

    def own(self, first_x):
        return (self.x, self.y) if first_x else (self.y, self.x)


class Copies:
    def __init__(self, place, waiting=False):
        self.place = place
        self.waiting = waiting

    def start(self, cond, src, dst, send_sem, recv_sem, dp, section=None):
        section = self.place.section if section is None else section

        def act():
            copy = pltpu.make_async_remote_copy(
                src_ref=src,
                dst_ref=dst,
                send_sem=send_sem,
                recv_sem=recv_sem,
                device_id=(section, dp),
                device_id_type=MESH,
            )
            if self.waiting:
                copy.wait_send()
            else:
                copy.start()

        if cond is None:
            act()
        else:
            pl.when(cond)(act)

    def arrived(self, dst, send_sem, recv_sem):
        if self.waiting:
            return
        pltpu.make_async_remote_copy(
            src_ref=dst,
            dst_ref=dst,
            send_sem=send_sem,
            recv_sem=recv_sem,
            device_id=(self.place.section, self.place.me),
            device_id_type=MESH,
        ).wait_recv()


def guarded(cond, step, *args):
    if cond is None:
        step(*args)
    else:
        pl.when(cond)(functools.partial(step, *args))


def greet(place, shards, both):
    barrier = pltpu.get_barrier_semaphore()
    for step in range(1, shards):
        pl.semaphore_signal(
            barrier,
            inc=1,
            device_id=(place.section, lax.rem(place.me + step, shards)),
            device_id_type=MESH,
        )
    if both:
        pl.semaphore_signal(
            barrier, inc=1, device_id=(1 - place.section, place.me), device_id_type=MESH
        )
    pl.semaphore_wait(barrier, shards - 1 + int(both))


class Gather:
    def __init__(self, copies, place, depth, rows, cuts, w, send_sems, recv_sems, gate):
        self.copies = copies
        self.gate = gate
        self.place = place
        self.depth = depth
        self.rows = rows
        self.cuts = cuts
        self.w = w
        self.send_sems = send_sems
        self.recv_sems = recv_sems
        self.late = (2, 3) if cuts[2][1] else ()

    def piece(self, cls, shard):
        start, size = self.cuts[cls]
        return self.w.at[pl.ds(pl.multiple_of(shard * self.rows + start, TILE), size)]

    def send(self, cls, shard, way, dp):
        piece = self.piece(cls, shard)
        self.copies.start(
            None, piece, piece, self.send_sems.at[cls, shard, way], self.recv_sems.at[cls, shard], dp
        )

    def arrived(self, cls, shard):
        self.copies.arrived(
            self.piece(cls, shard), self.send_sems.at[cls, shard, 0], self.recv_sems.at[cls, shard]
        )

    def along(self, plane, distance, act):
        z, last = self.place.z, self.depth - 1
        if distance == 0:
            pl.when(z == plane)(lambda: act(plane, plane < last, plane > 0))
            return
        if plane + distance <= last:
            pl.when(z == plane + distance)(
                lambda: act(plane + distance, plane + distance < last, False)
            )
        if plane - distance >= 0:
            pl.when(z == plane - distance)(
                lambda: act(plane - distance, False, plane - distance > 0)
            )

    def L(self, plane, distance):
        place = self.place

        def act(at, up, down):
            shard = place.shard(plane, place.y, place.x)
            for cls in (0, 1):
                a, b = place.own(cls == 0)
                if distance:
                    self.arrived(cls, shard)
                if up:
                    self.send(cls, shard, 0, place.me + 4)
                if down:
                    self.send(cls, shard, 1, place.me - 4)
                self.send(cls, shard, 2, place.pair(cls == 0, at, 1 - a, b))

        self.along(plane, distance, act)

    def G(self, plane, distance):
        place = self.place

        def act(at, up, down):
            for cls in (0, 1):
                a, b = place.own(cls == 0)
                other = place.pair(cls == 0, plane, 1 - a, b)
                self.arrived(cls, other)
                to = place.pair(cls == 0, at, a, 1 - b)
                self.send(cls, place.shard(plane, place.y, place.x), 3, to)
                self.send(cls, other, 3, to)

        self.along(plane, distance, act)

    def H(self, plane):
        place = self.place
        for cls in (0, 1):
            a, b = place.own(cls == 0)
            self.arrived(cls, place.pair(cls == 0, plane, a, 1 - b))
            self.arrived(cls, place.pair(cls == 0, plane, 1 - a, 1 - b))

    def X(self):
        if not self.copies.waiting:
            self.gate()

    def M(self):
        place = self.place
        for cls in self.late:
            a, b = place.own(cls == 2)
            self.send(cls, place.me, 2, place.pair(cls == 2, place.z, 1 - a, b))

    def N(self):
        place = self.place
        for cls in self.late:
            a, b = place.own(cls == 2)
            other = place.pair(cls == 2, place.z, 1 - a, b)
            self.arrived(cls, other)
            to = place.pair(cls == 2, place.z, a, 1 - b)
            self.send(cls, place.me, 3, to)
            self.send(cls, other, 3, to)

    def T(self, plane, distance):
        place = self.place

        def act(at, up, down):
            for cls in self.late:
                a, b = place.own(cls == 2)
                if distance == 0:
                    self.arrived(cls, place.pair(cls == 2, plane, a, 1 - b))
                    self.arrived(cls, place.pair(cls == 2, plane, 1 - a, 1 - b))
                for index in range(4):
                    shard = plane * 4 + index
                    if distance:
                        self.arrived(cls, shard)
                    if up:
                        self.send(cls, shard, 0, place.me + 4)
                    if down:
                        self.send(cls, shard, 1, place.me - 4)

        self.along(plane, distance, act)


def add_rows(total, total_start, part, part_start, size):
    step = next(n for n in (64, 48, 32, TILE) if size % n == 0)

    @pl.loop(0, size // step)
    def _(index):
        at = pl.ds(pl.multiple_of(total_start + index * step, TILE), step)
        of = pl.ds(pl.multiple_of(part_start + index * step, TILE), step)
        total[at] = total[at] + part[of]


class Scatter:
    def __init__(self, copies, place, depth, rows, cuts, g, land, send_sems, recv_sems, done):
        self.copies = copies
        self.done = done
        self.place = place
        self.depth = depth
        self.rows = rows
        self.cuts = cuts
        self.g = g
        self.land = land
        self.send_sems = send_sems
        self.recv_sems = recv_sems
        self.late = (2, 3) if cuts[2][1] else ()
        self.early_slots = 4 * depth + 1
        self.late_slots = 4 * depth + 7

    @staticmethod
    def land_rows(depth, cuts):
        early = (4 * depth + 1) * (cuts[0][1] + cuts[1][1])
        return early + (4 * depth + 7) * (cuts[2][1] + cuts[3][1])

    def start_of(self, cls, shard):
        return pl.multiple_of(shard * self.rows + self.cuts[cls][0], TILE)

    def slot_start(self, cls, slot):
        base = 0
        for other in range(cls):
            base += (self.early_slots if other < 2 else self.late_slots) * self.cuts[other][1]
        return base + slot * self.cuts[cls][1]

    def slot_ref(self, cls, slot):
        return self.land.at[pl.ds(self.slot_start(cls, slot), self.cuts[cls][1])]

    def send(self, cls, shard, slot, dp):
        self.copies.start(
            None,
            self.g.at[pl.ds(self.start_of(cls, shard), self.cuts[cls][1])],
            self.slot_ref(cls, slot),
            self.send_sems.at[cls, slot],
            self.recv_sems.at[cls, slot],
            dp,
        )

    def take(self, cls, shard, slot):
        if self.copies.waiting:
            return
        self.copies.arrived(
            self.slot_ref(cls, slot), self.send_sems.at[cls, slot], self.recv_sems.at[cls, slot]
        )
        add_rows(
            self.g,
            self.start_of(cls, shard),
            self.land,
            self.slot_start(cls, slot),
            self.cuts[cls][1],
        )

    def A(self, plane):
        place = self.place
        for cls in (0, 1):
            first_x = cls == 0
            a, b = place.own(first_x)
            to = place.pair(first_x, place.z, 1 - a, b)
            self.send(cls, place.pair(first_x, plane, 1 - a, 1 - b), plane * 3, to)
            self.send(cls, place.pair(first_x, plane, 1 - a, b), plane * 3 + 1, to)

    def B(self, plane):
        place = self.place
        for cls in (0, 1):
            first_x = cls == 0
            a, b = place.own(first_x)
            away = place.pair(first_x, plane, a, 1 - b)
            self.take(cls, away, plane * 3)
            self.send(cls, away, plane * 3 + 2, place.pair(first_x, place.z, a, 1 - b))
        for cls in (0, 1):
            first_x = cls == 0
            a, b = place.own(first_x)
            self.take(cls, place.pair(first_x, plane, a, b), plane * 3 + 1)

    def P(self, plane):
        place = self.place
        for cls in (0, 1):
            self.take(cls, place.shard(plane, place.y, place.x), plane * 3 + 2)

    def hop(self, plane, number, act):
        z = self.place.z
        low, high = number - 1, self.depth - number
        if low < plane:
            pl.when(z == low)(lambda: act(1, low + 1 == plane))
        if high > plane:
            pl.when(z == high)(lambda: act(-1, high - 1 == plane))

    def Z(self, plane, number):
        place = self.place
        slot = 3 * self.depth + plane

        def act(way, ends):
            shard = place.shard(plane, place.y, place.x)
            for cls in (0, 1):
                if number > 1:
                    self.take(cls, shard, slot)
                to = 4 * self.depth if ends and way < 0 else slot
                self.send(cls, shard, to, place.me + 4 * way)

        self.hop(plane, number, act)

    def E(self, plane):
        place = self.place

        @pl.when(place.z == plane)
        def _():
            shard = place.shard(plane, place.y, place.x)
            for cls in (0, 1):
                if plane > 0:
                    self.take(cls, shard, 3 * self.depth + plane)
                if plane < self.depth - 1:
                    self.take(cls, shard, 4 * self.depth)
                if not self.copies.waiting:
                    self.done(cls)

    def Q(self, plane, number):
        place = self.place

        def act(way, ends):
            for cls in self.late:
                for index in range(4):
                    slot = plane * 4 + index
                    if number > 1:
                        self.take(cls, slot, slot)
                    to = 4 * self.depth + index if ends and way < 0 else slot
                    self.send(cls, slot, to, place.me + 4 * way)

        self.hop(plane, number, act)

    def R(self, plane):
        place = self.place
        base = 4 * self.depth + 4

        @pl.when(place.z == plane)
        def _():
            for cls in self.late:
                for index in range(4):
                    slot = plane * 4 + index
                    if plane > 0:
                        self.take(cls, slot, slot)
                    if plane < self.depth - 1:
                        self.take(cls, slot, 4 * self.depth + index)
                first_x = cls == 2
                a, b = place.own(first_x)
                to = place.pair(first_x, plane, 1 - a, b)
                self.send(cls, place.pair(first_x, plane, 1 - a, 1 - b), base, to)
                self.send(cls, place.pair(first_x, plane, 1 - a, b), base + 1, to)

    def S(self, plane):
        place = self.place
        base = 4 * self.depth + 4

        @pl.when(place.z == plane)
        def _():
            for cls in self.late:
                first_x = cls == 2
                a, b = place.own(first_x)
                away = place.pair(first_x, plane, a, 1 - b)
                self.take(cls, away, base)
                self.send(cls, away, base + 2, place.pair(first_x, plane, a, 1 - b))
            for cls in self.late:
                a, b = place.own(cls == 2)
                self.take(cls, place.pair(cls == 2, plane, a, b), base + 1)
            for cls in self.late:
                self.take(cls, place.me, base + 2)
                if not self.copies.waiting:
                    self.done(cls)


STEPS = "CLGHMNTABPZEQRSX"


LAG = 14


class Plan:
    def __init__(self, steps, copies, sent, stages):
        self.steps = steps
        self.copies = copies
        self.sent = sent
        self.stages = stages
        self.open = []

    @staticmethod
    def act(copies, step):
        kind, plane, hop = step // 100, step // 10 % 10, step % 10
        act = getattr(copies, STEPS[kind])
        if STEPS[kind] in "LGTZQ":
            act(plane, hop)
        elif STEPS[kind] in "MNX":
            act()
        else:
            act(plane)

    def run(self):
        for step in self.steps:
            if step < 100:
                self.stages[step]()
                continue
            self.act(self.copies, step)
            self.open.append(step)
            if len(self.open) > LAG:
                self.act(self.sent, self.open.pop(0))

    def flush(self):
        for step in self.open:
            self.act(self.sent, step)
        self.open.clear()


BLOCK = 256
LINES = 32
NORM_ROWS = 64
UNROLL = 3
ATTEND_UNROLL = 2
PAIRS = D // 128
VEC_UNIT = 48
VEC_ROWS = 32
F32 = jnp.float32
BF16 = jnp.bfloat16


def dot_nn(left, right):
    return lax.dot_general(left, right, (((1,), (0,)), ((), ())), preferred_element_type=F32)


def dot_nt(left, right):
    return lax.dot_general(left, right, (((1,), (1,)), ((), ())), preferred_element_type=F32)


def dot_tn(left, right):
    return lax.dot_general(left, right, (((0,), (0,)), ((), ())), preferred_element_type=F32)


def chunk(start, size=BLOCK):
    if isinstance(start, int):
        return pl.ds(start, size)
    return pl.ds(pl.multiple_of(start, 128 if size % 128 == 0 else TILE), size)


def iota(shape, dim):
    return lax.broadcasted_iota(jnp.int32, shape, dim)


def unit_of(column):
    return lax.shift_right_logical(column * 1366, 16)


def unit_spread():
    column = iota((128, D), 1)
    return (column - VEC_UNIT * unit_of(column) == iota((128, D), 0)).astype(BF16)


def vec_gathered(tiles, per):
    shards = tiles.shape[0]
    count = shards * VEC_ROWS
    spread = dot_nn(tiles[...].reshape(count, 128), unit_spread())
    row = iota((count, D), 0)
    inner = row & (VEC_ROWS - 1)
    unit = lax.shift_right_logical(row, 5) * per + inner
    mask = ((unit & 15) == unit_of(iota((count, D), 1))) & (inner < per)
    spread = jnp.where(mask, spread, 0.0).astype(BF16)
    row = iota((VEC_ROWS, count), 1)
    inner = row & (VEC_ROWS - 1)
    unit = lax.shift_right_logical(row, 5) * per + inner
    pick = (lax.shift_right_logical(unit, 4) == iota((VEC_ROWS, count), 0)) & (inner < per)
    return dot_nn(pick.astype(F32).astype(BF16), spread)


def exact_dot(pick, values, dot):
    high = values.astype(BF16)
    rest = values - high.astype(F32)
    middle = rest.astype(BF16)
    low = (rest - middle.astype(F32)).astype(BF16)
    return dot(pick, high) + dot(pick, middle) + dot(pick, low)


def vec_shard(rows, me, per):
    unit = me * per + iota((VEC_ROWS, VEC_ROWS), 0)
    pick = (lax.shift_right_logical(unit, 4) == iota((VEC_ROWS, VEC_ROWS), 1)).astype(F32)
    lines = exact_dot(pick.astype(BF16), rows, dot_nn)
    unit = me * per + iota((VEC_ROWS, D), 0)
    mask = (unit & 15) == unit_of(iota((VEC_ROWS, D), 1))
    lines = jnp.where(mask, lines, 0.0)
    spread = unit_spread()
    return exact_dot(spread, lines, lambda pick, part: dot_nt(part, pick))


def in_line(tile):
    group = 8 * VEC_UNIT
    column = iota((128, group), 1)
    pick = (column - VEC_UNIT * unit_of(column) == iota((128, group), 0)).astype(F32)
    spread = exact_dot(pick.astype(BF16), tile, lambda pick, part: dot_nn(part, pick))
    mask = (iota((VEC_ROWS, group), 0) & 7) == unit_of(iota((VEC_ROWS, group), 1))
    spread = jnp.where(mask, spread, 0.0)
    gather = lax.shift_right_logical(iota((8, VEC_ROWS), 1), 3) == iota((8, VEC_ROWS), 0)
    lines = exact_dot(gather.astype(F32).astype(BF16), spread, dot_nn)
    rows = [lines[row // 3 : row // 3 + 1, row % 3 * 128 : row % 3 * 128 + 128] for row in range(8)]
    return jnp.concatenate(rows, axis=0)


class Compute:
    def __init__(self, w, vrows, gvec, red, eye):
        self.w = w
        self.eye = eye
        self.vrows = vrows
        self.gvec = gvec
        self.red = red

    def vec(self, index):
        return self.vrows[pl.ds(index, 1), :]

    def turned(self, values):
        size = values.shape[1]
        return dot_nt(self.eye[pl.ds(0, size), pl.ds(0, size)], values).astype(BF16)

    def norm(self, src, src_row, dst, dst_row, rows, gain, shift, unit, unit_row, rate, rate_row):
        scale_vec, shift_vec = self.vec(gain), self.vec(shift)

        @pl.loop(0, rows // NORM_ROWS)
        def _(index):
            x = src[chunk(src_row + index * NORM_ROWS, NORM_ROWS), :].astype(F32)
            centre = x - jnp.mean(x, axis=-1, keepdims=True)
            spread = jnp.mean(centre * centre, axis=-1, keepdims=True)
            scale = lax.rsqrt(spread + 1e-06)
            even = centre * scale
            result = even * scale_vec + shift_vec
            dst[chunk(dst_row + index * NORM_ROWS, NORM_ROWS), :] = result.astype(BF16)
            if unit is not None:
                unit[chunk(unit_row + index * NORM_ROWS, NORM_ROWS), :] = even.astype(unit.dtype)
            rate[chunk(rate_row + index * NORM_ROWS, NORM_ROWS), :] = jnp.broadcast_to(
                scale, (NORM_ROWS, 128)
            )

    def unit_rows(self, src, rows):
        @pl.loop(0, rows // NORM_ROWS)
        def _(index):
            at = chunk(index * NORM_ROWS, NORM_ROWS)
            x = src[at, :].astype(F32)
            centre = x - jnp.mean(x, axis=-1, keepdims=True)
            spread = jnp.mean(centre * centre, axis=-1, keepdims=True)
            src[at, :] = (centre * lax.rsqrt(spread + 1e-06)).astype(src.dtype)

    def norm_back(
        self, unit, unit_row, rate, rate_row, grad, rest, out, low, rows, gain, shift
    ):
        scale_vec = self.vec(gain)
        self.red[...] = jnp.zeros_like(self.red)

        @pl.loop(0, rows // NORM_ROWS)
        def _(index):
            at = chunk(index * NORM_ROWS, NORM_ROWS)
            even = unit[chunk(unit_row + index * NORM_ROWS, NORM_ROWS), :].astype(F32)
            scale = rate[chunk(rate_row + index * NORM_ROWS, NORM_ROWS), 0:1]
            d = grad[at, :]
            along = d * even
            self.red[0] += jnp.sum(along.reshape(NORM_ROWS // 8, 8, D), axis=0)
            self.red[1] += jnp.sum(d.reshape(NORM_ROWS // 8, 8, D), axis=0)
            d = d * scale_vec
            mean = jnp.mean(d, axis=-1, keepdims=True)
            along = jnp.mean(along * scale_vec, axis=-1, keepdims=True)
            total = rest[at, :].astype(F32) + scale * (d - mean - even * along)
            if out is not None:
                out[at, :] = total
            if low is not None:
                low[at, :] = total.astype(BF16)

        self.gvec[pl.ds(gain, 1), :] = jnp.sum(self.red[0], axis=0, keepdims=True)
        self.gvec[pl.ds(shift, 1), :] = jnp.sum(self.red[1], axis=0, keepdims=True)

    def row_sum(self, values):
        ones = jnp.ones((TILE, values.shape[0]), BF16)
        return dot_nn(ones, values)[0:1]

    def linear(self, src, row, rows, index, bias, emit):
        @pl.loop(0, D // BLOCK, unroll=UNROLL)
        def _(part):
            cols = chunk(part * BLOCK)
            made = dot_nn(src[pl.ds(row, rows), :], self.w[chunk(index * D, D), cols])
            if bias is not None:
                made = made + self.vrows[pl.ds(bias, 1), cols]
            emit(cols, made)

    def linear_back(self, pairs, emit):
        @pl.loop(0, D // BLOCK, unroll=UNROLL)
        def _(part):
            total = None
            for grad, index in pairs:
                made = dot_nt(grad(), self.w[chunk(index * D + part * BLOCK), :])
                total = made if total is None else total + made
            emit(chunk(part * BLOCK), total)

    def weight_grad(self, left, right, index, parts=D // BLOCK):
        @pl.loop(0, parts, unroll=UNROLL)
        def _(part):
            total = None
            for one, other in zip(left(part), right):
                made = dot_tn(one, other())
                total = made if total is None else total + made
            self.w[chunk(index * D + part * BLOCK), :] = total.astype(BF16)

    def hidden(self, src, row, rows, first, bias, act, slope, pieces=(0, FF // D)):
        each = D // BLOCK

        @pl.loop(pieces[0] * each, pieces[1] * each, unroll=UNROLL)
        def _(part):
            piece = lax.div(part, each)
            u = dot_nt(src[pl.ds(row, rows), :], self.w[chunk(first * D + part * BLOCK), :])
            u = u + self.vrows[pl.ds(bias + piece, 1), chunk(lax.rem(part, each) * BLOCK)]
            square = u * u
            t = jnp.tanh(u * (0.7978845608028654 + 0.035677408136300125 * square))
            half = 0.5 + 0.5 * t
            at = (pl.ds(0, rows), chunk(part * BLOCK))
            made = u * half
            act[at] = made.astype(BF16)
            rise = 1.5957691216057308 + 0.21406444881780074 * square
            slope[at] = (half + made * (1.0 - half) * rise).astype(BF16)

    def project(self, act, rows, first, emit):
        @pl.loop(0, D // BLOCK)
        def _(part):
            cols = chunk(part * BLOCK)
            emit(cols, dot_nn(act[pl.ds(0, rows), :], self.w[chunk(first * D, FF), cols]))

    def hidden_back(self, low, rows, first, slope):
        @pl.loop(0, FF // BLOCK, unroll=UNROLL)
        def _(part):
            made = dot_nt(low[pl.ds(0, rows), :], self.w[chunk(first * D + part * BLOCK), :])
            at = (pl.ds(0, rows), chunk(part * BLOCK))
            slope[at] = (made * slope[at].astype(F32)).astype(BF16)

    def wide_grad(self, left, rows, right, first):
        self.weight_grad(
            lambda part: [left[pl.ds(0, rows), chunk(part * BLOCK)]], [right], first, FF // BLOCK
        )

    def wide_sums(self, slope, rows, bias):
        for piece in range(FF // D):
            self.gvec[pl.ds(bias + piece, 1), :] = self.row_sum(
                slope[pl.ds(0, rows), pl.ds(piece * D, D)]
            )

    @staticmethod
    def halves(tile, scale=1.0):
        low = jnp.where(iota(tile.shape, 1) < HEAD, scale, 0.0).astype(BF16)
        high = jnp.where(iota(tile.shape, 1) < HEAD, 0.0, scale).astype(BF16)
        return tile * low, tile * high

    def attend(self, allowed, q_at, k_at, v_at, p_at, o_at):
        @pl.loop(0, PAIRS, unroll=ATTEND_UNROLL)
        def _(pair):
            keys = k_at(pair)[...]
            values = self.turned(v_at(pair)[...])
            mixed = []
            for half, queries in enumerate(self.halves(q_at(pair)[...], 0.125)):
                scores = jnp.where(allowed, dot_nt(keys, queries), -1000000000.0)
                expd = jnp.exp(scores - jnp.max(scores, axis=0, keepdims=True))
                rate = 1.0 / jnp.sum(expd, axis=0, keepdims=True)
                probs = (expd * rate).astype(BF16)
                p_at(pair, half)[...] = probs
                mixed.append(dot_nn(values, probs)[half * HEAD : (half + 1) * HEAD])
            o_at(pair)[...] = self.turned(jnp.concatenate(mixed, axis=0).astype(BF16))

    def attend_back(self, q_at, k_at, v_at, p_at, do_at):
        @pl.loop(0, PAIRS, unroll=ATTEND_UNROLL)
        def _(pair):
            keys = self.turned(k_at(pair)[...])
            values = v_at(pair)[...]
            grad_q, grad_k, grad_v = [], 0.0, 0.0
            both = zip(self.halves(q_at(pair)[...], 0.125), self.halves(do_at(pair)[...]))
            for half, (queries, grads) in enumerate(both):
                low = p_at(pair, half)[...]
                probs = low.astype(F32)
                grad_probs = dot_nt(values, grads)
                inner = jnp.sum(probs * grad_probs, axis=0, keepdims=True)
                grad_scores = (probs * (grad_probs - inner)).astype(BF16)
                grad_q.append(dot_nn(keys, grad_scores)[half * HEAD : (half + 1) * HEAD])
                grad_k = grad_k + dot_nn(grad_scores, queries)
                grad_v = grad_v + dot_nn(low, grads)
            grad_q = jnp.concatenate(grad_q, axis=0) * 0.125
            q_at(pair)[...] = self.turned(grad_q.astype(BF16))
            k_at(pair)[...] = grad_k.astype(BF16)
            v_at(pair)[...] = grad_v.astype(BF16)


def store_to(ref, row, rows, col=0):
    def emit(cols, values):
        ref[pl.ds(row, rows), chunk(col + cols.start)] = values.astype(ref.dtype)

    return emit


def fused_kernel(
    depth,
    sizes,
    pers,
    slots,
    words,
    images_in,
    enc_cot,
    tissue,
    text_len,
    text_in,
    enc_in,
    dec_in,
    enc_tile,
    dec_tile,
    dec_cot,
    enc_out,
    dec_out,
    image_out,
    text_out,
    enc_g,
    dec_g,
    enc_v,
    dec_v,
    w,
    land,
    xin,
    n1,
    q,
    k,
    v,
    o,
    h,
    n2,
    act,
    gp,
    e,
    cot,
    acc,
    dh,
    low,
    dmix,
    keep_col,
    rates,
    tiles,
    vrows,
    gvec,
    vland,
    vout,
    red,
    eye,
    load_sems,
    ag_send,
    ag_recv,
    vec_send,
    vec_recv,
    rs_send,
    rs_recv,
    sum_send,
    sum_recv,
    x_send,
    x_recv,
    out_local,
    out_send,
    out_recv,
    gate_sem,
):
    shards = depth * 4
    place = Place(depth)
    me, z = place.me, place.z
    section = place.section
    image_rows, text_rows = xin.shape[0], text_in.shape[0]
    images, used = tissue.shape
    comp = Compute(w, vrows, gvec, red, eye)
    cuts = [split_rows(rows, LATE) for rows in sizes]

    def load(index, src, dst, waiting=False):
        copy = pltpu.make_async_copy(src, dst, load_sems.at[index])
        if waiting:
            copy.wait()
        else:
            copy.start()

    def own_rows(which):
        return w.at[pl.ds(pl.multiple_of(me * sizes[which], TILE), sizes[which])]

    def load_own(which, waiting):
        load(0, (enc_in, dec_in)[which], own_rows(which), waiting)
        load(1, (enc_tile, dec_tile)[which], tiles.at[me], waiting)

    def load_text(waiting):
        load(2, text_in, xin.at[pl.ds(0, text_rows)], waiting)
        load(3, dec_cot, low.at[pl.ds(0, text_rows)], waiting)

    for which in (0, 1):

        @pl.when(section == which)
        def _():
            load_own(which, False)
            if which == 1:
                load_text(False)

    greet(place, shards, True)

    def give_vecs(waiting):
        src = tiles.at[me]
        for step in range(1, shards):
            Copies(place, waiting).start(
                None, src, src, vec_send.at[step], vec_recv.at[me], lax.rem(me + step, shards)
            )

    def got_vecs():
        for step in range(1, shards):
            frm = lax.rem(me + step, shards)
            Copies(place).arrived(tiles.at[frm], vec_send.at[step], vec_recv.at[frm])

    def across(waiting, index, src, dst):
        Copies(place, waiting).start(
            None, src, dst, x_send.at[index], x_recv.at[index], me, 1 - section
        )

    def crossed(index, dst):
        Copies(place).arrived(dst, x_send.at[index], x_recv.at[index])

    def give(waiting, index, src, dst):
        local = pltpu.make_async_copy(src, dst, out_local.at[index])
        if waiting:
            local.wait()
        else:
            local.start()
        Copies(place, waiting).start(
            None, src, dst, out_send.at[index], out_recv.at[index], me, 1 - section
        )

    def got(index, dst):
        Copies(place).arrived(dst, out_send.at[index], out_recv.at[index])

    def share_sums(waiting, slot, to):
        Copies(place, waiting).start(
            None, gvec, vland.at[slot], sum_send.at[slot], sum_recv.at[slot], to
        )

    def got_sums(slot):
        Copies(place).arrived(vland.at[slot], sum_send.at[slot], sum_recv.at[slot])

    def open_gate():
        pl.semaphore_signal(
            gate_sem, inc=1, device_id=(1 - section, me), device_id_type=MESH
        )

    def pass_gate():
        pl.semaphore_wait(gate_sem, 1)

    flips = (place.shard(z, place.y, 1 - place.x), place.shard(z, 1 - place.y, place.x))

    def sum_stages(which):
        def along_x():
            share_sums(False, 0, flips[0])

        def along_y():
            got_sums(0)
            share_sums(True, 0, flips[0])
            gvec[...] = gvec[...] + vland[0]
            share_sums(False, 1, flips[1])

        def along_z():
            got_sums(1)
            share_sums(True, 1, flips[1])
            gvec[...] = gvec[...] + vland[1]
            for step in range(1, depth):
                share_sums(False, 1 + step, lax.rem(me + 4 * step, shards))

        def ended():
            summed = gvec[...]
            for step in range(1, depth):
                got_sums(1 + step)
                share_sums(True, 1 + step, lax.rem(me + 4 * step, shards))
                summed = summed + vland[1 + step]
            vout[...] = vec_shard(summed, me, pers[which])
            give(False, 6, vout, (enc_v, dec_v)[which])

        return {30: along_x, 31: along_y, 32: along_z, 33: ended}

    def gather(which, waiting=False):
        return Gather(
            Copies(place, waiting),
            place,
            depth,
            sizes[which],
            cuts[which],
            w,
            ag_send,
            ag_recv,
            open_gate if which == 0 else pass_gate,
        )

    def give_class(waiting, which, cls):
        start, size = cuts[which][cls]
        if size:
            src = w.at[pl.ds(pl.multiple_of(me * sizes[which] + start, TILE), size)]
            give(waiting, 2 + cls, src, (enc_g, dec_g)[which].at[pl.ds(start, size)])

    def got_class(which, cls):
        start, size = cuts[which][cls]
        if size:
            got(2 + cls, (enc_g, dec_g)[which].at[pl.ds(start, size)])

    def scatter(which, waiting=False):
        return Scatter(
            Copies(place, waiting),
            place,
            depth,
            sizes[which],
            cuts[which],
            w,
            land,
            rs_send,
            rs_recv,
            functools.partial(give_class, False, which),
        )

    def start_stage(which):
        eye[...] = jnp.where(
            iota((BLOCK, BLOCK), 0) == iota((BLOCK, BLOCK), 1), 1.0, 0.0
        ).astype(BF16)
        got_vecs()
        vrows[...] = vec_gathered(tiles, pers[which])
        gvec[...] = jnp.zeros_like(gvec)

    def padded(src):
        row = iota((image_rows, src.shape[0]), 0)
        slot = row & (slots - 1)
        frm = lax.shift_right_logical(row, 8) * used + slot
        pick = (iota((image_rows, src.shape[0]), 1) == frm) & (slot < used)
        return dot_nn(pick.astype(F32).astype(BF16), src[...]).astype(BF16)

    def fill_keep():
        keep_col[...] = jnp.zeros_like(keep_col)
        for image in range(images):
            line = tissue[pl.ds(image, 1), :].astype(F32).astype(BF16)
            lines = jnp.broadcast_to(line, (TILE, used))
            keep_col[pl.ds(image * slots, used), :] = dot_tn(
                lines, jnp.full((TILE, 128), 1.0 / TILE, BF16)
            )

    def spread(column, wide):
        return jnp.concatenate([column] * (wide // 128), axis=1) > 0.5

    def section_program(which, make):
        stages = sum_stages(which)
        gathering = Plan(GATHER_PLANS[which], gather(which), gather(which, True), stages)
        scattering = Plan(SCATTER_PLANS[which], scatter(which), scatter(which, True), stages)

        def gathered():
            gathering.flush()
            give_vecs(True)

        made, last = make(gathered)
        stages.update(made)
        load_own(which, True)
        gathering.run()
        scattering.run()
        scattering.flush()
        for cls in range(4):
            give_class(True, which, cls)
        give(True, 6, vout, (enc_v, dec_v)[which])
        last()
        for cls in range(4):
            got_class(1 - which, cls)
        got(6, (enc_v, dec_v)[1 - which])

    def encoder(gathered):
        rows = image_rows
        every = pl.ds(0, rows)
        stages = {}

        def stage(number):
            def keep(step):
                stages[number] = step
                return step

            return keep

        spare = shards * sizes[0]

        def at(ref, image):
            return lambda pair: ref.at[pl.ds(image * slots, slots), chunk(pair * 128, 128)]

        def p_at(image):
            def of(pair, half):
                index = (image * PAIRS + pair) * 2 + half
                row = spare + lax.div(index, 3) * slots
                return w.at[chunk(row, slots), chunk(lax.rem(index, 3) * slots, slots)]

            return of

        stages[8] = lambda: give_vecs(False)

        @stage(0)
        def _():
            fill_keep()
            xin[...] = padded(images_in)
            start_stage(0)
            comp.norm(xin, 0, n1, 0, rows, 0, 1, None, 0, rates.at[0], 0)

        @stage(1)
        def _():
            comp.linear(n1, 0, rows, 0, 2, store_to(q, 0, rows))
            comp.linear(n1, 0, rows, 1, None, store_to(k, 0, rows))
            comp.linear(n1, 0, rows, 2, 3, store_to(v, 0, rows))

        @stage(2)
        def _():
            for image in range(images):
                allowed = spread(keep_col[pl.ds(image * slots, slots), :], slots)
                comp.attend(
                    allowed, at(q, image), at(k, image), at(v, image), p_at(image), at(o, image)
                )

        @stage(3)
        def _():
            def add_input(cols, values):
                h[every, cols] = xin[every, cols].astype(F32) + values

            comp.linear(o, 0, rows, 3, 4, add_input)
            comp.norm(h, 0, n2, 0, rows, 5, 6, dh, 0, rates.at[1], 0)

        @stage(4)
        def _():
            comp.hidden(n2, 0, rows, 4, 8, act, gp, (0, 2))

        @stage(5)
        def _():
            comp.hidden(n2, 0, rows, 4, 8, act, gp, (2, 4))

        @stage(6)
        def _():
            def add_middle(cols, values):
                keep = jnp.concatenate([keep_col[...]] * (BLOCK // 128), axis=1)
                made = h[every, cols] + values + vrows[pl.ds(7, 1), cols]
                e[every, cols] = (made * keep).astype(BF16)

            comp.project(act, rows, 8, add_middle)
            across(False, 0, e, e)
            load(5, e, enc_out)

        @stage(7)
        def _():
            gathered()

            comp.unit_rows(xin, rows)

        @stage(10)
        def _():
            crossed(1, cot)

            @pl.loop(0, rows // LINES)
            def _(index):
                some = chunk(index * LINES, LINES)
                low[some, :] = (cot[some, :].astype(F32) * keep_col[some, 0:1]).astype(BF16)

            gvec[pl.ds(7, 1), :] = comp.row_sum(low[...])

        @stage(11)
        def _():
            comp.hidden_back(low, rows, 8, gp)

        @stage(12)
        def _():
            comp.wide_grad(act, rows, lambda: low[...], 8)

        @stage(13)
        def _():
            comp.project(gp, rows, 4, store_to(acc, 0, rows))

        @stage(14)
        def _():
            comp.wide_sums(gp, rows, 8)
            comp.wide_grad(gp, rows, lambda: n2[...], 4)

        @stage(15)
        def _():
            comp.norm_back(dh, 0, rates.at[1], 0, acc, low, dh, low, rows, 5, 6)

        @stage(16)
        def _():
            comp.linear_back([(lambda: low[...], 3)], store_to(dmix, 0, rows))

        @stage(17)
        def _():
            gvec[pl.ds(4, 1), :] = comp.row_sum(low[...])
            comp.weight_grad(lambda part: [o[:, chunk(part * BLOCK)]], [lambda: low[...]], 3)

        def heads_back(image):
            comp.attend_back(
                at(q, image), at(k, image), at(v, image), p_at(image), at(dmix, image)
            )

        stages[18] = lambda: heads_back(0)
        stages[19] = lambda: [heads_back(image) for image in range(1, images)]

        @stage(20)
        def _():
            comp.linear_back(
                [(lambda: q[...], 0), (lambda: k[...], 1), (lambda: v[...], 2)],
                store_to(acc, 0, rows),
            )

        @stage(21)
        def _():
            gvec[pl.ds(2, 1), :] = comp.row_sum(q[...])
            gvec[pl.ds(3, 1), :] = comp.row_sum(v[...])
            for index, ref in enumerate((q, k, v)):
                comp.weight_grad(
                    lambda part: [n1[:, chunk(part * BLOCK)]], [lambda: ref[...]], index
                )

        @stage(22)
        def _():
            comp.norm_back(xin, 0, rates.at[0], 0, acc, dh, None, low, rows, 0, 1)
            give(False, 1, low, image_out)

        def last():
            across(True, 0, e, e)
            load(5, e, enc_out, True)
            give(True, 1, low, image_out)
            got(0, dec_out)
            got(1, text_out)

        return stages, last

    def decoder(gathered):
        half = text_rows
        lower, upper = pl.ds(0, half), pl.ds(half, half)
        stages = {}

        def stage(number):
            def keep(step):
                stages[number] = step
                return step

            return keep

        def at(ref, image, base=0):
            return lambda pair: ref.at[
                pl.ds(base + image * words, words), chunk(pair * 128, 128)
            ]

        def p_self(image):
            ref = (k, v)[image]

            def of(pair, side):
                row = half + lax.div(pair, 3) * words
                return ref.at[
                    chunk(row, words), chunk((lax.rem(pair, 3) * 2 + side) * words, words)
                ]

            return of

        def p_cross(image):
            return lambda pair, side: act.at[
                upper, chunk(((image * PAIRS + pair) * 2 + side) * words, words)
            ]

        def cross_kv(image, which):
            col = (which * images + image) * D
            return lambda pair: gp.at[pl.ds(half, slots), chunk(col + pair * 128, 128)]

        def pair_ref(image, which):
            return lambda: gp[pl.ds(half, slots), pl.ds((which * images + image) * D, D)]

        def low_rows():
            return low[lower, :]

        dz = dmix.at[upper]
        decoded = xin.at[upper]
        text_grad = low.at[upper]

        stages[29] = lambda: give_vecs(False)

        @stage(0)
        def _():
            load_text(True)
            fill_keep()
            cot[...] = padded(enc_cot)
            start_stage(1)
            comp.norm(xin, 0, n1, 0, half, 0, 1, n1, half, rates.at[0], 0)

        @stage(1)
        def _():
            comp.linear(n1, 0, half, 0, 2, store_to(q, 0, half))
            comp.linear(n1, 0, half, 1, None, store_to(k, 0, half))
            comp.linear(n1, 0, half, 2, 3, store_to(v, 0, half))

        @stage(2)
        def _():
            key, query = iota((words, words), 0), iota((words, words), 1)
            for image in range(images):
                allowed = (key <= query) & (key < text_len[image])
                comp.attend(
                    allowed, at(q, image), at(k, image), at(v, image), p_self(image), at(o, image)
                )

        @stage(3)
        def _():
            def add_input(cols, values):
                h[lower, cols] = xin[lower, cols].astype(F32) + values

            comp.linear(o, 0, half, 3, 4, add_input)
            comp.norm(h, 0, n2, 0, half, 5, 6, acc, half, rates.at[1], 0)

        @stage(4)
        def _():
            comp.linear(n2, 0, half, 4, 7, store_to(q, half, half))

        @stage(5)
        def _():
            crossed(0, e)
            load(5, e, enc_out)
            for image in range(images):
                row = image * slots
                comp.linear(e, row, slots, 5, None, store_to(gp, half, slots, image * D))
                comp.linear(e, row, slots, 6, 8, store_to(gp, half, slots, (images + image) * D))

        @stage(6)
        def _():
            for image in range(images):
                allowed = spread(keep_col[pl.ds(image * slots, slots), :], words)
                comp.attend(
                    allowed,
                    at(q, image, half),
                    cross_kv(image, 0),
                    cross_kv(image, 1),
                    p_cross(image),
                    at(o, image, half),
                )

        @stage(7)
        def _():
            def add_self(cols, values):
                h[upper, cols] = h[lower, cols] + values

            comp.linear(o, half, half, 7, 9, add_self)
            comp.norm(h, half, n2, half, half, 10, 11, dh, half, rates.at[2], 0)

        @stage(8)
        def _():
            comp.hidden(n2, half, half, 8, 13, act, gp)

        @stage(9)
        def _():
            def add_middle(cols, values):
                made = h[upper, cols] + values + vrows[pl.ds(12, 1), cols]
                xin[upper, cols] = made.astype(BF16)

            comp.project(act.at[lower], half, 12, add_middle)
            give(False, 0, decoded, dec_out)

        @stage(10)
        def _():
            comp.hidden_back(low, half, 12, gp)
            dz[...] = low_rows()

        @stage(11)
        def _():
            gathered()
            gvec[pl.ds(12, 1), :] = comp.row_sum(dz[...])
            comp.wide_grad(act, half, lambda: dz[...], 12)

        @stage(12)
        def _():
            comp.project(gp.at[lower], half, 8, store_to(acc, 0, half))

        @stage(13)
        def _():
            comp.wide_sums(gp, half, 13)
            comp.wide_grad(gp, half, lambda: n2[upper, :], 8)

        @stage(14)
        def _():
            comp.norm_back(dh, half, rates.at[2], 0, acc, low, dh, low, half, 10, 11)
            comp.linear_back([(low_rows, 7)], store_to(dmix, 0, half))

        @stage(15)
        def _():
            for image in range(images):
                comp.attend_back(
                    at(q, image, half),
                    cross_kv(image, 0),
                    cross_kv(image, 1),
                    p_cross(image),
                    at(dmix, image),
                )

        @stage(16)
        def _():
            for image in range(images):
                rows = pl.ds(image * slots, slots)

                def add_cot(cols, values):
                    cot[rows, cols] = (cot[rows, cols].astype(F32) + values).astype(BF16)

                comp.linear_back([(pair_ref(image, 0), 5), (pair_ref(image, 1), 6)], add_cot)
            across(False, 1, cot, cot)

        @stage(17)
        def _():
            gvec[pl.ds(9, 1), :] = comp.row_sum(low_rows())
            comp.weight_grad(lambda part: [o[upper, chunk(part * BLOCK)]], [low_rows], 7)

        @stage(18)
        def _():
            comp.linear_back([(lambda: q[upper, :], 4)], store_to(acc, 0, half))

        @stage(19)
        def _():
            gvec[pl.ds(7, 1), :] = comp.row_sum(q[upper, :])
            total = comp.row_sum(pair_ref(0, 1)())
            for image in range(1, images):
                total = total + comp.row_sum(pair_ref(image, 1)())
            gvec[pl.ds(8, 1), :] = total
            comp.weight_grad(
                lambda part: [n2[lower, chunk(part * BLOCK)]], [lambda: q[upper, :]], 4
            )
            for which in (0, 1):
                comp.weight_grad(
                    lambda part: [
                        e[pl.ds(image * slots, slots), chunk(part * BLOCK)]
                        for image in range(images)
                    ],
                    [pair_ref(image, which) for image in range(images)],
                    5 + which,
                )

        @stage(20)
        def _():
            comp.norm_back(acc, half, rates.at[1], 0, acc, dh, dh, low, half, 5, 6)

        @stage(21)
        def _():
            comp.linear_back([(low_rows, 3)], store_to(dmix, 0, half))

        @stage(22)
        def _():
            gvec[pl.ds(4, 1), :] = comp.row_sum(low_rows())
            comp.weight_grad(lambda part: [o[lower, chunk(part * BLOCK)]], [low_rows], 3)

        @stage(23)
        def _():
            for image in range(images):
                comp.attend_back(
                    at(q, image), at(k, image), at(v, image), p_self(image), at(dmix, image)
                )

        @stage(24)
        def _():
            comp.linear_back(
                [(lambda: q[lower, :], 0), (lambda: k[lower, :], 1), (lambda: v[lower, :], 2)],
                store_to(acc, 0, half),
            )

        @stage(25)
        def _():
            gvec[pl.ds(2, 1), :] = comp.row_sum(q[lower, :])
            gvec[pl.ds(3, 1), :] = comp.row_sum(v[lower, :])
            for index, ref in enumerate((q, k, v)):
                comp.weight_grad(
                    lambda part: [n1[lower, chunk(part * BLOCK)]], [lambda: ref[lower, :]], index
                )

        @stage(26)
        def _():
            comp.norm_back(n1, half, rates.at[0], 0, acc, dh, None, text_grad, half, 0, 1)
            give(False, 1, text_grad, text_out)

        def last():
            across(True, 1, cot, cot)
            load(5, e, enc_out, True)
            give(True, 0, decoded, dec_out)
            give(True, 1, text_grad, text_out)
            got(1, image_out)

        return stages, last

    pl.when(section == 0)(lambda: section_program(0, encoder))
    pl.when(section == 1)(lambda: section_program(1, decoder))


def finish_kernel(
    used, encoded, decoded, images, text, enc, dec, enc_v, dec_v, *outs
):
    enc_out, dec_out, image_out, text_out, enc_out_g, dec_out_g, enc_out_v, dec_out_v = outs
    slots = BLOCK

    def cut(ref):
        rows = ref[...].astype(F32)
        parts = [
            rows[image * slots : image * slots + used] for image in range(rows.shape[0] // slots)
        ]
        return jnp.concatenate(parts, axis=0)

    @pl.when(pl.program_id(0) == 0)
    def _():
        enc_out[...] = cut(encoded).astype(BF16)
        image_out[...] = cut(images)
        enc_out_v[...] = in_line(enc_v[...])
        dec_out_v[...] = in_line(dec_v[...])

    dec_out[...] = decoded[...]
    text_out[...] = text[...].astype(F32)
    enc_out_g[...] = enc[...].astype(F32)
    dec_out_g[...] = dec[...].astype(F32)


def vec_tile_of(vecs):
    units = vecs.reshape(-1, VEC_UNIT)
    return jnp.pad(units, ((0, VEC_ROWS - units.shape[0]), (0, 128 - VEC_UNIT)))


def body_fast(
    images, text, enc_mats, enc_vecs, dec_mats, dec_vecs, tissue, text_len, enc_cot, dec_cot
):
    shards = lax.axis_size("dp")
    depth = grid_of(shards)[0]
    img_count, slots = tissue.shape
    words = text.shape[0] // img_count
    sizes = (enc_mats.shape[0], dec_mats.shape[0])
    pers = (enc_vecs.shape[0] // VEC_UNIT, dec_vecs.shape[0] // VEC_UNIT)
    wide = BLOCK
    image_rows, text_rows = img_count * wide, img_count * words
    any_space = pl.BlockSpec(memory_space=pl.ANY)
    vmem_space = pl.BlockSpec(memory_space=pltpu.VMEM)
    smem_space = pl.BlockSpec(memory_space=pltpu.SMEM)
    most = sizes[1]

    def low_buffer(rows=image_rows, columns=D):
        return pltpu.VMEM((rows, columns), BF16)

    def wide_buffer(rows=image_rows):
        return pltpu.VMEM((rows, D), F32)

    dma = pltpu.SemaphoreType.DMA
    made = pl.pallas_call(
        functools.partial(fused_kernel, depth, sizes, pers, wide, words),
        out_shape=(
            jax.ShapeDtypeStruct((image_rows, D), BF16),
            jax.ShapeDtypeStruct((text_rows, D), BF16),
            jax.ShapeDtypeStruct((image_rows, D), BF16),
            jax.ShapeDtypeStruct((text_rows, D), BF16),
            jax.ShapeDtypeStruct((sizes[0], D), BF16),
            jax.ShapeDtypeStruct((sizes[1], D), BF16),
            jax.ShapeDtypeStruct((VEC_ROWS, 128), F32),
            jax.ShapeDtypeStruct((VEC_ROWS, 128), F32),
        ),
        in_specs=[vmem_space] * 3 + [smem_space] + [any_space] * 6,
        out_specs=[any_space] * 8,
        scratch_shapes=[
            low_buffer(shards * most),
            low_buffer(max(Scatter.land_rows(depth, split_rows(rows, LATE)) for rows in sizes)),
            low_buffer(),
            low_buffer(),
            low_buffer(),
            low_buffer(),
            low_buffer(),
            low_buffer(),
            wide_buffer(),
            low_buffer(),
            low_buffer(image_rows, FF),
            low_buffer(image_rows, FF),
            low_buffer(),
            low_buffer(),
            wide_buffer(),
            wide_buffer(),
            low_buffer(),
            low_buffer(),
            pltpu.VMEM((image_rows, 128), F32),
            pltpu.VMEM((3, image_rows, 128), F32),
            pltpu.VMEM((shards, VEC_ROWS, 128), BF16),
            wide_buffer(VEC_ROWS),
            wide_buffer(VEC_ROWS),
            pltpu.VMEM((1 + depth, VEC_ROWS, D), F32),
            pltpu.VMEM((VEC_ROWS, 128), F32),
            pltpu.VMEM((2, 8, D), F32),
            low_buffer(BLOCK, BLOCK),
            dma((6,)),
            dma((4, shards, 4)),
            dma((4, shards)),
            dma((shards,)),
            dma((shards,)),
            dma((4, 4 * depth + 7)),
            dma((4, 4 * depth + 7)),
            dma((1 + depth,)),
            dma((1 + depth,)),
            dma((2,)),
            dma((2,)),
            dma((7,)),
            dma((7,)),
            dma((7,)),
            pltpu.SemaphoreType.REGULAR,
        ],
        compiler_params=pltpu.CompilerParams(
            collective_id=0, has_side_effects=True, vmem_limit_bytes=VMEM_LIMIT
        ),
        name="blocks_and_grads",
    )(
        images,
        enc_cot,
        tissue,
        text_len,
        text,
        enc_mats,
        dec_mats,
        vec_tile_of(enc_vecs),
        vec_tile_of(dec_vecs),
        dec_cot,
    )

    def tiled(rows):
        return pl.BlockSpec((rows // FINISH_STEPS, D), lambda step: (step, 0))

    def whole(shape):
        return pl.BlockSpec(shape, lambda step: (0, 0))

    image_spec, tile_spec = whole((image_rows, D)), whole((VEC_ROWS, 128))
    out_spec = whole((img_count * slots, D))
    outs = pl.pallas_call(
        functools.partial(finish_kernel, slots),
        grid=(FINISH_STEPS,),
        in_specs=[
            image_spec,
            tiled(text_rows),
            image_spec,
            tiled(text_rows),
            tiled(sizes[0]),
            tiled(sizes[1]),
            tile_spec,
            tile_spec,
        ],
        out_specs=[
            out_spec,
            tiled(text_rows),
            out_spec,
            tiled(text_rows),
            tiled(sizes[0]),
            tiled(sizes[1]),
            whole((8, 128)),
            whole((8, 128)),
        ],
        out_shape=(
            jax.ShapeDtypeStruct((img_count * slots, D), BF16),
            jax.ShapeDtypeStruct((text_rows, D), BF16),
            jax.ShapeDtypeStruct((img_count * slots, D), F32),
            jax.ShapeDtypeStruct((text_rows, D), F32),
            jax.ShapeDtypeStruct((sizes[0], D), F32),
            jax.ShapeDtypeStruct((sizes[1], D), F32),
            jax.ShapeDtypeStruct((8, 128), F32),
            jax.ShapeDtypeStruct((8, 128), F32),
        ),
        name="finish_outputs",
    )(*made)

    def vec_of(tile, per):
        return tile.reshape(-1)[: per * VEC_UNIT]

    return (
        outs[0],
        outs[1],
        outs[2],
        outs[3],
        outs[4],
        vec_of(outs[6], pers[0]),
        outs[5],
        vec_of(outs[7], pers[1]),
    )


FINISH_STEPS = 4
VMEM_LIMIT = 63 * 2**20
LATE = 0.21
GATHER_PLANS = (
    (
        120, 110, 400, 100, 130, 500, 121, 131, 8, 101, 111, 200, 231, 620, 630, 230, 102, 1500,
        221, 112, 201, 600, 631, 621, 601, 0, 103, 122, 211, 202, 132, 203, 610, 602, 603, 300,
        212, 220, 210, 611, 133, 1, 222, 2, 233, 632, 622, 612, 232, 310, 3, 4, 320, 5, 633, 330,
    ),
    (
        400, 500, 110, 130, 630, 100, 120, 101, 121, 102, 201, 1500, 29, 131, 111, 210, 600, 202,
        103, 601, 132, 112, 203, 631, 212, 610, 632, 620, 621, 200, 602, 0, 122, 222, 133, 603,
        211, 300, 221, 1, 2, 611, 232, 230, 3, 231, 612, 310, 233, 220, 4, 5, 633, 6, 7, 622, 320,
        8, 330, 10, 12,
    ),
)
SCATTER_PLANS = (
    (
        6, 7, 10, 11, 13, 14, 12, 1221, 730, 15, 16, 1231, 17, 1211, 18, 720, 19, 20, 1212, 830,
        1232, 21, 700, 1201, 1202, 930, 1310, 1031, 1233, 800, 1222, 820, 22, 30, 710, 1203, 900,
        1001, 920, 1021, 1002, 31, 1032, 810, 1300, 32, 1033, 1320, 1022, 910, 1410, 1011, 1330,
        1430, 1400, 33, 1012, 1003, 1110, 1420, 1130, 1100, 1120,
    ),
    (
        9, 11, 1231, 730, 14, 15, 16, 830, 13, 720, 1221, 18, 19, 17, 710, 1211, 930, 1031, 820,
        20, 21, 22, 23, 24, 1212, 25, 810, 700, 920, 1201, 1202, 26, 1222, 1021, 1232, 910, 1310,
        1011, 30, 1233, 1032, 800, 1022, 31, 1320, 32, 1012, 1420, 900, 1203, 1033, 1001, 1410,
        1130, 1002, 33, 1300, 1110, 1330, 1120, 1003, 1400, 1100, 1430,
    ),
)


def body(images, text, enc_mats, enc_vecs, dec_mats, dec_vecs, tissue, text_len, enc_cot, dec_cot):
    shards = lax.axis_size("dp")
    img_count, slots = tissue.shape
    words = text.shape[0] // img_count
    fits = (
        shards == 16
        and img_count == 2
        and slots <= BLOCK == 256
        and img_count * words == BLOCK
        and enc_mats.shape[0] % LINES == 0
        and dec_mats.shape[0] % LINES == 0
        and enc_vecs.shape[0] % VEC_UNIT == 0
        and dec_vecs.shape[0] % VEC_UNIT == 0
    )
    run = body_fast if fits else body_plain
    return run(
        images, text, enc_mats, enc_vecs, dec_mats, dec_vecs, tissue, text_len, enc_cot, dec_cot
    )


def solution(mesh):
    placed = (
        P("dp", None),
        P("dp", None),
        P("dp", None),
        P("dp"),
        P("dp", None),
        P("dp"),
        P("dp", None),
        P("dp"),
        P("dp", None),
        P("dp", None),
    )
    return jax.shard_map(
        body,
        mesh=mesh,
        in_specs=placed,
        out_specs=(
            P("dp", None),
            P("dp", None),
            P("dp", None),
            P("dp", None),
            P("dp", None),
            P("dp"),
            P("dp", None),
            P("dp"),
        ),
        check_vma=False,
    )
```

```python
import functools

import jax
import jax.numpy as jnp
from jax import lax
from jax.experimental import pallas as pl
from jax.experimental.pallas import tpu as pltpu
from jax.sharding import PartitionSpec as P

D = 768
HEAD = 64
FF = 3072
MICRO = 2


def shifted(block, axis, distance):
    devices = range(lax.axis_size(axis))
    route = [(i - distance, i) for i in devices if i - distance in devices]
    return lax.ppermute(block, axis, route)


def layer_norm(inputs, scale_vec, shift_vec):
    centre = inputs - jnp.mean(inputs, axis=-1, keepdims=True)
    spread = jnp.mean(centre * centre, axis=-1, keepdims=True)
    return centre * lax.rsqrt(spread + 1e-06) * scale_vec + shift_vec


def norm_back(inputs, scale_vec, shift_vec, grads):
    _, pullback = jax.vjp(layer_norm, inputs, scale_vec, shift_vec)
    return pullback(grads)


def gelu_back(inner, grads):
    _, pullback = jax.vjp(jax.nn.gelu, inner)
    return pullback(grads)[0]


def part_of(vecs, index):
    return vecs[index * D : (index + 1) * D].astype(jnp.float32)


def split_heads(rows):
    return rows.reshape(rows.shape[0], rows.shape[1], -1, HEAD)


def project(rows, weight):
    return jnp.einsum("bsd,de->bse", rows, weight, preferred_element_type=jnp.float32)


def row_sum(values):
    return jnp.sum(values.astype(jnp.float32), axis=(0, 1))


def attn_scores(queries, key_rows, allowed):
    scores = (
        jnp.einsum(
            "bqhe,bkhe->bhqk",
            split_heads(queries),
            split_heads(key_rows),
            preferred_element_type=jnp.float32,
        )
        * 0.125
    )
    return jnp.where(allowed, scores, -1000000000.0)


def attn_forward(queries, key_rows, value_rows, allowed):
    scores = attn_scores(queries, key_rows, allowed)
    peak = jnp.max(scores, axis=-1, keepdims=True)
    expd = jnp.exp(scores - peak)
    total = jnp.sum(expd, axis=-1, keepdims=True)
    probs = (expd / total).astype(jnp.bfloat16)
    mixed = jnp.einsum(
        "bhqk,bkhe->bqhe", probs, split_heads(value_rows), preferred_element_type=jnp.float32
    )
    return (mixed.reshape(queries.shape).astype(jnp.bfloat16), peak + jnp.log(total))


def attn_backward(queries, key_rows, value_rows, allowed, log_total, grad_mixed):
    scores = attn_scores(queries, key_rows, allowed)
    probs = jnp.exp(scores - log_total)
    grad_heads = split_heads(grad_mixed)
    grad_probs = jnp.einsum(
        "bqhe,bkhe->bhqk", grad_heads, split_heads(value_rows), preferred_element_type=jnp.float32
    )
    grad_scores = probs * (grad_probs - jnp.sum(grad_probs * probs, axis=-1, keepdims=True))
    grad_low = grad_scores.astype(jnp.bfloat16)
    grad_q = (
        jnp.einsum(
            "bhqk,bkhe->bqhe", grad_low, split_heads(key_rows), preferred_element_type=jnp.float32
        )
        * 0.125
    )
    grad_k = (
        jnp.einsum(
            "bhqk,bqhe->bkhe", grad_low, split_heads(queries), preferred_element_type=jnp.float32
        )
        * 0.125
    )
    grad_v = jnp.einsum(
        "bhqk,bqhe->bkhe",
        probs.astype(jnp.bfloat16),
        grad_heads,
        preferred_element_type=jnp.float32,
    )
    return (
        grad_q.reshape(queries.shape),
        grad_k.reshape(key_rows.shape),
        grad_v.reshape(value_rows.shape),
    )


def self_block(inputs, allowed, mats, vecs):
    wqkv = mats[0 : 3 * D].reshape(3, D, D)
    normed = layer_norm(inputs, part_of(vecs, 0), part_of(vecs, 1)).astype(jnp.bfloat16)
    qkv = jnp.einsum("bsd,kde->kbse", normed, wqkv, preferred_element_type=jnp.float32)
    queries = (qkv[0] + part_of(vecs, 2)).astype(jnp.bfloat16)
    key_rows = qkv[1].astype(jnp.bfloat16)
    value_rows = (qkv[2] + part_of(vecs, 3)).astype(jnp.bfloat16)
    mixed, log_total = attn_forward(queries, key_rows, value_rows, allowed)
    after = inputs + project(mixed, mats[3 * D : 4 * D]) + part_of(vecs, 4)
    return (after, (normed, queries, key_rows, value_rows, mixed, log_total))


def self_block_back(inputs, allowed, mats, vecs, saved, grad_after):
    normed, queries, key_rows, value_rows, mixed, log_total = saved
    wqkv = mats[0 : 3 * D].reshape(3, D, D)
    grad_low = grad_after.astype(jnp.bfloat16)
    grad_wout = jnp.einsum("bsd,bse->de", mixed, grad_low, preferred_element_type=jnp.float32)
    grad_mixed = jnp.einsum(
        "bse,de->bsd", grad_low, mats[3 * D : 4 * D], preferred_element_type=jnp.float32
    ).astype(jnp.bfloat16)
    grad_q, grad_k, grad_v = attn_backward(
        queries, key_rows, value_rows, allowed, log_total, grad_mixed
    )
    grad_qkv = jnp.stack([grad_q, grad_k, grad_v]).astype(jnp.bfloat16)
    grad_wqkv = jnp.einsum(
        "bsd,kbse->kde", normed, grad_qkv, preferred_element_type=jnp.float32
    ).reshape(3 * D, D)
    grad_normed = jnp.einsum("kbse,kde->bsd", grad_qkv, wqkv, preferred_element_type=jnp.float32)
    grad_in, grad_gain, grad_shift = norm_back(
        inputs, part_of(vecs, 0), part_of(vecs, 1), grad_normed
    )
    vec_grads = [
        grad_gain,
        grad_shift,
        row_sum(grad_qkv[0]),
        row_sum(grad_qkv[2]),
        row_sum(grad_low),
    ]
    return (grad_after + grad_in, [grad_wqkv, grad_wout], vec_grads)


def cross_block(inputs, image_rows, allowed, mats, vecs):
    normed = layer_norm(inputs, part_of(vecs, 5), part_of(vecs, 6)).astype(jnp.bfloat16)
    queries = (project(normed, mats[4 * D : 5 * D]) + part_of(vecs, 7)).astype(jnp.bfloat16)
    pair = jnp.einsum(
        "bsd,kde->kbse",
        image_rows,
        mats[5 * D : 7 * D].reshape(2, D, D),
        preferred_element_type=jnp.float32,
    )
    key_rows = pair[0].astype(jnp.bfloat16)
    value_rows = (pair[1] + part_of(vecs, 8)).astype(jnp.bfloat16)
    mixed, log_total = attn_forward(queries, key_rows, value_rows, allowed)
    after = inputs + project(mixed, mats[7 * D : 8 * D]) + part_of(vecs, 9)
    return (after, (normed, queries, key_rows, value_rows, mixed, log_total))


def cross_block_back(inputs, image_rows, allowed, mats, vecs, saved, grad_after):
    normed, queries, key_rows, value_rows, mixed, log_total = saved
    grad_low = grad_after.astype(jnp.bfloat16)
    grad_wout = jnp.einsum("bsd,bse->de", mixed, grad_low, preferred_element_type=jnp.float32)
    grad_mixed = jnp.einsum(
        "bse,de->bsd", grad_low, mats[7 * D : 8 * D], preferred_element_type=jnp.float32
    ).astype(jnp.bfloat16)
    grad_q, grad_k, grad_v = attn_backward(
        queries, key_rows, value_rows, allowed, log_total, grad_mixed
    )
    grad_query = grad_q.astype(jnp.bfloat16)
    grad_pair = jnp.stack([grad_k, grad_v]).astype(jnp.bfloat16)
    pair_weight = mats[5 * D : 7 * D].reshape(2, D, D)
    grad_wq = jnp.einsum("bsd,bse->de", normed, grad_query, preferred_element_type=jnp.float32)
    grad_wpair = jnp.einsum(
        "bsd,kbse->kde", image_rows, grad_pair, preferred_element_type=jnp.float32
    ).reshape(2 * D, D)
    grad_image = jnp.einsum(
        "kbse,kde->bsd", grad_pair, pair_weight, preferred_element_type=jnp.float32
    )
    grad_normed = jnp.einsum(
        "bse,de->bsd", grad_query, mats[4 * D : 5 * D], preferred_element_type=jnp.float32
    )
    grad_in, grad_gain, grad_shift = norm_back(
        inputs, part_of(vecs, 5), part_of(vecs, 6), grad_normed
    )
    vec_grads = [
        grad_gain,
        grad_shift,
        row_sum(grad_query),
        row_sum(grad_pair[1]),
        row_sum(grad_low),
    ]
    return (grad_after + grad_in, grad_image, [grad_wq, grad_wpair, grad_wout], vec_grads)


def mlp_block(inputs, w_in_t, w_out, norm_gain, norm_shift, bias_in, bias_out):
    normed = layer_norm(inputs, norm_gain, norm_shift).astype(jnp.bfloat16)
    inner = jnp.einsum("bsd,fd->bsf", normed, w_in_t, preferred_element_type=jnp.float32) + bias_in
    hidden = jax.nn.gelu(inner).astype(jnp.bfloat16)
    result = (
        inputs
        + jnp.einsum("bsf,fd->bsd", hidden, w_out, preferred_element_type=jnp.float32)
        + bias_out
    )
    return (result, (normed, inner, hidden))


def mlp_block_back(inputs, w_in_t, w_out, norm_gain, norm_shift, saved, grad_result):
    normed, inner, hidden = saved
    grad_low = grad_result.astype(jnp.bfloat16)
    grad_w_out = jnp.einsum("bsf,bsd->fd", hidden, grad_low, preferred_element_type=jnp.float32)
    grad_hidden = jnp.einsum("bsd,fd->bsf", grad_low, w_out, preferred_element_type=jnp.float32)
    grad_inner = gelu_back(inner, grad_hidden).astype(jnp.bfloat16)
    grad_w_in = jnp.einsum("bsf,bsd->fd", grad_inner, normed, preferred_element_type=jnp.float32)
    grad_normed = jnp.einsum("bsf,fd->bsd", grad_inner, w_in_t, preferred_element_type=jnp.float32)
    grad_in, grad_gain, grad_shift = norm_back(inputs, norm_gain, norm_shift, grad_normed)
    return (
        grad_result + grad_in,
        [grad_w_in, grad_w_out],
        [grad_gain, grad_shift, row_sum(grad_low), row_sum(grad_inner)],
    )


def encode(image_mb, keep, mats, vecs):
    inputs = image_mb.astype(jnp.float32)
    allowed = (keep > 0.5)[:, None, None, :]
    middle, saved_self = self_block(inputs, allowed, mats, vecs)
    result, saved_mlp = mlp_block(
        middle,
        mats[4 * D : 4 * D + FF],
        mats[4 * D + FF :],
        part_of(vecs, 5),
        part_of(vecs, 6),
        vecs[8 * D : 8 * D + FF].astype(jnp.float32),
        part_of(vecs, 7),
    )
    output = (result * keep[..., None]).astype(jnp.bfloat16)
    return (output, (inputs, allowed, middle, saved_self, saved_mlp))


def encode_back(saved, keep, mats, vecs, grad_out):
    inputs, allowed, middle, saved_self, saved_mlp = saved
    grad_result = grad_out.astype(jnp.float32) * keep[..., None]
    grad_middle, mats_mlp, vecs_mlp = mlp_block_back(
        middle,
        mats[4 * D : 4 * D + FF],
        mats[4 * D + FF :],
        part_of(vecs, 5),
        part_of(vecs, 6),
        saved_mlp,
        grad_result,
    )
    grad_inputs, mats_self, vecs_self = self_block_back(
        inputs, allowed, mats, vecs, saved_self, grad_middle
    )
    return (grad_inputs, mats_self + mats_mlp, vecs_self + vecs_mlp)


def decode(text_mb, image_rows, keep, length, mats, vecs):
    inputs = text_mb.astype(jnp.float32)
    positions = jnp.arange(inputs.shape[1])
    causal = (positions[None, :] <= positions[:, None])[None, None] & (
        positions[None, None, None, :] < length[:, None, None, None]
    )
    crossing = (keep > 0.5)[:, None, None, :]
    after_self, saved_self = self_block(inputs, causal, mats, vecs)
    after_cross, saved_cross = cross_block(after_self, image_rows, crossing, mats, vecs)
    result, saved_mlp = mlp_block(
        after_cross,
        mats[8 * D : 8 * D + FF],
        mats[8 * D + FF :],
        part_of(vecs, 10),
        part_of(vecs, 11),
        vecs[13 * D : 13 * D + FF].astype(jnp.float32),
        part_of(vecs, 12),
    )
    return (
        result.astype(jnp.bfloat16),
        (
            inputs,
            image_rows,
            causal,
            crossing,
            after_self,
            after_cross,
            saved_self,
            saved_cross,
            saved_mlp,
        ),
    )


def decode_back(saved, mats, vecs, grad_out):
    (
        inputs,
        image_rows,
        causal,
        crossing,
        after_self,
        after_cross,
        saved_self,
        saved_cross,
        saved_mlp,
    ) = saved
    grad_result = grad_out.astype(jnp.float32)
    grad_cross, mats_mlp, vecs_mlp = mlp_block_back(
        after_cross,
        mats[8 * D : 8 * D + FF],
        mats[8 * D + FF :],
        part_of(vecs, 10),
        part_of(vecs, 11),
        saved_mlp,
        grad_result,
    )
    grad_self, grad_image, mats_cross, vecs_cross = cross_block_back(
        after_self, image_rows, crossing, mats, vecs, saved_cross, grad_cross
    )
    grad_inputs, mats_self, vecs_self = self_block_back(
        inputs, causal, mats, vecs, saved_self, grad_self
    )
    return (
        grad_inputs,
        grad_image,
        mats_self + mats_cross + mats_mlp,
        vecs_self + vecs_cross + vecs_mlp,
    )


def body_plain(images, text, enc_mats, enc_vecs, dec_mats, dec_vecs, tissue, text_len, enc_cot, dec_cot):
    first = lax.axis_index("section") == 0
    shards = lax.axis_size("dp")
    img_count, slots = tissue.shape
    batch = img_count // MICRO
    text_rows = text.shape[0] // img_count
    enc_rows, dec_rows = (enc_mats.shape[0], dec_mats.shape[0])
    enc_len, dec_len = (enc_vecs.shape[0], dec_vecs.shape[0])
    keep_all = tissue.astype(jnp.float32).reshape(MICRO, batch, slots)
    image_in = images.reshape(MICRO, batch, slots, D)
    text_in = text.reshape(MICRO, batch, text_rows, D)
    length_in = text_len.reshape(MICRO, batch)
    image_cot = enc_cot.reshape(MICRO, batch, slots, D)
    text_cot = dec_cot.reshape(MICRO, batch, text_rows, D)

    def enc_view(weights):
        mats_part = (
            weights[0].reshape(shards, dec_rows, D)[:, :enc_rows].reshape(shards * enc_rows, D)
        )
        vecs_part = weights[1].reshape(shards, dec_len)[:, :enc_len].reshape(shards * enc_len)
        return (mats_part, vecs_part)

    def dec_view(weights):
        return (weights[0], weights[1])

    def to_padded(grad_mats, grad_vecs):
        mats_part = jnp.pad(
            grad_mats.reshape(shards, enc_rows, D), ((0, 0), (0, dec_rows - enc_rows), (0, 0))
        )
        vecs_part = jnp.pad(grad_vecs.reshape(shards, enc_len), ((0, 0), (0, dec_len - enc_len)))
        return (mats_part.reshape(shards * dec_rows, D), vecs_part.reshape(shards * dec_len))

    mats_pad = jnp.pad(enc_mats, ((0, dec_rows - enc_rows), (0, 0)))
    vecs_pad = jnp.pad(enc_vecs, (0, dec_len - enc_len))
    own_mats = jnp.where(first, mats_pad, dec_mats)
    own_vecs = jnp.where(first, vecs_pad, dec_vecs)
    weights = (
        lax.all_gather(own_mats, "dp", axis=0, tiled=True),
        lax.all_gather(own_vecs, "dp", axis=0, tiled=True),
    )
    zero_image = jnp.zeros((batch, slots, D), jnp.bfloat16)
    zero_text = jnp.zeros((batch, text_rows, D), jnp.bfloat16)
    encoded = [zero_image] * MICRO
    decoded = [zero_text] * MICRO
    for tick in range(MICRO + 1):

        def forward_encoder_work():
            if tick < MICRO:
                mats_part, vecs_part = enc_view(weights)
                return (encode(image_in[tick], keep_all[tick], mats_part, vecs_part)[0], zero_text)
            return (zero_image, zero_text)

        def forward_decoder_work():
            if tick > 0:
                mats_part, vecs_part = dec_view(weights)
                made = decode(
                    text_in[tick - 1],
                    encoded[tick - 1],
                    keep_all[tick - 1],
                    length_in[tick - 1],
                    mats_part,
                    vecs_part,
                )[0]
                return (zero_image, made)
            return (zero_image, zero_text)

        made_image, made_text = lax.cond(first, forward_encoder_work, forward_decoder_work)
        if tick < MICRO:
            arrived = shifted(made_image, "section", 1)
            encoded[tick] = jnp.where(first, made_image, arrived)
        if tick > 0:
            decoded[tick - 1] = made_text
    back_weights = weights
    zero_image_grad = jnp.zeros((batch, slots, D), jnp.float32)
    zero_text_grad = jnp.zeros((batch, text_rows, D), jnp.float32)
    zero_mats = jnp.zeros((shards * dec_rows, D), jnp.float32)
    zero_vecs = jnp.zeros((shards * dec_len,), jnp.float32)
    returned = [zero_image] * MICRO
    image_grads = [zero_image_grad] * MICRO
    text_grads = [zero_text_grad] * MICRO
    total_mats, total_vecs = (zero_mats, zero_vecs)
    for tick in range(MICRO + 1):

        def backward_encoder_work():
            if tick > 0:
                index = MICRO - tick
                mats_part, vecs_part = enc_view(back_weights)
                _, saved = encode(image_in[index], keep_all[index], mats_part, vecs_part)
                grad_in, grad_mats, grad_vecs = encode_back(
                    saved, keep_all[index], mats_part, vecs_part, returned[index]
                )
                grad_mats, grad_vecs = to_padded(
                    jnp.concatenate(grad_mats, axis=0), jnp.concatenate(grad_vecs, axis=0)
                )
                return (zero_image, zero_text_grad, grad_in, grad_mats, grad_vecs)
            return (zero_image, zero_text_grad, zero_image_grad, zero_mats, zero_vecs)

        def backward_decoder_work():
            if tick < MICRO:
                index = MICRO - 1 - tick
                mats_part, vecs_part = dec_view(back_weights)
                _, saved = decode(
                    text_in[index],
                    encoded[index],
                    keep_all[index],
                    length_in[index],
                    mats_part,
                    vecs_part,
                )
                grad_text, grad_image, grad_mats, grad_vecs = decode_back(
                    saved, mats_part, vecs_part, text_cot[index]
                )
                grad_mats = jnp.concatenate(grad_mats, axis=0)
                grad_vecs = jnp.concatenate(grad_vecs, axis=0)
                outgoing = (grad_image + image_cot[index].astype(jnp.float32)).astype(jnp.bfloat16)
                return (outgoing, grad_text, zero_image_grad, grad_mats, grad_vecs)
            return (zero_image, zero_text_grad, zero_image_grad, zero_mats, zero_vecs)

        outgoing, grad_text, grad_in, grad_mats, grad_vecs = lax.cond(
            first, backward_encoder_work, backward_decoder_work
        )
        if tick == 0:
            total_mats, total_vecs = (grad_mats, grad_vecs)
        else:
            total_mats = total_mats + grad_mats
            total_vecs = total_vecs + grad_vecs
        if tick < MICRO:
            returned[MICRO - 1 - tick] = shifted(outgoing, "section", -1)
            text_grads[MICRO - 1 - tick] = grad_text
        if tick > 0:
            image_grads[MICRO - tick] = grad_in
    shard_mats, shard_vecs = (
        lax.psum_scatter(total_mats, "dp", scatter_dimension=0, tiled=True),
        lax.psum_scatter(total_vecs, "dp", scatter_dimension=0, tiled=True),
    )
    image_grad_all = jnp.concatenate(image_grads, axis=0).reshape(-1, D)
    text_grad_all = jnp.concatenate(text_grads, axis=0).reshape(-1, D)
    decoded_all = jnp.concatenate(decoded, axis=0).reshape(-1, D).astype(jnp.float32)
    enc_mats_own = jnp.where(first, shard_mats[:enc_rows], 0.0)
    enc_vecs_own = jnp.where(first, shard_vecs[:enc_len], 0.0)
    dec_mats_own = jnp.where(first, 0.0, shard_mats)
    dec_vecs_own = jnp.where(first, 0.0, shard_vecs)
    image_own = jnp.where(first, image_grad_all, 0.0)
    decoded_own = jnp.where(first, 0.0, decoded_all)
    text_own = jnp.where(first, 0.0, text_grad_all)
    combined = (
        lax.psum(enc_mats_own.astype(jnp.bfloat16), "section").astype(jnp.float32),
        lax.psum(enc_vecs_own.astype(jnp.bfloat16), "section").astype(jnp.float32),
        lax.psum(dec_mats_own.astype(jnp.bfloat16), "section").astype(jnp.float32),
        lax.psum(dec_vecs_own.astype(jnp.bfloat16), "section").astype(jnp.float32),
        lax.psum(image_own.astype(jnp.bfloat16), "section").astype(jnp.float32),
        lax.psum(decoded_own.astype(jnp.bfloat16), "section").astype(jnp.float32),
        lax.psum(text_own.astype(jnp.bfloat16), "section").astype(jnp.float32),
    )
    enc_mats_grad, enc_vecs_grad, dec_mats_grad, dec_vecs_grad, image_grad, dec_full, text_grad = (
        combined
    )
    dec_out = dec_full.astype(jnp.bfloat16)
    enc_out = jnp.concatenate(encoded, axis=0).reshape(-1, D)
    return (
        enc_out,
        dec_out,
        image_grad,
        text_grad,
        enc_mats_grad,
        enc_vecs_grad,
        dec_mats_grad,
        dec_vecs_grad,
    )


MESH = pl.DeviceIdType.MESH
TILE = 16
ADD_ROWS = 32


def grid_of(shards):
    return (shards // 4, 2, 2)


def split_rows(rows, late):
    part = int(rows * late / 2) // TILE * TILE
    first = (rows - 2 * part) // 2 // TILE * TILE
    sizes = (first, rows - 2 * part - first, part, part)
    starts = (0, first, rows - 2 * part, rows - part)
    return tuple(zip(starts, sizes))


class Place:
    def __init__(self, depth):
        self.section = lax.axis_index("section")
        self.me = lax.axis_index("dp")
        self.depth = depth
        self.z = lax.div(self.me, 4)
        self.y = lax.rem(lax.div(self.me, 2), 2)
        self.x = lax.rem(self.me, 2)

    def shard(self, z, y, x):
        return (z * 2 + y) * 2 + x

    def pair(self, first_x, z, first, second):
        return self.shard(z, second, first) if first_x else self.shard(z, first, second)

    def own(self, first_x):
        return (self.x, self.y) if first_x else (self.y, self.x)


class Copies:
    def __init__(self, place, waiting=False):
        self.place = place
        self.waiting = waiting

    def start(self, cond, src, dst, send_sem, recv_sem, dp, section=None):
        section = self.place.section if section is None else section

        def act():
            copy = pltpu.make_async_remote_copy(
                src_ref=src,
                dst_ref=dst,
                send_sem=send_sem,
                recv_sem=recv_sem,
                device_id=(section, dp),
                device_id_type=MESH,
            )
            if self.waiting:
                copy.wait_send()
            else:
                copy.start()

        if cond is None:
            act()
        else:
            pl.when(cond)(act)

    def arrived(self, dst, send_sem, recv_sem):
        if self.waiting:
            return
        pltpu.make_async_remote_copy(
            src_ref=dst,
            dst_ref=dst,
            send_sem=send_sem,
            recv_sem=recv_sem,
            device_id=(self.place.section, self.place.me),
            device_id_type=MESH,
        ).wait_recv()


def guarded(cond, step, *args):
    if cond is None:
        step(*args)
    else:
        pl.when(cond)(functools.partial(step, *args))


def greet(place, shards, both):
    barrier = pltpu.get_barrier_semaphore()
    for step in range(1, shards):
        pl.semaphore_signal(
            barrier,
            inc=1,
            device_id=(place.section, lax.rem(place.me + step, shards)),
            device_id_type=MESH,
        )
    if both:
        pl.semaphore_signal(
            barrier, inc=1, device_id=(1 - place.section, place.me), device_id_type=MESH
        )
    pl.semaphore_wait(barrier, shards - 1 + int(both))


class Gather:
    def __init__(self, copies, place, depth, rows, cuts, w, send_sems, recv_sems, gate):
        self.copies = copies
        self.gate = gate
        self.place = place
        self.depth = depth
        self.rows = rows
        self.cuts = cuts
        self.w = w
        self.send_sems = send_sems
        self.recv_sems = recv_sems
        self.late = (2, 3) if cuts[2][1] else ()

    def piece(self, cls, shard):
        start, size = self.cuts[cls]
        return self.w.at[pl.ds(pl.multiple_of(shard * self.rows + start, TILE), size)]

    def send(self, cls, shard, way, dp):
        piece = self.piece(cls, shard)
        self.copies.start(
            None, piece, piece, self.send_sems.at[cls, shard, way], self.recv_sems.at[cls, shard], dp
        )

    def arrived(self, cls, shard):
        self.copies.arrived(
            self.piece(cls, shard), self.send_sems.at[cls, shard, 0], self.recv_sems.at[cls, shard]
        )

    def along(self, plane, distance, act):
        z, last = self.place.z, self.depth - 1
        if distance == 0:
            pl.when(z == plane)(lambda: act(plane, plane < last, plane > 0))
            return
        if plane + distance <= last:
            pl.when(z == plane + distance)(
                lambda: act(plane + distance, plane + distance < last, False)
            )
        if plane - distance >= 0:
            pl.when(z == plane - distance)(
                lambda: act(plane - distance, False, plane - distance > 0)
            )

    def L(self, plane, distance):
        place = self.place

        def act(at, up, down):
            shard = place.shard(plane, place.y, place.x)
            for cls in (0, 1):
                a, b = place.own(cls == 0)
                if distance:
                    self.arrived(cls, shard)
                if up:
                    self.send(cls, shard, 0, place.me + 4)
                if down:
                    self.send(cls, shard, 1, place.me - 4)
                self.send(cls, shard, 2, place.pair(cls == 0, at, 1 - a, b))

        self.along(plane, distance, act)

    def G(self, plane, distance):
        place = self.place

        def act(at, up, down):
            for cls in (0, 1):
                a, b = place.own(cls == 0)
                other = place.pair(cls == 0, plane, 1 - a, b)
                self.arrived(cls, other)
                to = place.pair(cls == 0, at, a, 1 - b)
                self.send(cls, place.shard(plane, place.y, place.x), 3, to)
                self.send(cls, other, 3, to)

        self.along(plane, distance, act)

    def H(self, plane):
        place = self.place
        for cls in (0, 1):
            a, b = place.own(cls == 0)
            self.arrived(cls, place.pair(cls == 0, plane, a, 1 - b))
            self.arrived(cls, place.pair(cls == 0, plane, 1 - a, 1 - b))

    def drain(self):
        place = self.place
        z, last = place.z, self.depth - 1

        def left(cls, shard, way):
            piece = self.piece(cls, shard)
            pltpu.make_async_remote_copy(
                src_ref=piece,
                dst_ref=piece,
                send_sem=self.send_sems.at[cls, shard, way],
                recv_sem=self.recv_sems.at[cls, shard],
                device_id=(place.section, place.me),
                device_id_type=MESH,
            ).wait_send()

        for cls in (0, 1) + self.late:
            first_x = cls in (0, 2)
            a, b = place.own(first_x)
            early = cls < 2

            def in_plane(plane):
                own = place.shard(plane, place.y, place.x)
                left(cls, own, 2)
                left(cls, own, 3)
                left(cls, place.pair(first_x, plane, 1 - a, b), 3)

            def along(plane, way):
                if early:
                    left(cls, place.shard(plane, place.y, place.x), way)
                else:
                    pl.loop(0, 4)(lambda index: left(cls, plane * 4 + index, way))

            @pl.loop(0, self.depth)
            def _(plane):
                if early:
                    in_plane(plane)
                pl.when((z >= plane) & (z < last))(lambda: along(plane, 0))
                pl.when((z <= plane) & (z > 0))(lambda: along(plane, 1))

            if not early:
                in_plane(z)

    def X(self):
        if not self.copies.waiting:
            self.gate()

    def M(self):
        place = self.place
        for cls in self.late:
            a, b = place.own(cls == 2)
            self.send(cls, place.me, 2, place.pair(cls == 2, place.z, 1 - a, b))

    def N(self):
        place = self.place
        for cls in self.late:
            a, b = place.own(cls == 2)
            other = place.pair(cls == 2, place.z, 1 - a, b)
            self.arrived(cls, other)
            to = place.pair(cls == 2, place.z, a, 1 - b)
            self.send(cls, place.me, 3, to)
            self.send(cls, other, 3, to)

    def T(self, plane, distance):
        place = self.place

        def act(at, up, down):
            for cls in self.late:
                a, b = place.own(cls == 2)
                if distance == 0:
                    self.arrived(cls, place.pair(cls == 2, plane, a, 1 - b))
                    self.arrived(cls, place.pair(cls == 2, plane, 1 - a, 1 - b))
                for index in range(4):
                    shard = plane * 4 + index
                    if distance:
                        self.arrived(cls, shard)
                    if up:
                        self.send(cls, shard, 0, place.me + 4)
                    if down:
                        self.send(cls, shard, 1, place.me - 4)

        self.along(plane, distance, act)


def add_rows(total, total_start, part, part_start, size):
    step = next(n for n in (64, 48, 32, TILE) if size % n == 0)

    @pl.loop(0, size // step)
    def _(index):
        at = pl.ds(pl.multiple_of(total_start + index * step, TILE), step)
        of = pl.ds(pl.multiple_of(part_start + index * step, TILE), step)
        total[at] = total[at] + part[of]


class Scatter:
    def __init__(self, copies, place, depth, rows, cuts, g, land, send_sems, recv_sems, done):
        self.copies = copies
        self.done = done
        self.place = place
        self.depth = depth
        self.rows = rows
        self.cuts = cuts
        self.g = g
        self.land = land
        self.send_sems = send_sems
        self.recv_sems = recv_sems
        self.late = (2, 3) if cuts[2][1] else ()
        self.early_slots = 4 * depth + 1
        self.late_slots = 4 * depth + 7

    @staticmethod
    def land_rows(depth, cuts):
        early = (4 * depth + 1) * (cuts[0][1] + cuts[1][1])
        return early + (4 * depth + 7) * (cuts[2][1] + cuts[3][1])

    def start_of(self, cls, shard):
        return pl.multiple_of(shard * self.rows + self.cuts[cls][0], TILE)

    def slot_start(self, cls, slot):
        base = 0
        for other in range(cls):
            base += (self.early_slots if other < 2 else self.late_slots) * self.cuts[other][1]
        return base + slot * self.cuts[cls][1]

    def slot_ref(self, cls, slot):
        return self.land.at[pl.ds(self.slot_start(cls, slot), self.cuts[cls][1])]

    def send(self, cls, shard, slot, dp):
        self.copies.start(
            None,
            self.g.at[pl.ds(self.start_of(cls, shard), self.cuts[cls][1])],
            self.slot_ref(cls, slot),
            self.send_sems.at[cls, slot],
            self.recv_sems.at[cls, slot],
            dp,
        )

    def take(self, cls, shard, slot):
        if self.copies.waiting:
            return
        self.copies.arrived(
            self.slot_ref(cls, slot), self.send_sems.at[cls, slot], self.recv_sems.at[cls, slot]
        )
        add_rows(
            self.g,
            self.start_of(cls, shard),
            self.land,
            self.slot_start(cls, slot),
            self.cuts[cls][1],
        )

    def drain(self):
        z, depth = self.place.z, self.depth

        def left(cls, slot):
            piece = self.slot_ref(cls, slot)
            pltpu.make_async_remote_copy(
                src_ref=piece,
                dst_ref=piece,
                send_sem=self.send_sems.at[cls, slot],
                recv_sem=self.recv_sems.at[cls, slot],
                device_id=(self.place.section, self.place.me),
                device_id_type=MESH,
            ).wait_send()

        for cls in (0, 1):
            pl.loop(0, 3 * depth)(lambda slot: left(cls, slot))

            @pl.loop(0, depth)
            def _(plane):
                pl.when(z == plane + 1)(lambda: left(cls, 4 * depth))
                pl.when((z > plane + 1) | (z < plane))(lambda: left(cls, 3 * depth + plane))

        for cls in self.late:

            @pl.loop(0, 4 * depth)
            def _(index):
                plane, piece = lax.div(index, 4), lax.rem(index, 4)
                pl.when(z == plane + 1)(lambda: left(cls, 4 * depth + piece))
                pl.when((z > plane + 1) | (z < plane))(lambda: left(cls, index))

            pl.loop(0, 3)(lambda hop: left(cls, 4 * depth + 4 + hop))

    def A(self, plane):
        place = self.place
        for cls in (0, 1):
            first_x = cls == 0
            a, b = place.own(first_x)
            to = place.pair(first_x, place.z, 1 - a, b)
            self.send(cls, place.pair(first_x, plane, 1 - a, 1 - b), plane * 3, to)
            self.send(cls, place.pair(first_x, plane, 1 - a, b), plane * 3 + 1, to)

    def B(self, plane):
        place = self.place
        for cls in (0, 1):
            first_x = cls == 0
            a, b = place.own(first_x)
            away = place.pair(first_x, plane, a, 1 - b)
            self.take(cls, away, plane * 3)
            self.send(cls, away, plane * 3 + 2, place.pair(first_x, place.z, a, 1 - b))
        for cls in (0, 1):
            first_x = cls == 0
            a, b = place.own(first_x)
            self.take(cls, place.pair(first_x, plane, a, b), plane * 3 + 1)

    def P(self, plane):
        place = self.place
        for cls in (0, 1):
            self.take(cls, place.shard(plane, place.y, place.x), plane * 3 + 2)

    def hop(self, plane, number, act):
        z = self.place.z
        low, high = number - 1, self.depth - number
        if low < plane:
            pl.when(z == low)(lambda: act(1, low + 1 == plane))
        if high > plane:
            pl.when(z == high)(lambda: act(-1, high - 1 == plane))

    def Z(self, plane, number):
        place = self.place
        slot = 3 * self.depth + plane

        def act(way, ends):
            shard = place.shard(plane, place.y, place.x)
            for cls in (0, 1):
                if number > 1:
                    self.take(cls, shard, slot)
                to = 4 * self.depth if ends and way < 0 else slot
                self.send(cls, shard, to, place.me + 4 * way)

        self.hop(plane, number, act)

    def E(self, plane):
        place = self.place

        @pl.when(place.z == plane)
        def _():
            shard = place.shard(plane, place.y, place.x)
            for cls in (0, 1):
                if plane > 0:
                    self.take(cls, shard, 3 * self.depth + plane)
                if plane < self.depth - 1:
                    self.take(cls, shard, 4 * self.depth)
                if not self.copies.waiting:
                    self.done(cls)

    def Q(self, plane, number):
        place = self.place

        def act(way, ends):
            for cls in self.late:
                for index in range(4):
                    slot = plane * 4 + index
                    if number > 1:
                        self.take(cls, slot, slot)
                    to = 4 * self.depth + index if ends and way < 0 else slot
                    self.send(cls, slot, to, place.me + 4 * way)

        self.hop(plane, number, act)

    def R(self, plane):
        place = self.place
        base = 4 * self.depth + 4

        @pl.when(place.z == plane)
        def _():
            for cls in self.late:
                for index in range(4):
                    slot = plane * 4 + index
                    if plane > 0:
                        self.take(cls, slot, slot)
                    if plane < self.depth - 1:
                        self.take(cls, slot, 4 * self.depth + index)
                first_x = cls == 2
                a, b = place.own(first_x)
                to = place.pair(first_x, plane, 1 - a, b)
                self.send(cls, place.pair(first_x, plane, 1 - a, 1 - b), base, to)
                self.send(cls, place.pair(first_x, plane, 1 - a, b), base + 1, to)

    def S(self, plane):
        place = self.place
        base = 4 * self.depth + 4

        @pl.when(place.z == plane)
        def _():
            for cls in self.late:
                first_x = cls == 2
                a, b = place.own(first_x)
                away = place.pair(first_x, plane, a, 1 - b)
                self.take(cls, away, base)
                self.send(cls, away, base + 2, place.pair(first_x, plane, a, 1 - b))
            for cls in self.late:
                a, b = place.own(cls == 2)
                self.take(cls, place.pair(cls == 2, plane, a, b), base + 1)
            for cls in self.late:
                self.take(cls, place.me, base + 2)
                if not self.copies.waiting:
                    self.done(cls)


STEPS = "CLGHMNTABPZEQRSX"


def run_plan(steps, copies, stages):
    for step in steps:
        if step < 100:
            stages[step]()
            continue
        kind, plane, hop = step // 100, step // 10 % 10, step % 10
        act = getattr(copies, STEPS[kind])
        if STEPS[kind] in "LGTZQ":
            act(plane, hop)
        elif STEPS[kind] in "MNX":
            act()
        else:
            act(plane)


BLOCK = 256
LINES = 32
NORM_ROWS = 64
UNROLL = 3
ATTEND_UNROLL = 2
PAIRS = D // 128
VEC_UNIT = 48
VEC_ROWS = 32
F32 = jnp.float32
BF16 = jnp.bfloat16


def dot_nn(left, right):
    return lax.dot_general(left, right, (((1,), (0,)), ((), ())), preferred_element_type=F32)


def dot_nt(left, right):
    return lax.dot_general(left, right, (((1,), (1,)), ((), ())), preferred_element_type=F32)


def dot_tn(left, right):
    return lax.dot_general(left, right, (((0,), (0,)), ((), ())), preferred_element_type=F32)


def chunk(start, size=BLOCK):
    if isinstance(start, int):
        return pl.ds(start, size)
    return pl.ds(pl.multiple_of(start, 128 if size % 128 == 0 else TILE), size)


def iota(shape, dim):
    return lax.broadcasted_iota(jnp.int32, shape, dim)


def unit_of(column):
    return lax.shift_right_logical(column * 1366, 16)


def unit_spread():
    column = iota((128, D), 1)
    return (column - VEC_UNIT * unit_of(column) == iota((128, D), 0)).astype(BF16)


def vec_gathered(tiles, per):
    shards = tiles.shape[0]
    count = shards * VEC_ROWS
    spread = dot_nn(tiles[...].reshape(count, 128), unit_spread())
    row = iota((count, D), 0)
    inner = row & (VEC_ROWS - 1)
    unit = lax.shift_right_logical(row, 5) * per + inner
    mask = ((unit & 15) == unit_of(iota((count, D), 1))) & (inner < per)
    spread = jnp.where(mask, spread, 0.0).astype(BF16)
    row = iota((VEC_ROWS, count), 1)
    inner = row & (VEC_ROWS - 1)
    unit = lax.shift_right_logical(row, 5) * per + inner
    pick = (lax.shift_right_logical(unit, 4) == iota((VEC_ROWS, count), 0)) & (inner < per)
    return dot_nn(pick.astype(F32).astype(BF16), spread)


def exact_dot(pick, values, dot):
    high = values.astype(BF16)
    rest = values - high.astype(F32)
    middle = rest.astype(BF16)
    low = (rest - middle.astype(F32)).astype(BF16)
    return dot(pick, high) + dot(pick, middle) + dot(pick, low)


def vec_shard(rows, me, per):
    unit = me * per + iota((VEC_ROWS, VEC_ROWS), 0)
    pick = (lax.shift_right_logical(unit, 4) == iota((VEC_ROWS, VEC_ROWS), 1)).astype(F32)
    lines = exact_dot(pick.astype(BF16), rows, dot_nn)
    unit = me * per + iota((VEC_ROWS, D), 0)
    mask = (unit & 15) == unit_of(iota((VEC_ROWS, D), 1))
    lines = jnp.where(mask, lines, 0.0)
    spread = unit_spread()
    return exact_dot(spread, lines, lambda pick, part: dot_nt(part, pick))


def in_line(tile):
    group = 8 * VEC_UNIT
    column = iota((128, group), 1)
    pick = (column - VEC_UNIT * unit_of(column) == iota((128, group), 0)).astype(F32)
    spread = exact_dot(pick.astype(BF16), tile, lambda pick, part: dot_nn(part, pick))
    mask = (iota((VEC_ROWS, group), 0) & 7) == unit_of(iota((VEC_ROWS, group), 1))
    spread = jnp.where(mask, spread, 0.0)
    gather = lax.shift_right_logical(iota((8, VEC_ROWS), 1), 3) == iota((8, VEC_ROWS), 0)
    lines = exact_dot(gather.astype(F32).astype(BF16), spread, dot_nn)
    rows = [lines[row // 3 : row // 3 + 1, row % 3 * 128 : row % 3 * 128 + 128] for row in range(8)]
    return jnp.concatenate(rows, axis=0)


class Compute:
    def __init__(self, w, vrows, gvec, red):
        self.w = w
        self.vrows = vrows
        self.gvec = gvec
        self.red = red

    def vec(self, index):
        return self.vrows[pl.ds(index, 1), :]

    def norm(self, src, src_row, dst, dst_row, rows, gain, shift, unit, unit_row, rate, rate_row):
        scale_vec, shift_vec = self.vec(gain), self.vec(shift)

        @pl.loop(0, rows // NORM_ROWS)
        def _(index):
            x = src[chunk(src_row + index * NORM_ROWS, NORM_ROWS), :].astype(F32)
            centre = x - jnp.mean(x, axis=-1, keepdims=True)
            spread = jnp.mean(centre * centre, axis=-1, keepdims=True)
            scale = lax.rsqrt(spread + 1e-06)
            even = centre * scale
            result = even * scale_vec + shift_vec
            dst[chunk(dst_row + index * NORM_ROWS, NORM_ROWS), :] = result.astype(BF16)
            if unit is not None:
                unit[chunk(unit_row + index * NORM_ROWS, NORM_ROWS), :] = even.astype(unit.dtype)
            rate[chunk(rate_row + index * NORM_ROWS, NORM_ROWS), :] = jnp.broadcast_to(
                scale, (NORM_ROWS, 128)
            )

    def unit_rows(self, src, rows):
        @pl.loop(0, rows // NORM_ROWS)
        def _(index):
            at = chunk(index * NORM_ROWS, NORM_ROWS)
            x = src[at, :].astype(F32)
            centre = x - jnp.mean(x, axis=-1, keepdims=True)
            spread = jnp.mean(centre * centre, axis=-1, keepdims=True)
            src[at, :] = (centre * lax.rsqrt(spread + 1e-06)).astype(src.dtype)

    def norm_back(
        self, unit, unit_row, rate, rate_row, grad, rest, out, low, rows, gain, shift
    ):
        scale_vec = self.vec(gain)
        self.red[...] = jnp.zeros_like(self.red)

        @pl.loop(0, rows // NORM_ROWS)
        def _(index):
            at = chunk(index * NORM_ROWS, NORM_ROWS)
            even = unit[chunk(unit_row + index * NORM_ROWS, NORM_ROWS), :].astype(F32)
            scale = rate[chunk(rate_row + index * NORM_ROWS, NORM_ROWS), 0:1]
            d = grad[at, :]
            along = d * even
            self.red[0] += jnp.sum(along.reshape(NORM_ROWS // 8, 8, D), axis=0)
            self.red[1] += jnp.sum(d.reshape(NORM_ROWS // 8, 8, D), axis=0)
            d = d * scale_vec
            mean = jnp.mean(d, axis=-1, keepdims=True)
            along = jnp.mean(along * scale_vec, axis=-1, keepdims=True)
            total = rest[at, :].astype(F32) + scale * (d - mean - even * along)
            if out is not None:
                out[at, :] = total
            if low is not None:
                low[at, :] = total.astype(BF16)

        self.gvec[pl.ds(gain, 1), :] = jnp.sum(self.red[0], axis=0, keepdims=True)
        self.gvec[pl.ds(shift, 1), :] = jnp.sum(self.red[1], axis=0, keepdims=True)

    def row_sum(self, values):
        ones = jnp.ones((TILE, values.shape[0]), BF16)
        return dot_nn(ones, values)[0:1]

    def linear(self, src, row, rows, index, bias, emit):
        @pl.loop(0, D // BLOCK, unroll=UNROLL)
        def _(part):
            cols = chunk(part * BLOCK)
            made = dot_nn(src[pl.ds(row, rows), :], self.w[chunk(index * D, D), cols])
            if bias is not None:
                made = made + self.vrows[pl.ds(bias, 1), cols]
            emit(cols, made)

    def linear_back(self, pairs, emit):
        @pl.loop(0, D // BLOCK, unroll=UNROLL)
        def _(part):
            total = None
            for grad, index in pairs:
                made = dot_nt(grad(), self.w[chunk(index * D + part * BLOCK), :])
                total = made if total is None else total + made
            emit(chunk(part * BLOCK), total)

    def weight_grad(self, left, right, index, parts=D // BLOCK):
        @pl.loop(0, parts, unroll=UNROLL)
        def _(part):
            total = None
            for one, other in zip(left(part), right):
                made = dot_tn(one, other())
                total = made if total is None else total + made
            self.w[chunk(index * D + part * BLOCK), :] = total.astype(BF16)

    def hidden(self, src, row, rows, first, bias, act, slope, pieces=(0, FF // D)):
        each = D // BLOCK

        @pl.loop(pieces[0] * each, pieces[1] * each, unroll=UNROLL)
        def _(part):
            piece = lax.div(part, each)
            u = dot_nt(src[pl.ds(row, rows), :], self.w[chunk(first * D + part * BLOCK), :])
            u = u + self.vrows[pl.ds(bias + piece, 1), chunk(lax.rem(part, each) * BLOCK)]
            square = u * u
            t = jnp.tanh(u * (0.7978845608028654 + 0.035677408136300125 * square))
            half = 0.5 + 0.5 * t
            at = (pl.ds(0, rows), chunk(part * BLOCK))
            made = u * half
            act[at] = made.astype(BF16)
            rise = 1.5957691216057308 + 0.21406444881780074 * square
            slope[at] = (half + made * (1.0 - half) * rise).astype(BF16)

    def project(self, act, rows, first, emit):
        @pl.loop(0, D // BLOCK)
        def _(part):
            cols = chunk(part * BLOCK)
            emit(cols, dot_nn(act[pl.ds(0, rows), :], self.w[chunk(first * D, FF), cols]))

    def hidden_back(self, low, rows, first, slope):
        @pl.loop(0, FF // BLOCK, unroll=UNROLL)
        def _(part):
            made = dot_nt(low[pl.ds(0, rows), :], self.w[chunk(first * D + part * BLOCK), :])
            at = (pl.ds(0, rows), chunk(part * BLOCK))
            slope[at] = (made * slope[at].astype(F32)).astype(BF16)

    def wide_grad(self, left, rows, right, first):
        self.weight_grad(
            lambda part: [left[pl.ds(0, rows), chunk(part * BLOCK)]], [right], first, FF // BLOCK
        )

    def wide_sums(self, slope, rows, bias):
        for piece in range(FF // D):
            self.gvec[pl.ds(bias + piece, 1), :] = self.row_sum(
                slope[pl.ds(0, rows), pl.ds(piece * D, D)]
            )

    @staticmethod
    def halves(tile, scale=1.0):
        low = jnp.where(iota(tile.shape, 1) < HEAD, scale, 0.0).astype(BF16)
        high = jnp.where(iota(tile.shape, 1) < HEAD, 0.0, scale).astype(BF16)
        return tile * low, tile * high

    def attend(self, allowed, q_at, k_at, v_at, p_at, o_at):
        @pl.loop(0, PAIRS, unroll=ATTEND_UNROLL)
        def _(pair):
            keys = k_at(pair)[...]
            values = v_at(pair)[...].T
            mixed = []
            for half, queries in enumerate(self.halves(q_at(pair)[...], 0.125)):
                scores = jnp.where(allowed, dot_nt(keys, queries), -1000000000.0)
                expd = jnp.exp(scores - jnp.max(scores, axis=0, keepdims=True))
                rate = 1.0 / jnp.sum(expd, axis=0, keepdims=True)
                probs = (expd * rate).astype(BF16)
                p_at(pair, half)[...] = probs
                mixed.append(dot_nn(values, probs)[half * HEAD : (half + 1) * HEAD])
            o_at(pair)[...] = jnp.concatenate(mixed, axis=0).T.astype(BF16)

    def attend_back(self, q_at, k_at, v_at, p_at, do_at):
        @pl.loop(0, PAIRS, unroll=ATTEND_UNROLL)
        def _(pair):
            keys = k_at(pair)[...].T
            values = v_at(pair)[...]
            grad_q, grad_k, grad_v = [], 0.0, 0.0
            both = zip(self.halves(q_at(pair)[...], 0.125), self.halves(do_at(pair)[...]))
            for half, (queries, grads) in enumerate(both):
                low = p_at(pair, half)[...]
                probs = low.astype(F32)
                grad_probs = dot_nt(values, grads)
                inner = jnp.sum(probs * grad_probs, axis=0, keepdims=True)
                grad_scores = (probs * (grad_probs - inner)).astype(BF16)
                grad_q.append(dot_nn(keys, grad_scores)[half * HEAD : (half + 1) * HEAD])
                grad_k = grad_k + dot_nn(grad_scores, queries)
                grad_v = grad_v + dot_nn(low, grads)
            q_at(pair)[...] = (jnp.concatenate(grad_q, axis=0) * 0.125).T.astype(BF16)
            k_at(pair)[...] = grad_k.astype(BF16)
            v_at(pair)[...] = grad_v.astype(BF16)


def store_to(ref, row, rows, col=0):
    def emit(cols, values):
        ref[pl.ds(row, rows), chunk(col + cols.start)] = values.astype(ref.dtype)

    return emit


def fused_kernel(
    depth,
    sizes,
    pers,
    slots,
    words,
    images_in,
    enc_cot,
    tissue,
    text_len,
    text_in,
    enc_in,
    dec_in,
    enc_tile,
    dec_tile,
    dec_cot,
    enc_out,
    dec_out,
    image_out,
    text_out,
    enc_g,
    dec_g,
    enc_v,
    dec_v,
    w,
    land,
    xin,
    n1,
    q,
    k,
    v,
    o,
    h,
    n2,
    act,
    gp,
    e,
    cot,
    acc,
    dh,
    low,
    dmix,
    keep_col,
    rates,
    tiles,
    vrows,
    gvec,
    vland,
    vout,
    red,
    load_sems,
    ag_send,
    ag_recv,
    vec_send,
    vec_recv,
    rs_send,
    rs_recv,
    sum_send,
    sum_recv,
    x_send,
    x_recv,
    out_local,
    out_send,
    out_recv,
    gate_sem,
):
    shards = depth * 4
    place = Place(depth)
    me, z = place.me, place.z
    section = place.section
    image_rows, text_rows = xin.shape[0], text_in.shape[0]
    images, used = tissue.shape
    comp = Compute(w, vrows, gvec, red)
    cuts = [split_rows(rows, LATE) for rows in sizes]

    def load(index, src, dst, waiting=False):
        copy = pltpu.make_async_copy(src, dst, load_sems.at[index])
        if waiting:
            copy.wait()
        else:
            copy.start()

    def own_rows(which):
        return w.at[pl.ds(pl.multiple_of(me * sizes[which], TILE), sizes[which])]

    def load_own(which, waiting):
        load(0, (enc_in, dec_in)[which], own_rows(which), waiting)
        load(1, (enc_tile, dec_tile)[which], tiles.at[me], waiting)

    def load_text(waiting):
        load(2, text_in, xin.at[pl.ds(0, text_rows)], waiting)
        load(3, dec_cot, low.at[pl.ds(0, text_rows)], waiting)

    for which in (0, 1):

        @pl.when(section == which)
        def _():
            load_own(which, False)
            if which == 1:
                load_text(False)

    greet(place, shards, True)

    def give_vecs(waiting):
        src = tiles.at[me]
        for step in range(1, shards):
            Copies(place, waiting).start(
                None, src, src, vec_send.at[step], vec_recv.at[me], lax.rem(me + step, shards)
            )

    def got_vecs():
        for step in range(1, shards):
            frm = lax.rem(me + step, shards)
            Copies(place).arrived(tiles.at[frm], vec_send.at[step], vec_recv.at[frm])

    def across(waiting, index, src, dst):
        Copies(place, waiting).start(
            None, src, dst, x_send.at[index], x_recv.at[index], me, 1 - section
        )

    def crossed(index, dst):
        Copies(place).arrived(dst, x_send.at[index], x_recv.at[index])

    def give(waiting, index, src, dst):
        local = pltpu.make_async_copy(src, dst, out_local.at[index])
        if waiting:
            local.wait()
        else:
            local.start()
        Copies(place, waiting).start(
            None, src, dst, out_send.at[index], out_recv.at[index], me, 1 - section
        )

    def got(index, dst):
        Copies(place).arrived(dst, out_send.at[index], out_recv.at[index])

    def share_sums(waiting, slot, to):
        Copies(place, waiting).start(
            None, gvec, vland.at[slot], sum_send.at[slot], sum_recv.at[slot], to
        )

    def got_sums(slot):
        Copies(place).arrived(vland.at[slot], sum_send.at[slot], sum_recv.at[slot])

    def open_gate():
        pl.semaphore_signal(
            gate_sem, inc=1, device_id=(1 - section, me), device_id_type=MESH
        )

    def pass_gate():
        pl.semaphore_wait(gate_sem, 1)

    flips = (place.shard(z, place.y, 1 - place.x), place.shard(z, 1 - place.y, place.x))

    def sum_stages(which):
        def along_x():
            share_sums(False, 0, flips[0])

        def along_y():
            got_sums(0)
            share_sums(True, 0, flips[0])
            gvec[...] = gvec[...] + vland[0]
            share_sums(False, 1, flips[1])

        def along_z():
            got_sums(1)
            share_sums(True, 1, flips[1])
            gvec[...] = gvec[...] + vland[1]
            for step in range(1, depth):
                share_sums(False, 1 + step, lax.rem(me + 4 * step, shards))

        def ended():
            summed = gvec[...]
            for step in range(1, depth):
                got_sums(1 + step)
                share_sums(True, 1 + step, lax.rem(me + 4 * step, shards))
                summed = summed + vland[1 + step]
            vout[...] = vec_shard(summed, me, pers[which])
            give(False, 6, vout, (enc_v, dec_v)[which])

        return {30: along_x, 31: along_y, 32: along_z, 33: ended}

    def gather(which, waiting=False):
        return Gather(
            Copies(place, waiting),
            place,
            depth,
            sizes[which],
            cuts[which],
            w,
            ag_send,
            ag_recv,
            open_gate if which == 0 else pass_gate,
        )

    def give_class(waiting, which, cls):
        start, size = cuts[which][cls]
        if size:
            src = w.at[pl.ds(pl.multiple_of(me * sizes[which] + start, TILE), size)]
            give(waiting, 2 + cls, src, (enc_g, dec_g)[which].at[pl.ds(start, size)])

    def got_class(which, cls):
        start, size = cuts[which][cls]
        if size:
            got(2 + cls, (enc_g, dec_g)[which].at[pl.ds(start, size)])

    def scatter(which, waiting=False):
        return Scatter(
            Copies(place, waiting),
            place,
            depth,
            sizes[which],
            cuts[which],
            w,
            land,
            rs_send,
            rs_recv,
            functools.partial(give_class, False, which),
        )

    def start_stage(which):
        got_vecs()
        vrows[...] = vec_gathered(tiles, pers[which])
        gvec[...] = jnp.zeros_like(gvec)

    def padded(src):
        row = iota((image_rows, src.shape[0]), 0)
        slot = row & (slots - 1)
        frm = lax.shift_right_logical(row, 8) * used + slot
        pick = (iota((image_rows, src.shape[0]), 1) == frm) & (slot < used)
        return dot_nn(pick.astype(F32).astype(BF16), src[...]).astype(BF16)

    def fill_keep():
        keep_col[...] = jnp.zeros_like(keep_col)
        for image in range(images):
            line = tissue[pl.ds(image, 1), :].astype(F32).astype(BF16)
            lines = jnp.broadcast_to(line, (TILE, used))
            keep_col[pl.ds(image * slots, used), :] = dot_tn(
                lines, jnp.full((TILE, 128), 1.0 / TILE, BF16)
            )

    def spread(column, wide):
        return jnp.concatenate([column] * (wide // 128), axis=1) > 0.5

    def section_program(which, make):
        stages = sum_stages(which)
        def gathered():
            gather(which).drain()
            give_vecs(True)

        made, last = make(gathered)
        stages.update(made)
        load_own(which, True)
        run_plan(GATHER_PLANS[which], gather(which), stages)
        run_plan(SCATTER_PLANS[which], scatter(which), stages)
        scatter(which).drain()
        for cls in range(4):
            give_class(True, which, cls)
        give(True, 6, vout, (enc_v, dec_v)[which])
        last()
        for cls in range(4):
            got_class(1 - which, cls)
        got(6, (enc_v, dec_v)[1 - which])

    def encoder(gathered):
        rows = image_rows
        every = pl.ds(0, rows)
        stages = {}

        def stage(number):
            def keep(step):
                stages[number] = step
                return step

            return keep

        spare = shards * sizes[0]

        def at(ref, image):
            return lambda pair: ref.at[pl.ds(image * slots, slots), chunk(pair * 128, 128)]

        def p_at(image):
            def of(pair, half):
                index = (image * PAIRS + pair) * 2 + half
                row = spare + lax.div(index, 3) * slots
                return w.at[chunk(row, slots), chunk(lax.rem(index, 3) * slots, slots)]

            return of

        stages[8] = lambda: give_vecs(False)

        @stage(0)
        def _():
            fill_keep()
            xin[...] = padded(images_in)
            start_stage(0)
            comp.norm(xin, 0, n1, 0, rows, 0, 1, None, 0, rates.at[0], 0)

        @stage(1)
        def _():
            comp.linear(n1, 0, rows, 0, 2, store_to(q, 0, rows))
            comp.linear(n1, 0, rows, 1, None, store_to(k, 0, rows))
            comp.linear(n1, 0, rows, 2, 3, store_to(v, 0, rows))

        @stage(2)
        def _():
            for image in range(images):
                allowed = spread(keep_col[pl.ds(image * slots, slots), :], slots)
                comp.attend(
                    allowed, at(q, image), at(k, image), at(v, image), p_at(image), at(o, image)
                )

        @stage(3)
        def _():
            def add_input(cols, values):
                h[every, cols] = xin[every, cols].astype(F32) + values

            comp.linear(o, 0, rows, 3, 4, add_input)
            comp.norm(h, 0, n2, 0, rows, 5, 6, dh, 0, rates.at[1], 0)

        @stage(4)
        def _():
            comp.hidden(n2, 0, rows, 4, 8, act, gp, (0, 2))

        @stage(5)
        def _():
            comp.hidden(n2, 0, rows, 4, 8, act, gp, (2, 4))

        @stage(6)
        def _():
            def add_middle(cols, values):
                keep = jnp.concatenate([keep_col[...]] * (BLOCK // 128), axis=1)
                made = h[every, cols] + values + vrows[pl.ds(7, 1), cols]
                e[every, cols] = (made * keep).astype(BF16)

            comp.project(act, rows, 8, add_middle)
            across(False, 0, e, e)
            load(5, e, enc_out)

        @stage(7)
        def _():
            gathered()

            comp.unit_rows(xin, rows)

        @stage(10)
        def _():
            crossed(1, cot)

            @pl.loop(0, rows // LINES)
            def _(index):
                some = chunk(index * LINES, LINES)
                low[some, :] = (cot[some, :].astype(F32) * keep_col[some, 0:1]).astype(BF16)

            gvec[pl.ds(7, 1), :] = comp.row_sum(low[...])

        @stage(11)
        def _():
            comp.hidden_back(low, rows, 8, gp)

        @stage(12)
        def _():
            comp.wide_grad(act, rows, lambda: low[...], 8)

        @stage(13)
        def _():
            comp.project(gp, rows, 4, store_to(acc, 0, rows))

        @stage(14)
        def _():
            comp.wide_sums(gp, rows, 8)
            comp.wide_grad(gp, rows, lambda: n2[...], 4)

        @stage(15)
        def _():
            comp.norm_back(dh, 0, rates.at[1], 0, acc, low, dh, low, rows, 5, 6)

        @stage(16)
        def _():
            comp.linear_back([(lambda: low[...], 3)], store_to(dmix, 0, rows))

        @stage(17)
        def _():
            gvec[pl.ds(4, 1), :] = comp.row_sum(low[...])
            comp.weight_grad(lambda part: [o[:, chunk(part * BLOCK)]], [lambda: low[...]], 3)

        def heads_back(image):
            comp.attend_back(
                at(q, image), at(k, image), at(v, image), p_at(image), at(dmix, image)
            )

        stages[18] = lambda: heads_back(0)
        stages[19] = lambda: [heads_back(image) for image in range(1, images)]

        @stage(20)
        def _():
            comp.linear_back(
                [(lambda: q[...], 0), (lambda: k[...], 1), (lambda: v[...], 2)],
                store_to(acc, 0, rows),
            )

        @stage(21)
        def _():
            gvec[pl.ds(2, 1), :] = comp.row_sum(q[...])
            gvec[pl.ds(3, 1), :] = comp.row_sum(v[...])
            for index, ref in enumerate((q, k, v)):
                comp.weight_grad(
                    lambda part: [n1[:, chunk(part * BLOCK)]], [lambda: ref[...]], index
                )

        @stage(22)
        def _():
            comp.norm_back(xin, 0, rates.at[0], 0, acc, dh, None, low, rows, 0, 1)
            give(False, 1, low, image_out)

        def last():
            across(True, 0, e, e)
            load(5, e, enc_out, True)
            give(True, 1, low, image_out)
            got(0, dec_out)
            got(1, text_out)

        return stages, last

    def decoder(gathered):
        half = text_rows
        lower, upper = pl.ds(0, half), pl.ds(half, half)
        stages = {}

        def stage(number):
            def keep(step):
                stages[number] = step
                return step

            return keep

        def at(ref, image, base=0):
            return lambda pair: ref.at[
                pl.ds(base + image * words, words), chunk(pair * 128, 128)
            ]

        def p_self(image):
            ref = (k, v)[image]

            def of(pair, side):
                row = half + lax.div(pair, 3) * words
                return ref.at[
                    chunk(row, words), chunk((lax.rem(pair, 3) * 2 + side) * words, words)
                ]

            return of

        def p_cross(image):
            return lambda pair, side: act.at[
                upper, chunk(((image * PAIRS + pair) * 2 + side) * words, words)
            ]

        def cross_kv(image, which):
            col = (which * images + image) * D
            return lambda pair: gp.at[pl.ds(half, slots), chunk(col + pair * 128, 128)]

        def pair_ref(image, which):
            return lambda: gp[pl.ds(half, slots), pl.ds((which * images + image) * D, D)]

        def low_rows():
            return low[lower, :]

        dz = dmix.at[upper]
        decoded = xin.at[upper]
        text_grad = low.at[upper]

        stages[29] = lambda: give_vecs(False)

        @stage(0)
        def _():
            load_text(True)
            fill_keep()
            cot[...] = padded(enc_cot)
            start_stage(1)
            comp.norm(xin, 0, n1, 0, half, 0, 1, n1, half, rates.at[0], 0)

        @stage(1)
        def _():
            comp.linear(n1, 0, half, 0, 2, store_to(q, 0, half))
            comp.linear(n1, 0, half, 1, None, store_to(k, 0, half))
            comp.linear(n1, 0, half, 2, 3, store_to(v, 0, half))

        @stage(2)
        def _():
            key, query = iota((words, words), 0), iota((words, words), 1)
            for image in range(images):
                allowed = (key <= query) & (key < text_len[image])
                comp.attend(
                    allowed, at(q, image), at(k, image), at(v, image), p_self(image), at(o, image)
                )

        @stage(3)
        def _():
            def add_input(cols, values):
                h[lower, cols] = xin[lower, cols].astype(F32) + values

            comp.linear(o, 0, half, 3, 4, add_input)
            comp.norm(h, 0, n2, 0, half, 5, 6, acc, half, rates.at[1], 0)

        @stage(4)
        def _():
            comp.linear(n2, 0, half, 4, 7, store_to(q, half, half))

        @stage(5)
        def _():
            crossed(0, e)
            load(5, e, enc_out)
            for image in range(images):
                row = image * slots
                comp.linear(e, row, slots, 5, None, store_to(gp, half, slots, image * D))
                comp.linear(e, row, slots, 6, 8, store_to(gp, half, slots, (images + image) * D))

        @stage(6)
        def _():
            for image in range(images):
                allowed = spread(keep_col[pl.ds(image * slots, slots), :], words)
                comp.attend(
                    allowed,
                    at(q, image, half),
                    cross_kv(image, 0),
                    cross_kv(image, 1),
                    p_cross(image),
                    at(o, image, half),
                )

        @stage(7)
        def _():
            def add_self(cols, values):
                h[upper, cols] = h[lower, cols] + values

            comp.linear(o, half, half, 7, 9, add_self)
            comp.norm(h, half, n2, half, half, 10, 11, dh, half, rates.at[2], 0)

        @stage(8)
        def _():
            comp.hidden(n2, half, half, 8, 13, act, gp)

        @stage(9)
        def _():
            def add_middle(cols, values):
                made = h[upper, cols] + values + vrows[pl.ds(12, 1), cols]
                xin[upper, cols] = made.astype(BF16)

            comp.project(act.at[lower], half, 12, add_middle)
            give(False, 0, decoded, dec_out)

        @stage(10)
        def _():
            comp.hidden_back(low, half, 12, gp)
            dz[...] = low_rows()

        @stage(11)
        def _():
            gathered()
            gvec[pl.ds(12, 1), :] = comp.row_sum(dz[...])
            comp.wide_grad(act, half, lambda: dz[...], 12)

        @stage(12)
        def _():
            comp.project(gp.at[lower], half, 8, store_to(acc, 0, half))

        @stage(13)
        def _():
            comp.wide_sums(gp, half, 13)
            comp.wide_grad(gp, half, lambda: n2[upper, :], 8)

        @stage(14)
        def _():
            comp.norm_back(dh, half, rates.at[2], 0, acc, low, dh, low, half, 10, 11)
            comp.linear_back([(low_rows, 7)], store_to(dmix, 0, half))

        @stage(15)
        def _():
            for image in range(images):
                comp.attend_back(
                    at(q, image, half),
                    cross_kv(image, 0),
                    cross_kv(image, 1),
                    p_cross(image),
                    at(dmix, image),
                )

        @stage(16)
        def _():
            for image in range(images):
                rows = pl.ds(image * slots, slots)

                def add_cot(cols, values):
                    cot[rows, cols] = (cot[rows, cols].astype(F32) + values).astype(BF16)

                comp.linear_back([(pair_ref(image, 0), 5), (pair_ref(image, 1), 6)], add_cot)
            across(False, 1, cot, cot)

        @stage(17)
        def _():
            gvec[pl.ds(9, 1), :] = comp.row_sum(low_rows())
            comp.weight_grad(lambda part: [o[upper, chunk(part * BLOCK)]], [low_rows], 7)

        @stage(18)
        def _():
            comp.linear_back([(lambda: q[upper, :], 4)], store_to(acc, 0, half))

        @stage(19)
        def _():
            gvec[pl.ds(7, 1), :] = comp.row_sum(q[upper, :])
            total = comp.row_sum(pair_ref(0, 1)())
            for image in range(1, images):
                total = total + comp.row_sum(pair_ref(image, 1)())
            gvec[pl.ds(8, 1), :] = total
            comp.weight_grad(
                lambda part: [n2[lower, chunk(part * BLOCK)]], [lambda: q[upper, :]], 4
            )
            for which in (0, 1):
                comp.weight_grad(
                    lambda part: [
                        e[pl.ds(image * slots, slots), chunk(part * BLOCK)]
                        for image in range(images)
                    ],
                    [pair_ref(image, which) for image in range(images)],
                    5 + which,
                )

        @stage(20)
        def _():
            comp.norm_back(acc, half, rates.at[1], 0, acc, dh, dh, low, half, 5, 6)

        @stage(21)
        def _():
            comp.linear_back([(low_rows, 3)], store_to(dmix, 0, half))

        @stage(22)
        def _():
            gvec[pl.ds(4, 1), :] = comp.row_sum(low_rows())
            comp.weight_grad(lambda part: [o[lower, chunk(part * BLOCK)]], [low_rows], 3)

        @stage(23)
        def _():
            for image in range(images):
                comp.attend_back(
                    at(q, image), at(k, image), at(v, image), p_self(image), at(dmix, image)
                )

        @stage(24)
        def _():
            comp.linear_back(
                [(lambda: q[lower, :], 0), (lambda: k[lower, :], 1), (lambda: v[lower, :], 2)],
                store_to(acc, 0, half),
            )

        @stage(25)
        def _():
            gvec[pl.ds(2, 1), :] = comp.row_sum(q[lower, :])
            gvec[pl.ds(3, 1), :] = comp.row_sum(v[lower, :])
            for index, ref in enumerate((q, k, v)):
                comp.weight_grad(
                    lambda part: [n1[lower, chunk(part * BLOCK)]], [lambda: ref[lower, :]], index
                )

        @stage(26)
        def _():
            comp.norm_back(n1, half, rates.at[0], 0, acc, dh, None, text_grad, half, 0, 1)
            give(False, 1, text_grad, text_out)

        def last():
            across(True, 1, cot, cot)
            load(5, e, enc_out, True)
            give(True, 0, decoded, dec_out)
            give(True, 1, text_grad, text_out)
            got(1, image_out)

        return stages, last

    pl.when(section == 0)(lambda: section_program(0, encoder))
    pl.when(section == 1)(lambda: section_program(1, decoder))


def finish_kernel(
    used, encoded, decoded, images, text, enc, dec, enc_v, dec_v, *outs
):
    enc_out, dec_out, image_out, text_out, enc_out_g, dec_out_g, enc_out_v, dec_out_v = outs
    slots = BLOCK

    def cut(ref):
        rows = ref[...].astype(F32)
        parts = [
            rows[image * slots : image * slots + used] for image in range(rows.shape[0] // slots)
        ]
        return jnp.concatenate(parts, axis=0)

    @pl.when(pl.program_id(0) == 0)
    def _():
        enc_out[...] = cut(encoded).astype(BF16)
        image_out[...] = cut(images)
        enc_out_v[...] = in_line(enc_v[...])
        dec_out_v[...] = in_line(dec_v[...])

    dec_out[...] = decoded[...]
    text_out[...] = text[...].astype(F32)
    enc_out_g[...] = enc[...].astype(F32)
    dec_out_g[...] = dec[...].astype(F32)


def vec_tile_of(vecs):
    units = vecs.reshape(-1, VEC_UNIT)
    return jnp.pad(units, ((0, VEC_ROWS - units.shape[0]), (0, 128 - VEC_UNIT)))


def body_fast(
    images, text, enc_mats, enc_vecs, dec_mats, dec_vecs, tissue, text_len, enc_cot, dec_cot
):
    shards = lax.axis_size("dp")
    depth = grid_of(shards)[0]
    img_count, slots = tissue.shape
    words = text.shape[0] // img_count
    sizes = (enc_mats.shape[0], dec_mats.shape[0])
    pers = (enc_vecs.shape[0] // VEC_UNIT, dec_vecs.shape[0] // VEC_UNIT)
    wide = BLOCK
    image_rows, text_rows = img_count * wide, img_count * words
    any_space = pl.BlockSpec(memory_space=pl.ANY)
    vmem_space = pl.BlockSpec(memory_space=pltpu.VMEM)
    smem_space = pl.BlockSpec(memory_space=pltpu.SMEM)
    most = sizes[1]

    def low_buffer(rows=image_rows, columns=D):
        return pltpu.VMEM((rows, columns), BF16)

    def wide_buffer(rows=image_rows):
        return pltpu.VMEM((rows, D), F32)

    dma = pltpu.SemaphoreType.DMA
    made = pl.pallas_call(
        functools.partial(fused_kernel, depth, sizes, pers, wide, words),
        out_shape=(
            jax.ShapeDtypeStruct((image_rows, D), BF16),
            jax.ShapeDtypeStruct((text_rows, D), BF16),
            jax.ShapeDtypeStruct((image_rows, D), BF16),
            jax.ShapeDtypeStruct((text_rows, D), BF16),
            jax.ShapeDtypeStruct((sizes[0], D), BF16),
            jax.ShapeDtypeStruct((sizes[1], D), BF16),
            jax.ShapeDtypeStruct((VEC_ROWS, 128), F32),
            jax.ShapeDtypeStruct((VEC_ROWS, 128), F32),
        ),
        in_specs=[vmem_space] * 3 + [smem_space] + [any_space] * 6,
        out_specs=[any_space] * 8,
        scratch_shapes=[
            low_buffer(shards * most),
            low_buffer(max(Scatter.land_rows(depth, split_rows(rows, LATE)) for rows in sizes)),
            low_buffer(),
            low_buffer(),
            low_buffer(),
            low_buffer(),
            low_buffer(),
            low_buffer(),
            wide_buffer(),
            low_buffer(),
            low_buffer(image_rows, FF),
            low_buffer(image_rows, FF),
            low_buffer(),
            low_buffer(),
            wide_buffer(),
            wide_buffer(),
            low_buffer(),
            low_buffer(),
            pltpu.VMEM((image_rows, 128), F32),
            pltpu.VMEM((3, image_rows, 128), F32),
            pltpu.VMEM((shards, VEC_ROWS, 128), BF16),
            wide_buffer(VEC_ROWS),
            wide_buffer(VEC_ROWS),
            pltpu.VMEM((1 + depth, VEC_ROWS, D), F32),
            pltpu.VMEM((VEC_ROWS, 128), F32),
            pltpu.VMEM((2, 8, D), F32),
            dma((6,)),
            dma((4, shards, 4)),
            dma((4, shards)),
            dma((shards,)),
            dma((shards,)),
            dma((4, 4 * depth + 7)),
            dma((4, 4 * depth + 7)),
            dma((1 + depth,)),
            dma((1 + depth,)),
            dma((2,)),
            dma((2,)),
            dma((7,)),
            dma((7,)),
            dma((7,)),
            pltpu.SemaphoreType.REGULAR,
        ],
        compiler_params=pltpu.CompilerParams(
            collective_id=0, has_side_effects=True, vmem_limit_bytes=VMEM_LIMIT
        ),
        name="blocks_and_grads",
    )(
        images,
        enc_cot,
        tissue,
        text_len,
        text,
        enc_mats,
        dec_mats,
        vec_tile_of(enc_vecs),
        vec_tile_of(dec_vecs),
        dec_cot,
    )

    def tiled(rows):
        return pl.BlockSpec((rows // FINISH_STEPS, D), lambda step: (step, 0))

    def whole(shape):
        return pl.BlockSpec(shape, lambda step: (0, 0))

    image_spec, tile_spec = whole((image_rows, D)), whole((VEC_ROWS, 128))
    out_spec = whole((img_count * slots, D))
    outs = pl.pallas_call(
        functools.partial(finish_kernel, slots),
        grid=(FINISH_STEPS,),
        in_specs=[
            image_spec,
            tiled(text_rows),
            image_spec,
            tiled(text_rows),
            tiled(sizes[0]),
            tiled(sizes[1]),
            tile_spec,
            tile_spec,
        ],
        out_specs=[
            out_spec,
            tiled(text_rows),
            out_spec,
            tiled(text_rows),
            tiled(sizes[0]),
            tiled(sizes[1]),
            whole((8, 128)),
            whole((8, 128)),
        ],
        out_shape=(
            jax.ShapeDtypeStruct((img_count * slots, D), BF16),
            jax.ShapeDtypeStruct((text_rows, D), BF16),
            jax.ShapeDtypeStruct((img_count * slots, D), F32),
            jax.ShapeDtypeStruct((text_rows, D), F32),
            jax.ShapeDtypeStruct((sizes[0], D), F32),
            jax.ShapeDtypeStruct((sizes[1], D), F32),
            jax.ShapeDtypeStruct((8, 128), F32),
            jax.ShapeDtypeStruct((8, 128), F32),
        ),
        name="finish_outputs",
    )(*made)

    def vec_of(tile, per):
        return tile.reshape(-1)[: per * VEC_UNIT]

    return (
        outs[0],
        outs[1],
        outs[2],
        outs[3],
        outs[4],
        vec_of(outs[6], pers[0]),
        outs[5],
        vec_of(outs[7], pers[1]),
    )


FINISH_STEPS = 4
VMEM_LIMIT = 63 * 2**20
LATE = 0.21
GATHER_PLANS = (
    (
        120, 110, 400, 100, 130, 500, 121, 131, 8, 101, 111, 200, 231, 620, 630, 230, 102, 1500,
        221, 112, 201, 600, 631, 621, 601, 0, 103, 122, 211, 202, 132, 203, 610, 602, 603, 300,
        212, 220, 210, 611, 133, 1, 222, 2, 233, 632, 622, 612, 232, 310, 3, 4, 320, 5, 633, 330,
    ),
    (
        400, 500, 110, 130, 630, 100, 120, 101, 121, 102, 201, 1500, 29, 131, 111, 210, 600, 202,
        103, 601, 132, 112, 203, 631, 212, 610, 632, 620, 621, 200, 602, 0, 122, 222, 133, 603,
        211, 300, 221, 1, 2, 611, 232, 230, 3, 231, 612, 310, 233, 220, 4, 5, 633, 6, 7, 622, 320,
        8, 330, 10, 12,
    ),
)
SCATTER_PLANS = (
    (
        6, 7, 10, 11, 13, 14, 12, 1221, 730, 15, 16, 1231, 17, 1211, 18, 720, 19, 20, 1212, 830,
        1232, 21, 700, 1201, 1202, 930, 1310, 1031, 1233, 800, 1222, 820, 22, 30, 710, 1203, 900,
        1001, 920, 1021, 1002, 31, 1032, 810, 1300, 32, 1033, 1320, 1022, 910, 1410, 1011, 1330,
        1430, 1400, 33, 1012, 1003, 1110, 1420, 1130, 1100, 1120,
    ),
    (
        9, 11, 1231, 730, 14, 15, 16, 830, 13, 720, 1221, 18, 19, 17, 710, 1211, 930, 1031, 820,
        20, 21, 22, 23, 24, 1212, 25, 810, 700, 920, 1201, 1202, 26, 1222, 1021, 1232, 910, 1310,
        1011, 30, 1233, 1032, 800, 1022, 31, 1320, 32, 1012, 1420, 900, 1203, 1033, 1001, 1410,
        1130, 1002, 33, 1300, 1110, 1330, 1120, 1003, 1400, 1100, 1430,
    ),
)


def body(images, text, enc_mats, enc_vecs, dec_mats, dec_vecs, tissue, text_len, enc_cot, dec_cot):
    shards = lax.axis_size("dp")
    img_count, slots = tissue.shape
    words = text.shape[0] // img_count
    fits = (
        shards == 16
        and img_count == 2
        and slots <= BLOCK == 256
        and img_count * words == BLOCK
        and enc_mats.shape[0] % LINES == 0
        and dec_mats.shape[0] % LINES == 0
        and enc_vecs.shape[0] % VEC_UNIT == 0
        and dec_vecs.shape[0] % VEC_UNIT == 0
    )
    run = body_fast if fits else body_plain
    return run(
        images, text, enc_mats, enc_vecs, dec_mats, dec_vecs, tissue, text_len, enc_cot, dec_cot
    )


def solution(mesh):
    placed = (
        P("dp", None),
        P("dp", None),
        P("dp", None),
        P("dp"),
        P("dp", None),
        P("dp"),
        P("dp", None),
        P("dp"),
        P("dp", None),
        P("dp", None),
    )
    return jax.shard_map(
        body,
        mesh=mesh,
        in_specs=placed,
        out_specs=(
            P("dp", None),
            P("dp", None),
            P("dp", None),
            P("dp", None),
            P("dp", None),
            P("dp"),
            P("dp", None),
            P("dp"),
        ),
        check_vma=False,
    )
```
